32 devices in a mesh: depth: 4 (over y, x), dp: 8 (over z, core).
Axes of the slice: x: 2, y: 2, z: 4, core: 2. Of those that a mesh axis runs over, the one named last changes fastest.
Arguments:
- object_slices: float32 [4, 2, 768, 768], P('depth'), may hold values from -1.02 to 1.02, as said below
- positions: int32 [16, 2], P('dp'), may hold values from 0 to 640, as said below
- probe_field: float32 [2, 128, 128], replicated, may hold values from -6 to 6
- propagator_phase: float32 [128, 128], replicated, may hold values from -3.140625 to 3.140625
- measured: float32 [16, 128, 128], P('dp'), may hold values from 0.5 to 4
Outputs:
- slice_gradient: float32 [4, 2, 768, 768], P('depth', None, 'dp')
The draws below stay inside these ranges and needn't reach their ends.
Inputs may be any that keep to these rules, and one draw needn't show every extreme that they name: `object_slices`: every complex entry has magnitude between exp(-0.03) and exp(0.01). `positions`: each window lies inside the object; some window touches the last row and some the last column.
All inputs are finite; a program needn't handle non-finite values.
Results may differ from the reference program's by a relative error of at most 0.034.
Values may be sent and summed in bfloat16 or wider, within the bound.
No kernel may reach another device: no remote copies, remote signals or barrier semaphores. Data moves between devices by JAX's collectives and lax.ppermute only.
A program may use at most 64 MiB of HBM per device.

```python
import math
import jax
import jax.numpy as jnp
from jax import lax

Q = 128
OBJ = 768
LAYERS_DEV = 1
SLICES = 4
POSITIONS = 16


def draw_object_slices(key, part):
    key = jax.random.fold_in(key, 11)
    key_amp, key_angle = jax.random.split(key)
    shape = (SLICES, OBJ, OBJ)
    log_amp = jax.random.uniform(key_amp, shape, jnp.float32, -0.02, 0.01)
    angle = jax.random.uniform(key_angle, shape, jnp.float32, -0.4, 0.4)
    magnitude = jnp.exp(log_amp)
    return jnp.stack([magnitude * jnp.cos(angle), magnitude * jnp.sin(angle)], axis=1)


def draw_positions(key, part):
    key = jax.random.fold_in(key, 23)
    key_all, key_first, key_second = jax.random.split(key, 3)
    limit = OBJ - Q
    offsets = jax.random.randint(key_all, (POSITIONS, 2), 0, limit + 1, dtype=jnp.int32)
    first = jax.random.randint(key_first, (), 0, POSITIONS, dtype=jnp.int32)
    second = (first + jax.random.randint(key_second, (), 1, POSITIONS, dtype=jnp.int32)) % POSITIONS
    offsets = offsets.at[first].set(jnp.array([limit, 0], jnp.int32))
    offsets = offsets.at[second].set(jnp.array([0, limit], jnp.int32))
    return offsets


def block_levels(own_key, extent, shards, low, high):
    loudness = 1.0
    for axis_at, shards_of in shards:
        steps = jax.random.uniform(jax.random.fold_in(jax.random.fold_in(own_key, 6), axis_at), (shards_of,), jnp.float32, low / len(shards), high / len(shards))
        loudness = loudness * jnp.repeat(jnp.exp(steps), extent[axis_at] // shards_of).reshape((-1,) + (1,) * (len(extent) - 1 - axis_at))
    return loudness


def scatter_about(key, shape, deviation, reach, held_as=jnp.bfloat16):
    drawn = jax.random.normal(key, shape, jnp.float32) * deviation
    return jnp.minimum(jnp.maximum(drawn, -reach), reach).astype(held_as)


def setup_inputs(seed: int = 0) -> dict:
    streams_of = jax.random.split(jax.random.key(seed), 6)
    return {
        "object_slices": draw_object_slices(jax.random.fold_in(streams_of[5], 71), 0),
        "positions": draw_positions(jax.random.fold_in(streams_of[5], 71), 0),
        "probe_field": scatter_about(streams_of[2], (2, Q, Q), 1.0, 6.0, jnp.float32),
        "propagator_phase": jnp.clip(jax.random.uniform(streams_of[3], (Q, Q), jnp.float32, -3.140625, 3.140625), -3.140625, 3.140625),
        "measured": jnp.clip(jnp.exp(math.log(4.0) - 2.0794415 * jax.random.uniform(streams_of[4], (POSITIONS, Q, Q), jnp.float32) ** block_levels(streams_of[4], (POSITIONS, Q, Q), ((0, 8),), -0.2, 0.2)), 0.5, 4.0),
    }


grad_scale = 0.03125

def rounded(values):
    return lax.optimization_barrier(values.astype(jnp.bfloat16)).astype(jnp.float32)

def dft_tables(size):
    indices = jnp.arange(size, dtype=jnp.int32)
    folded = indices[:, None] * indices[None, :] % size
    angles = folded.astype(jnp.float32) * (2.0 * math.pi / size)
    norm_factor = 1.0 / math.sqrt(size)
    return jnp.stack([jnp.cos(angles) * norm_factor, jnp.sin(angles) * norm_factor])

def combine(result, sign_value):
    return jnp.stack([result[:, 0, 0] - sign_value * result[:, 1, 1], result[:, 0, 1] + sign_value * result[:, 1, 0]], axis=1)

def along_rows(field_in, tables, sign_value):
    result = jnp.einsum('tjk,mckl->mtcjl', tables, field_in, precision=lax.Precision.HIGHEST)
    return combine(result, sign_value)

def along_cols(field_in, tables, sign_value):
    result = jnp.einsum('mckl,tlj->mtckj', field_in, tables, precision=lax.Precision.HIGHEST)
    return combine(result, sign_value)

def transform(field_in, tables, sign_value):
    return along_cols(along_rows(field_in, tables, sign_value), tables, sign_value)

def complex_mul(left, right, conj_left):
    if conj_left:
        return jnp.stack([left[:, 0] * right[:, 0] + left[:, 1] * right[:, 1], left[:, 0] * right[:, 1] - left[:, 1] * right[:, 0]], axis=1)
    return jnp.stack([left[:, 0] * right[:, 0] - left[:, 1] * right[:, 1], left[:, 0] * right[:, 1] + left[:, 1] * right[:, 0]], axis=1)

def propagate(field_in, kernel, tables):
    spectrum = transform(field_in, tables, -1.0)
    spectrum = complex_mul(spectrum, kernel[None], False)
    return transform(spectrum, tables, 1.0)

def far_field(exit_wave, measured, tables):
    spectrum = transform(exit_wave, tables, -1.0)
    intensity = spectrum[:, 0] * spectrum[:, 0] + spectrum[:, 1] * spectrum[:, 1]
    residue = intensity - measured
    return transform(2.0 * residue[:, None] * spectrum, tables, 1.0)

def reference(object_slices, positions, probe_field, propagator_phase, measured):
    tables = dft_tables(Q)
    kernel = jnp.stack([jnp.cos(propagator_phase), jnp.sin(propagator_phase)])
    conj_kernel = jnp.stack([jnp.cos(propagator_phase), -jnp.sin(propagator_phase)])
    count = positions.shape[0]
    span = jnp.arange(Q, dtype=jnp.int32)
    row_index = (positions[:, 0:1].astype(jnp.int32) + span[None, :])[:, :, None]
    col_index = (positions[:, 1:2].astype(jnp.int32) + span[None, :])[:, None, :]
    current = jnp.broadcast_to(probe_field, (count, 2, Q, Q))
    stored = []
    for slice_no in range(SLICES):
        if slice_no > 0 and slice_no % LAYERS_DEV == 0:
            current = rounded(current)
        transmit = jnp.transpose(object_slices[slice_no][:, row_index, col_index], (1, 0, 2, 3))
        stored.append(current)
        current = propagate(complex_mul(transmit, current, False), kernel, tables)
    adjoint = far_field(current, measured, tables)
    layer_grads = []
    for slice_no in reversed(range(SLICES)):
        returned = propagate(adjoint, conj_kernel, tables)
        transmit = jnp.transpose(object_slices[slice_no][:, row_index, col_index], (1, 0, 2, 3))
        contrib = complex_mul(stored[slice_no], returned, True)
        layer_grad = jnp.zeros((2, OBJ, OBJ), jnp.float32).at[:, row_index, col_index].add(jnp.transpose(contrib, (1, 0, 2, 3)))
        layer_grads.append(layer_grad)
        adjoint = complex_mul(transmit, returned, True)
        if slice_no > 0 and slice_no % LAYERS_DEV == 0:
            adjoint = rounded(adjoint)
    return jnp.stack(layer_grads[::-1]) * grad_scale
```

```python
import functools
import math

import jax
import jax.numpy as jnp
import numpy as np
from jax import lax
from jax.experimental import pallas as pl
from jax.experimental.pallas import tpu as pltpu
from jax.sharding import PartitionSpec as P

grad_scale = 0.03125
f32 = jnp.float32
bf16 = jnp.bfloat16


def dft_matrices(size):
    k = np.arange(size)
    angles = 2.0 * np.pi * ((k[:, None] * k[None, :]) % size) / size
    c = np.cos(angles) / math.sqrt(size)
    s = np.sin(angles) / math.sqrt(size)
    plus = np.block([[c, s], [-s, c]]).astype(np.float32)
    minus = np.block([[c, -s], [s, c]]).astype(np.float32)
    parts = []
    for full in (plus, minus):
        high = full.astype(bf16)
        low = (full - high.astype(np.float32)).astype(bf16)
        parts.append((high, low))
    (ph, plo), (mh, mlo) = parts
    right = np.stack([np.concatenate([ph, ph, plo], 0), np.concatenate([mh, mh, mlo], 0)])
    left = np.stack([np.concatenate([mh, mh, mlo], 1), np.concatenate([ph, ph, plo], 1)])
    return left, right


def window_kernel(pos_ref, obj_ref, out_ref, buf, sems):
    count, _, window, _ = out_ref.shape
    rows, cols = obj_ref.shape[-2:]
    tall, wide = buf.shape[-2:]

    def corner(p):
        row_base = jnp.minimum(pos_ref[p, 0] // 8, (rows - tall) // 8) * 8
        col_base = jnp.minimum(pos_ref[p, 1] // 128, (cols - wide) // 128) * 128
        return pl.multiple_of(row_base, 8), pl.multiple_of(col_base, 128)

    def copy(p):
        row_base, col_base = corner(p)
        return pltpu.make_async_copy(
            obj_ref.at[:, pl.ds(row_base, tall), pl.ds(col_base, wide)], buf.at[p], sems.at[p]
        )

    for p in range(count):
        copy(p).start()
    for p in range(count):
        copy(p).wait()
        row_base, col_base = corner(p)
        row_off = pos_ref[p, 0] - row_base
        col_off = pos_ref[p, 1] - col_base
        lift = jnp.where(row_off == 0, 0, tall - row_off)
        shift = jnp.where(col_off == 0, 0, wide - col_off)
        for part in range(2):
            block = pltpu.roll(buf[p, part], lift, 0)[:window]
            block = pltpu.roll(block, shift, 1)
            out_ref[p, part] = block[:, :window].astype(out_ref.dtype)


def take_windows(obj, positions, window):
    count = positions.shape[0]
    tall, wide = window + 8, window + 128
    return pl.pallas_call(
        window_kernel,
        out_shape=jax.ShapeDtypeStruct((count, 2, window, window), bf16),
        in_specs=[pl.BlockSpec(memory_space=pltpu.SMEM), pl.BlockSpec(memory_space=pl.ANY)],
        out_specs=pl.BlockSpec(memory_space=pltpu.VMEM),
        scratch_shapes=[
            pltpu.VMEM((count, 2, tall, wide), f32),
            pltpu.SemaphoreType.DMA((count,)),
        ],
        name="take_windows",
    )(positions, obj)


def split(x):
    high = x.astype(bf16)
    return high, (x - high.astype(f32)).astype(bf16)


def cmul(a, b):
    return a[0] * b[0] - a[1] * b[1], a[0] * b[1] + a[1] * b[0]


def cmul_conj(a, b):
    return a[0] * b[0] + a[1] * b[1], a[0] * b[1] - a[1] * b[0]


def wave_kernel(meta_ref, probe_ref, kern_ref, meas_ref, left_ref, right_ref, *rest):
    t_refs, (out_ref, waves) = rest[:-2], rest[-2:]
    slices = len(t_refs)
    count, _, window, _ = out_ref.shape
    own = meta_ref[0]

    def t_of(k, p):
        def pick(m):
            return lambda: (t_refs[m][p, 0], t_refs[m][p, 1])

        return tuple(x.astype(f32) for x in lax.switch(own ^ k, [pick(m) for m in range(slices)]))

    def rows(fields, sign):
        x = jnp.concatenate(
            [jnp.concatenate([f[0], f[1]], axis=0) for f in fields], axis=1
        )
        high, low = split(x)
        y = jnp.dot(
            left_ref[sign], jnp.concatenate([high, low, high], axis=0), preferred_element_type=f32
        )
        return [
            (y[:window, p * window : (p + 1) * window], y[window:, p * window : (p + 1) * window])
            for p in range(len(fields))
        ]

    def cols(fields, sign):
        x = jnp.concatenate(
            [jnp.concatenate([f[0], f[1]], axis=1) for f in fields], axis=0
        )
        high, low = split(x)
        y = jnp.dot(
            jnp.concatenate([high, low, high], axis=1), right_ref[sign], preferred_element_type=f32
        )
        return [
            (y[p * window : (p + 1) * window, :window], y[p * window : (p + 1) * window, window:])
            for p in range(len(fields))
        ]

    plus, minus = 0, 1

    def transform(fields, sign):
        return cols(rows(fields, sign), sign)

    kern = (kern_ref[0], kern_ref[1])
    probe = (probe_ref[0], probe_ref[1])
    psi = [probe] * count
    spectrum = None
    for k in range(slices):

        @pl.when(own == k)
        def _():
            for p in range(count):
                waves[p, 0] = psi[p][0]
                waves[p, 1] = psi[p][1]

        spectrum = transform([cmul(t_of(k, p), psi[p]) for p in range(count)], minus)
        if k < slices - 1:
            psi = transform([cmul(kern, s) for s in spectrum], plus)

    def source(p):
        re, im = spectrum[p]
        scale = 2.0 * (re * re + im * im - meas_ref[p])
        return scale * re, scale * im

    returned = transform([source(p) for p in range(count)], plus)
    for k in reversed(range(slices)):

        @pl.when(own == k)
        def _():
            for p in range(count):
                re, im = cmul_conj((waves[p, 0], waves[p, 1]), returned[p])
                out_ref[p, 0] = (re * grad_scale).astype(out_ref.dtype)
                out_ref[p, 1] = (im * grad_scale).astype(out_ref.dtype)

        if k > 0:
            chi = [cmul_conj(t_of(k, p), returned[p]) for p in range(count)]
            spectrum = transform(chi, minus)
            returned = transform([cmul_conj(kern, s) for s in spectrum], plus)


def run_waves(depth_index, probe, kern, measured, gathered):
    count, _, window, _ = gathered[0].shape
    left, right = dft_matrices(window)
    vmem = pl.BlockSpec(memory_space=pltpu.VMEM)
    return pl.pallas_call(
        wave_kernel,
        out_shape=jax.ShapeDtypeStruct((count, 2, window, window), bf16),
        in_specs=[pl.BlockSpec(memory_space=pltpu.SMEM)] + [vmem] * (5 + len(gathered)),
        out_specs=vmem,
        scratch_shapes=[pltpu.VMEM((count, 2, window, window), f32)],
        compiler_params=pltpu.CompilerParams(vmem_limit_bytes=32 * 1024 * 1024),
        name="run_waves",
    )(depth_index, probe, kern, measured, jnp.asarray(left), jnp.asarray(right), *gathered)


def place_kernel(pos_ref, meta_ref, terms_ref, out_ref, canvas):
    count, _, window, _ = terms_ref.shape
    _, stripe, cols = out_ref.shape
    wide = window + 128
    canvas[:, window : window + stripe, :] = jnp.zeros((2, stripe, canvas.shape[2]), f32)
    first_row = meta_ref[0] * stripe

    def body(p, carry):
        row = pos_ref[p, 0] - first_row + window
        col = pos_ref[p, 1]
        row_base = pl.multiple_of(row // 8 * 8, 8)
        col_base = pl.multiple_of(col // 128 * 128, 128)

        @pl.when((row > 0) & (row < window + stripe))
        def _():
            for part in range(2):
                block = terms_ref[p, part].astype(f32)
                block = jnp.concatenate([block, jnp.zeros((window, 128), f32)], axis=1)
                block = pltpu.roll(block, col - col_base, 1)
                block = jnp.concatenate([block, jnp.zeros((8, wide), f32)], axis=0)
                block = pltpu.roll(block, row - row_base, 0)
                at = (part, pl.ds(row_base, window + 8), pl.ds(col_base, wide))
                canvas[at] = canvas[at] + block

        return carry

    lax.fori_loop(0, count, body, 0)
    out_ref[...] = canvas[:, window : window + stripe, :cols]


def place_windows(positions, dp_index, terms, stripe, cols):
    window = terms.shape[-1]
    vmem = pl.BlockSpec(memory_space=pltpu.VMEM)
    smem = pl.BlockSpec(memory_space=pltpu.SMEM)
    tall = window + (stripe + 7) // 8 * 8 + window + 8
    return pl.pallas_call(
        place_kernel,
        out_shape=jax.ShapeDtypeStruct((2, stripe, cols), f32),
        in_specs=[smem, smem, vmem],
        out_specs=vmem,
        scratch_shapes=[pltpu.VMEM((2, tall, cols + 128), f32)],
        compiler_params=pltpu.CompilerParams(vmem_limit_bytes=40 * 1024 * 1024),
        name="place_windows",
    )(positions, dp_index, terms)


def on_device(object_slices, positions, probe_field, propagator_phase, measured):
    depth_count = lax.axis_size("depth")
    depth_index = lax.axis_index("depth").astype(jnp.int32).reshape(1)
    dp_index = lax.axis_index("dp").astype(jnp.int32).reshape(1)
    window = probe_field.shape[-1]
    rows, cols = object_slices.shape[-2:]
    stripe = rows // lax.axis_size("dp")
    all_positions = lax.all_gather(positions, "dp", axis=0, tiled=True)
    kern = jnp.stack([jnp.cos(propagator_phase), jnp.sin(propagator_phase)])
    own = take_windows(object_slices[0], positions, window)
    gathered = [own] + [
        lax.ppermute(own, "depth", [(i, i ^ m) for i in range(depth_count)])
        for m in range(1, depth_count)
    ]
    terms = run_waves(depth_index, probe_field, kern, measured, gathered)
    all_terms = lax.all_gather(terms, "dp", axis=0, tiled=True)
    return place_windows(all_positions, dp_index, all_terms, stripe, cols)[None]


def solution(mesh):
    placed = (P("depth", None, None, None), P("dp", None), P(), P(), P("dp", None, None))
    return jax.shard_map(
        on_device,
        mesh=mesh,
        in_specs=placed,
        out_specs=P("depth", None, "dp", None),
        check_vma=False,
    )
```

```python
import functools
import math

import jax
import jax.numpy as jnp
import numpy as np
from jax import lax
from jax.experimental import pallas as pl
from jax.experimental.pallas import tpu as pltpu
from jax.sharding import PartitionSpec as P

grad_scale = 0.03125
f32 = jnp.float32
bf16 = jnp.bfloat16


def dft_matrices(size):
    k = np.arange(size)
    angles = 2.0 * np.pi * ((k[:, None] * k[None, :]) % size) / size
    c = np.cos(angles) / math.sqrt(size)
    s = np.sin(angles) / math.sqrt(size)
    plus = np.block([[c, s], [-s, c]]).astype(np.float32)
    minus = np.block([[c, -s], [s, c]]).astype(np.float32)
    parts = []
    for full in (plus, minus):
        high = full.astype(bf16)
        low = (full - high.astype(np.float32)).astype(bf16)
        parts.append((high, low))
    (ph, plo), (mh, mlo) = parts
    right = np.stack([np.concatenate([ph, ph, plo], 0), np.concatenate([mh, mh, mlo], 0)])
    left = np.stack([np.concatenate([mh, mh, mlo], 1), np.concatenate([ph, ph, plo], 1)])
    return left, right


def window_kernel(pos_ref, obj_ref, out_ref, buf, sems):
    count, _, window, _ = out_ref.shape
    rows, cols = obj_ref.shape[-2:]
    tall, wide = buf.shape[-2:]

    def corner(p):
        row_base = jnp.minimum(pos_ref[p, 0] // 8, (rows - tall) // 8) * 8
        col_base = jnp.minimum(pos_ref[p, 1] // 128, (cols - wide) // 128) * 128
        return pl.multiple_of(row_base, 8), pl.multiple_of(col_base, 128)

    def copy(p):
        row_base, col_base = corner(p)
        return pltpu.make_async_copy(
            obj_ref.at[:, pl.ds(row_base, tall), pl.ds(col_base, wide)], buf.at[p], sems.at[p]
        )

    for p in range(count):
        copy(p).start()
    for p in range(count):
        copy(p).wait()
        row_base, col_base = corner(p)
        row_off = pos_ref[p, 0] - row_base
        col_off = pos_ref[p, 1] - col_base
        lift = jnp.where(row_off == 0, 0, tall - row_off)
        shift = jnp.where(col_off == 0, 0, wide - col_off)
        for part in range(2):
            block = pltpu.roll(buf[p, part], lift, 0)[:window]
            block = pltpu.roll(block, shift, 1)
            out_ref[p, part] = block[:, :window].astype(out_ref.dtype)


def take_windows(obj, positions, window):
    count = positions.shape[0]
    tall, wide = window + 8, window + 128
    return pl.pallas_call(
        window_kernel,
        out_shape=jax.ShapeDtypeStruct((count, 2, window, window), bf16),
        in_specs=[pl.BlockSpec(memory_space=pltpu.SMEM), pl.BlockSpec(memory_space=pl.ANY)],
        out_specs=pl.BlockSpec(memory_space=pltpu.VMEM),
        scratch_shapes=[
            pltpu.VMEM((count, 2, tall, wide), f32),
            pltpu.SemaphoreType.DMA((count,)),
        ],
        name="take_windows",
    )(positions, obj)


def split(x):
    high = x.astype(bf16)
    return high, (x - high.astype(f32)).astype(bf16)


def cmul(a, b):
    return a[0] * b[0] - a[1] * b[1], a[0] * b[1] + a[1] * b[0]


def cmul_conj(a, b):
    return a[0] * b[0] + a[1] * b[1], a[0] * b[1] - a[1] * b[0]


def wave_kernel(meta_ref, pos_ref, probe_ref, kern_ref, meas_ref, left_ref, right_ref, *rest):
    t_refs, (out_ref, waves) = rest[:-2], rest[-2:]
    slices = len(t_refs)
    count, _, window, _ = out_ref.shape
    own = meta_ref[0]

    def t_of(k, p):
        def pick(m):
            return lambda: (t_refs[m][p, 0], t_refs[m][p, 1])

        return tuple(x.astype(f32) for x in lax.switch(own ^ k, [pick(m) for m in range(slices)]))

    def rows(fields, sign, exact):
        x = jnp.concatenate(
            [jnp.concatenate([f[0], f[1]], axis=0) for f in fields], axis=1
        )
        if exact:
            high, low = split(x)
            x = jnp.concatenate([high, low, high], axis=0)
        else:
            x = x.astype(bf16)
        y = jnp.dot(left_ref[sign, :, : x.shape[0]], x, preferred_element_type=f32)
        return [
            (y[:window, p * window : (p + 1) * window], y[window:, p * window : (p + 1) * window])
            for p in range(len(fields))
        ]

    def cols(fields, sign, exact):
        x = jnp.concatenate(
            [jnp.concatenate([f[0], f[1]], axis=1) for f in fields], axis=0
        )
        if exact:
            high, low = split(x)
            x = jnp.concatenate([high, low, high], axis=1)
        else:
            x = x.astype(bf16)
        y = jnp.dot(x, right_ref[sign, : x.shape[1]], preferred_element_type=f32)
        return [
            (y[p * window : (p + 1) * window, :window], y[p * window : (p + 1) * window, window:])
            for p in range(len(fields))
        ]

    plus, minus = 0, 1

    def transform(fields, sign, exact=True):
        return cols(rows(fields, sign, exact), sign, exact)

    kern = (kern_ref[0], kern_ref[1])
    probe = (probe_ref[0], probe_ref[1])
    psi = [probe] * count
    spectrum = None
    for k in range(slices):

        @pl.when(own == k)
        def _():
            for p in range(count):
                waves[p, 0] = psi[p][0]
                waves[p, 1] = psi[p][1]

        spectrum = transform([cmul(t_of(k, p), psi[p]) for p in range(count)], minus)
        if k < slices - 1:
            psi = transform([cmul(kern, s) for s in spectrum], plus)

    def source(p):
        re, im = spectrum[p]
        scale = 2.0 * (re * re + im * im - meas_ref[p])
        return scale * re, scale * im

    returned = transform([source(p) for p in range(count)], plus, False)
    for k in reversed(range(slices)):

        @pl.when(own == k)
        def _():
            for p in range(count):
                re, im = cmul_conj((waves[p, 0], waves[p, 1]), returned[p])
                out_ref[p, 0] = (re * grad_scale).astype(out_ref.dtype)
                out_ref[p, 1] = (im * grad_scale).astype(out_ref.dtype)

        if k > 0:
            chi = [cmul_conj(t_of(k, p), returned[p]) for p in range(count)]
            spectrum = transform(chi, minus, False)
            returned = transform([cmul_conj(kern, s) for s in spectrum], plus, False)


def run_waves(depth_index, positions, probe, kern, measured, gathered):
    count, _, window, _ = gathered[0].shape
    left, right = dft_matrices(window)
    smem = pl.BlockSpec(memory_space=pltpu.SMEM)
    vmem = pl.BlockSpec(memory_space=pltpu.VMEM)
    return pl.pallas_call(
        wave_kernel,
        out_shape=jax.ShapeDtypeStruct((count, 2, window, window), bf16),
        in_specs=[smem, smem] + [vmem] * (5 + len(gathered)),
        out_specs=vmem,
        scratch_shapes=[pltpu.VMEM((count, 2, window, window), f32)],
        compiler_params=pltpu.CompilerParams(vmem_limit_bytes=32 * 1024 * 1024),
        name="run_waves",
    )(depth_index, positions, probe, kern, measured, jnp.asarray(left), jnp.asarray(right), *gathered)


def place_kernel(pos_ref, meta_ref, *rest):
    terms_refs, (out_ref, canvas) = rest[:-2], rest[-2:]
    count, _, window, _ = terms_refs[0].shape
    _, stripe, cols = out_ref.shape
    wide = window + 128
    canvas[:, window : window + stripe, :] = jnp.zeros((2, stripe, canvas.shape[2]), f32)
    first_row = meta_ref[0] * stripe

    def body(p, terms_ref, base):
        row = pos_ref[base + p, 0] - first_row + window
        col = pos_ref[base + p, 1]
        row_base = pl.multiple_of(row // 8 * 8, 8)
        col_base = pl.multiple_of(col // 128 * 128, 128)

        @pl.when((row > 0) & (row < window + stripe))
        def _():
            for part in range(2):
                block = terms_ref[p, part].astype(f32)
                block = jnp.concatenate([block, jnp.zeros((window, 128), f32)], axis=1)
                block = pltpu.roll(block, col - col_base, 1)
                block = jnp.concatenate([block, jnp.zeros((8, wide), f32)], axis=0)
                block = pltpu.roll(block, row - row_base, 0)
                at = (part, pl.ds(row_base, window + 8), pl.ds(col_base, wide))
                canvas[at] = canvas[at] + block

    for source, terms_ref in enumerate(terms_refs):
        for p in range(count):
            body(p, terms_ref, source * count)
    out_ref[...] = canvas[:, window : window + stripe, :cols]


def place_windows(positions, dp_index, terms, stripe, cols):
    window = terms[0].shape[-1]
    vmem = pl.BlockSpec(memory_space=pltpu.VMEM)
    smem = pl.BlockSpec(memory_space=pltpu.SMEM)
    tall = window + (stripe + 7) // 8 * 8 + window + 8
    return pl.pallas_call(
        place_kernel,
        out_shape=jax.ShapeDtypeStruct((2, stripe, cols), f32),
        in_specs=[smem, smem] + [vmem] * len(terms),
        out_specs=vmem,
        scratch_shapes=[pltpu.VMEM((2, tall, cols + 128), f32)],
        compiler_params=pltpu.CompilerParams(vmem_limit_bytes=40 * 1024 * 1024),
        name="place_windows",
    )(positions, dp_index, *terms)


def swap(block, axis, distance):
    return lax.ppermute(block, axis, [(i, i ^ distance) for i in range(lax.axis_size(axis))])


def spread(block, axis):
    return [block] + [swap(block, axis, m) for m in range(2, lax.axis_size(axis), 2)]


def on_device(object_slices, positions, probe_field, propagator_phase, measured):
    depth_count = lax.axis_size("depth")
    depth_index = lax.axis_index("depth").astype(jnp.int32).reshape(1)
    dp_index = lax.axis_index("dp").astype(jnp.int32).reshape(1)
    window = probe_field.shape[-1]
    rows, cols = object_slices.shape[-2:]
    stripe = rows // lax.axis_size("dp")
    all_positions = jnp.concatenate(spread(positions, "dp"))
    all_positions = jnp.concatenate([all_positions, swap(all_positions, "dp", 1)])
    kern = jnp.stack([jnp.cos(propagator_phase), jnp.sin(propagator_phase)])
    own = take_windows(object_slices[0], positions, window)
    gathered = [own] + [swap(own, "depth", m) for m in range(1, depth_count)]
    terms = run_waves(depth_index, all_positions, probe_field, kern, measured, gathered)
    all_terms = spread(terms, "dp")
    all_terms += [swap(x, "dp", 1) for x in all_terms]
    return place_windows(all_positions, dp_index, all_terms, stripe, cols)[None]


def solution(mesh):
    placed = (P("depth", None, None, None), P("dp", None), P(), P(), P("dp", None, None))
    return jax.shard_map(
        on_device,
        mesh=mesh,
        in_specs=placed,
        out_specs=P("depth", None, "dp", None),
        check_vma=False,
    )
```

```python
import functools
import math

import jax
import jax.numpy as jnp
import numpy as np
from jax import lax
from jax.experimental import pallas as pl
from jax.experimental.pallas import tpu as pltpu
from jax.sharding import PartitionSpec as P

grad_scale = 0.03125
f32 = jnp.float32
bf16 = jnp.bfloat16


def dft_matrices(size):
    k = np.arange(size)
    angles = 2.0 * np.pi * ((k[:, None] * k[None, :]) % size) / size
    c = np.cos(angles) / math.sqrt(size)
    s = np.sin(angles) / math.sqrt(size)
    plus = np.block([[c, s], [-s, c]]).astype(np.float32)
    minus = np.block([[c, -s], [s, c]]).astype(np.float32)
    parts = []
    for full in (plus, minus):
        high = full.astype(bf16)
        low = (full - high.astype(np.float32)).astype(bf16)
        parts.append((high, low))
    (ph, plo), (mh, mlo) = parts
    right = np.stack([np.concatenate([ph, ph, plo], 0), np.concatenate([mh, mh, mlo], 0)])
    left = np.stack([np.concatenate([mh, mh, mlo], 1), np.concatenate([ph, ph, plo], 1)])
    return left, right


def indices(clusters):
    dp_index = lax.axis_index("dp")
    return lax.axis_index("depth"), lax.div(dp_index, lax.axis_size("dp") // clusters), dp_index


def window_kernel(obj_ref, *rest):
    buf, sems = rest[-2:]
    depth = buf.shape[0]
    clusters = len(rest) - 3 - depth
    pos_refs = rest[:clusters]
    out_refs = rest[clusters : clusters + depth]
    table_ref = rest[clusters + depth]
    own, cluster, _ = indices(clusters)
    per_home = depth // clusters
    window = out_refs[0].shape[-1]
    rows, cols = obj_ref.shape[-2:]
    tall, wide = buf.shape[-2:]

    for home in range(clusters):
        for q in range(per_home):
            for axis in range(2):
                value = pos_refs[0][q, axis]
                for m in range(1, clusters):
                    value = jnp.where(home ^ cluster == m, pos_refs[m][q, axis], value)
                table_ref[home * per_home + q, axis] = value

    def corner(m):
        at = own ^ m
        row, col = table_ref[at, 0], table_ref[at, 1]
        row_base = pl.multiple_of(jnp.minimum(row >> 3, (rows - tall) // 8) * 8, 8)
        col_base = pl.multiple_of(jnp.minimum(col >> 7, (cols - wide) // 128) * 128, 128)
        return row_base, col_base, row - row_base, col - col_base

    def copy(m):
        row_base, col_base, _, _ = corner(m)
        return pltpu.make_async_copy(
            obj_ref.at[:, pl.ds(row_base, tall), pl.ds(col_base, wide)], buf.at[m], sems.at[m]
        )

    for m in range(depth):
        copy(m).start()
    for m in range(depth):
        copy(m).wait()
        _, _, row_off, col_off = corner(m)
        lift = jnp.where(row_off == 0, 0, tall - row_off)
        shift = jnp.where(col_off == 0, 0, wide - col_off)
        for part in range(2):
            block = pltpu.roll(buf[m, part], shift, 1)[:, :window]
            block = pltpu.roll(block, lift, 0)[:window]
            out_refs[m][part] = block.astype(bf16)


def take_windows(obj, positions, window, depth):
    tall, wide = window + 8, window + 128
    smem = pl.BlockSpec(memory_space=pltpu.SMEM)
    vmem = pl.BlockSpec(memory_space=pltpu.VMEM)
    out = pl.pallas_call(
        window_kernel,
        out_shape=[jax.ShapeDtypeStruct((2, window, window), bf16)] * depth
        + [jax.ShapeDtypeStruct((depth, 2), jnp.int32)],
        in_specs=[pl.BlockSpec(memory_space=pl.ANY)] + [smem] * len(positions),
        out_specs=[vmem] * depth + [smem],
        scratch_shapes=[
            pltpu.VMEM((depth, 2, tall, wide), f32),
            pltpu.SemaphoreType.DMA((depth,)),
        ],
        name="take_windows",
    )(obj, *positions)
    return list(out[:depth]), out[depth]


def split(x):
    high = x.astype(bf16)
    return high, (x - high.astype(f32)).astype(bf16)


def cmul(a, b):
    return a[0] * b[0] - a[1] * b[1], a[0] * b[1] + a[1] * b[0]


def cmul_conj(a, b):
    return a[0] * b[0] + a[1] * b[1], a[0] * b[1] - a[1] * b[0]


def wave_kernel(slices, probe_ref, kern_ref, left_ref, right_ref, *rest):
    t_refs, rest = rest[:slices], rest[slices:]
    meas_refs = rest[: -slices - 3]
    out_refs = rest[-slices - 3 : -3]
    trans, terms, meas = rest[-3:]
    own, cluster, _ = indices(len(meas_refs))
    per_home = slices // len(meas_refs)
    window = probe_ref.shape[-1]

    for m in range(slices):
        trans[own ^ m] = t_refs[m][...]
    home = lax.div(own, per_home)
    for m, meas_ref in enumerate(meas_refs):

        @pl.when(home ^ cluster == m)
        def _():
            meas[...] = meas_ref[lax.rem(own, per_home)]

    def t_of(k):
        return trans[k, 0].astype(f32), trans[k, 1].astype(f32)

    def passes(x, axis, exact):
        if not exact:
            return x.astype(bf16)
        high, low = split(x)
        return jnp.concatenate([high, low, high], axis=axis)

    def rows(field, sign, exact):
        x = passes(jnp.concatenate(field, axis=0), 0, exact)
        y = jnp.dot(left_ref[sign, :, : x.shape[0]], x, preferred_element_type=f32)
        return y[:window], y[window:]

    def cols(field, sign, exact):
        x = passes(jnp.concatenate(field, axis=1), 1, exact)
        y = jnp.dot(x, right_ref[sign, : x.shape[1]], preferred_element_type=f32)
        return y[:, :window], y[:, window:]

    plus, minus = 0, 1

    def transform(field, sign, exact):
        return cols(rows(field, sign, exact), sign, exact)

    kern = (kern_ref[0], kern_ref[1])
    psi = (probe_ref[0], probe_ref[1])
    kept = []
    for k in range(slices):
        kept.append(psi)
        spectrum = transform(cmul(t_of(k), psi), minus, True)
        if k < slices - 1:
            psi = transform(cmul(kern, spectrum), plus, True)

    re, im = spectrum
    scale = 2.0 * (re * re + im * im - meas[...])
    returned = transform((scale * re, scale * im), plus, False)
    for k in reversed(range(slices)):
        re, im = cmul_conj(kept[k], returned)
        terms[own ^ k, 0] = (re * grad_scale).astype(bf16)
        terms[own ^ k, 1] = (im * grad_scale).astype(bf16)
        if k > 0:
            spectrum = transform(cmul_conj(t_of(k), returned), minus, False)
            returned = transform(cmul_conj(kern, spectrum), plus, False)
    for m in range(slices):
        out_refs[m][...] = terms[m]


def run_waves(probe, kern, windows, measured):
    slices = len(windows)
    window = probe.shape[-1]
    left, right = dft_matrices(window)
    vmem = pl.BlockSpec(memory_space=pltpu.VMEM)
    return pl.pallas_call(
        functools.partial(wave_kernel, slices),
        out_shape=[jax.ShapeDtypeStruct((2, window, window), bf16)] * slices,
        in_specs=[vmem] * (4 + slices + len(measured)),
        out_specs=[vmem] * slices,
        scratch_shapes=[
            pltpu.VMEM((slices, 2, window, window), bf16),
            pltpu.VMEM((slices, 2, window, window), bf16),
            pltpu.VMEM((window, window), f32),
        ],
        compiler_params=pltpu.CompilerParams(vmem_limit_bytes=40 * 1024 * 1024),
        name="run_waves",
    )(probe, kern, jnp.asarray(left), jnp.asarray(right), *windows, *measured)


def place_kernel(depth, *rest):
    out_ref, canvas = rest[-2:]
    groups = (len(rest) - 2) // (depth + 1)
    table_refs, terms_refs = rest[:groups], rest[groups:-2]
    _, stripe, cols = out_ref.shape
    window = terms_refs[0].shape[-1]
    wide = window + 128
    own, _, dp_index = indices(1)
    first_row = dp_index * stripe
    canvas[:, window : window + stripe, :] = jnp.zeros((2, stripe, canvas.shape[2]), f32)
    for group in range(groups):
        for m in range(depth):
            terms_ref = terms_refs[group * depth + m]
            row = table_refs[group][own ^ m, 0] - first_row + window
            col = table_refs[group][own ^ m, 1]
            row_base = pl.multiple_of((row >> 3) << 3, 8)
            col_base = pl.multiple_of((col >> 7) << 7, 128)

            @pl.when((row > 0) & (row < window + stripe))
            def _():
                for part in range(2):
                    block = terms_ref[part].astype(f32)
                    block = jnp.concatenate([block, jnp.zeros((8, window), f32)], axis=0)
                    block = pltpu.roll(block, row - row_base, 0)
                    block = jnp.concatenate([block, jnp.zeros((window + 8, 128), f32)], axis=1)
                    block = pltpu.roll(block, col - col_base, 1)
                    at = (part, pl.ds(row_base, window + 8), pl.ds(col_base, wide))
                    canvas[at] = canvas[at] + block

    out_ref[...] = canvas[:, window : window + stripe, :cols]


def place_windows(tables, terms, depth, stripe, cols):
    window = terms[0].shape[-1]
    vmem = pl.BlockSpec(memory_space=pltpu.VMEM)
    smem = pl.BlockSpec(memory_space=pltpu.SMEM)
    tall = window + (stripe + 7) // 8 * 8 + window + 8
    return pl.pallas_call(
        functools.partial(place_kernel, depth),
        out_shape=jax.ShapeDtypeStruct((2, stripe, cols), f32),
        in_specs=[smem] * len(tables) + [vmem] * len(terms),
        out_specs=vmem,
        scratch_shapes=[pltpu.VMEM((2, tall, cols + 128), f32)],
        compiler_params=pltpu.CompilerParams(vmem_limit_bytes=40 * 1024 * 1024),
        name="place_windows",
    )(*tables, *terms)


def swap(block, depth_distance, dp_distance):
    depth, dp = lax.axis_size("depth"), lax.axis_size("dp")
    route = [
        (d * dp + j, (d ^ depth_distance) * dp + (j ^ dp_distance))
        for d in range(depth)
        for j in range(dp)
    ]
    return lax.ppermute(block, ("depth", "dp"), route)


def on_device(object_slices, positions, probe_field, propagator_phase, measured):
    depth, dp = lax.axis_size("depth"), lax.axis_size("dp")
    clusters = depth // positions.shape[0]
    members = dp // clusters
    window = probe_field.shape[-1]
    rows, cols = object_slices.shape[-2:]
    homes = range(1, clusters)
    all_homes = [positions] + [swap(positions, 0, m * members) for m in homes]
    windows, table = take_windows(object_slices[0], all_homes, window, depth)
    windows = [windows[0]] + [swap(windows[m], m, 0) for m in range(1, depth)]
    targets = [measured] + [swap(measured, 0, m * members) for m in homes]
    kern = jnp.stack([jnp.cos(propagator_phase), jnp.sin(propagator_phase)])
    terms = run_waves(probe_field, kern, windows, targets)

    tables = [table] + [swap(table, 0, i) for i in range(1, members)]
    near = []
    for i in range(0, members, 2):
        near.append([terms[m] if m == i == 0 else swap(terms[m], m, i) for m in range(depth)])
    spread = []
    for i in range(members):
        group = near[i // 2]
        spread += group if i % 2 == 0 else [swap(x, 0, 1) for x in group]
    return place_windows(tables, spread, depth, rows // dp, cols)[None]


def solution(mesh):
    placed = (P("depth", None, None, None), P("dp", None), P(), P(), P("dp", None, None))
    return jax.shard_map(
        on_device,
        mesh=mesh,
        in_specs=placed,
        out_specs=P("depth", None, "dp", None),
        check_vma=False,
    )
```

```python
import functools
import math

import jax
import jax.numpy as jnp
import numpy as np
from jax import lax
from jax.experimental import pallas as pl
from jax.experimental.pallas import tpu as pltpu
from jax.sharding import PartitionSpec as P

grad_scale = 0.03125
f32 = jnp.float32
bf16 = jnp.bfloat16


def dft_matrices(size):
    k = np.arange(size)
    angles = 2.0 * np.pi * ((k[:, None] * k[None, :]) % size) / size
    c = np.cos(angles) / math.sqrt(size)
    s = np.sin(angles) / math.sqrt(size)
    plus = np.block([[c, s], [-s, c]]).astype(np.float32)
    minus = np.block([[c, -s], [s, c]]).astype(np.float32)
    parts = []
    for full in (plus, minus):
        high = full.astype(bf16)
        low = (full - high.astype(np.float32)).astype(bf16)
        parts.append((high, low))
    (ph, plo), (mh, mlo) = parts
    right = np.stack([np.concatenate([ph, ph, plo], 0), np.concatenate([mh, mh, mlo], 0)])
    left = np.stack([np.concatenate([mh, mh, mlo], 1), np.concatenate([ph, ph, plo], 1)])
    return left, right


def taken_by(d, i, members, dp, positions):
    per_home = positions // dp
    home = lax.div(d, per_home) * members + i
    return home * per_home + lax.rem(d, per_home)


def window_kernel(members, pos_ref, obj_ref, phase_ref, out_ref, kern_ref, buf, sems):
    depth, _, window, _ = out_ref.shape
    rows, cols = obj_ref.shape[-2:]
    tall, wide = buf.shape[-2:]
    lane = lax.rem(lax.axis_index("dp"), members)

    def corner(d):
        at = taken_by(d, lane, members, lax.axis_size("dp"), pos_ref.shape[0])
        row, col = pos_ref[at, 0], pos_ref[at, 1]
        row_base = pl.multiple_of(jnp.minimum(row >> 3, (rows - tall) // 8) * 8, 8)
        col_base = pl.multiple_of(jnp.minimum(col >> 7, (cols - wide) // 128) * 128, 128)
        return row_base, col_base, row - row_base, col - col_base

    def copy(d):
        row_base, col_base, _, _ = corner(d)
        return pltpu.make_async_copy(
            obj_ref.at[:, pl.ds(row_base, tall), pl.ds(col_base, wide)], buf.at[d], sems.at[d]
        )

    for d in range(depth):
        copy(d).start()
    kern_ref[0] = jnp.cos(phase_ref[...])
    kern_ref[1] = jnp.sin(phase_ref[...])
    for d in range(depth):
        copy(d).wait()
        _, _, row_off, col_off = corner(d)
        lift = jnp.where(row_off == 0, 0, tall - row_off)
        shift = jnp.where(col_off == 0, 0, wide - col_off)
        for part in range(2):
            block = pltpu.roll(buf[d, part], shift, 1)[:, :window]
            block = pltpu.roll(block, lift, 0)[:window]
            out_ref[d, part] = block.astype(bf16)


def take_windows(all_positions, obj, phase, depth, members):
    window = phase.shape[-1]
    tall, wide = window + 8, window + 128
    vmem = pl.BlockSpec(memory_space=pltpu.VMEM)
    return pl.pallas_call(
        functools.partial(window_kernel, members),
        out_shape=[
            jax.ShapeDtypeStruct((depth, 2, window, window), bf16),
            jax.ShapeDtypeStruct((2, window, window), f32),
        ],
        in_specs=[
            pl.BlockSpec(memory_space=pltpu.SMEM),
            pl.BlockSpec(memory_space=pl.ANY),
            vmem,
        ],
        out_specs=[vmem, vmem],
        scratch_shapes=[
            pltpu.VMEM((depth, 2, tall, wide), f32),
            pltpu.SemaphoreType.DMA((depth,)),
        ],
        name="take_windows",
    )(all_positions, obj, phase)


def split(x):
    high = x.astype(bf16)
    return high, (x - high.astype(f32)).astype(bf16)


def cmul(a, b):
    return a[0] * b[0] - a[1] * b[1], a[0] * b[1] + a[1] * b[0]


def cmul_conj(a, b):
    return a[0] * b[0] + a[1] * b[1], a[0] * b[1] - a[1] * b[0]


def wave_kernel(members, probe_ref, kern_ref, left_ref, right_ref, t_ref, *rest):
    meas_refs, (out_ref, meas) = rest[:-2], rest[-2:]
    slices = t_ref.shape[0]
    copies = out_ref.shape[0] // slices
    window = probe_ref.shape[-1]
    per_home = slices // len(meas_refs)
    own, cluster = lax.axis_index("depth"), lax.div(lax.axis_index("dp"), members)
    home = lax.div(own, per_home)
    for m, meas_ref in enumerate(meas_refs):

        @pl.when(home ^ cluster == m)
        def _():
            meas[...] = meas_ref[lax.rem(own, per_home)]

    def t_of(k):
        return t_ref[k, 0].astype(f32), t_ref[k, 1].astype(f32)

    def passes(x, axis, exact):
        if not exact:
            return x.astype(bf16)
        high, low = split(x)
        return jnp.concatenate([high, low, high], axis=axis)

    def rows(field, sign, exact):
        x = passes(jnp.concatenate(field, axis=0), 0, exact)
        y = jnp.dot(left_ref[sign, :, : x.shape[0]], x, preferred_element_type=f32)
        return y[:window], y[window:]

    def cols(field, sign, exact):
        x = passes(jnp.concatenate(field, axis=1), 1, exact)
        y = jnp.dot(x, right_ref[sign, : x.shape[1]], preferred_element_type=f32)
        return y[:, :window], y[:, window:]

    plus, minus = 0, 1

    def transform(field, sign, exact):
        return cols(rows(field, sign, exact), sign, exact)

    kern = (kern_ref[0], kern_ref[1])
    psi = (probe_ref[0], probe_ref[1])
    kept = []
    for k in range(slices):
        kept.append(psi)
        spectrum = transform(cmul(t_of(k), psi), minus, True)
        if k < slices - 1:
            psi = transform(cmul(kern, spectrum), plus, True)

    re, im = spectrum
    scale = 2.0 * (re * re + im * im - meas[...])
    returned = transform((scale * re, scale * im), plus, False)
    for k in reversed(range(slices)):
        re, im = cmul_conj(kept[k], returned)
        term = (re * grad_scale).astype(bf16), (im * grad_scale).astype(bf16)
        for n in range(copies):
            for part in range(2):
                out_ref[k * copies + n, part] = term[part]
        if k > 0:
            spectrum = transform(cmul_conj(t_of(k), returned), minus, False)
            returned = transform(cmul_conj(kern, spectrum), plus, False)


def run_waves(probe, kern, windows, measured, members):
    slices = windows.shape[0]
    window = probe.shape[-1]
    left, right = dft_matrices(window)
    vmem = pl.BlockSpec(memory_space=pltpu.VMEM)
    return pl.pallas_call(
        functools.partial(wave_kernel, members),
        out_shape=jax.ShapeDtypeStruct((slices * members // 2, 2, window, window), bf16),
        in_specs=[vmem] * (5 + len(measured)),
        out_specs=vmem,
        scratch_shapes=[pltpu.VMEM((window, window), f32)],
        compiler_params=pltpu.CompilerParams(vmem_limit_bytes=40 * 1024 * 1024),
        name="run_waves",
    )(probe, kern, jnp.asarray(left), jnp.asarray(right), windows, *measured)


def place_kernel(members, pos_ref, *rest):
    terms_refs, (out_ref, canvas) = rest[:2], rest[2:]
    _, stripe, cols = out_ref.shape
    count, _, window, _ = terms_refs[0].shape
    pairs = members // 2
    wide = window + 128
    dp_index = lax.axis_index("dp")
    first_row = dp_index * stripe
    canvas[:, window : window + stripe, :] = jnp.zeros((2, stripe, canvas.shape[2]), f32)
    for other, terms_ref in enumerate(terms_refs):
        for n in range(count):
            i = n % pairs * 2 + (dp_index + other) % 2
            at = taken_by(n // pairs, i, members, lax.axis_size("dp"), pos_ref.shape[0])
            row = pos_ref[at, 0] - first_row + window
            col = pos_ref[at, 1]
            row_base = pl.multiple_of((row >> 3) << 3, 8)
            col_base = pl.multiple_of((col >> 7) << 7, 128)

            @pl.when((row > 0) & (row < window + stripe))
            def _():
                for part in range(2):
                    block = terms_ref[n, part].astype(f32)
                    block = jnp.concatenate([block, jnp.zeros((8, window), f32)], axis=0)
                    block = pltpu.roll(block, row - row_base, 0)
                    block = jnp.concatenate([block, jnp.zeros((window + 8, 128), f32)], axis=1)
                    block = pltpu.roll(block, col - col_base, 1)
                    put = (part, pl.ds(row_base, window + 8), pl.ds(col_base, wide))
                    canvas[put] = canvas[put] + block

    out_ref[...] = canvas[:, window : window + stripe, :cols]


def place_windows(positions, own, other, members, stripe, cols):
    window = own.shape[-1]
    vmem = pl.BlockSpec(memory_space=pltpu.VMEM)
    tall = window + (stripe + 7) // 8 * 8 + window + 8
    return pl.pallas_call(
        functools.partial(place_kernel, members),
        out_shape=jax.ShapeDtypeStruct((2, stripe, cols), f32),
        in_specs=[pl.BlockSpec(memory_space=pltpu.SMEM), vmem, vmem],
        out_specs=vmem,
        scratch_shapes=[pltpu.VMEM((2, tall, cols + 128), f32)],
        compiler_params=pltpu.CompilerParams(vmem_limit_bytes=40 * 1024 * 1024),
        name="place_windows",
    )(positions, own, other)


def swap(block, distance):
    return lax.ppermute(block, "dp", [(j, j ^ distance) for j in range(lax.axis_size("dp"))])


def on_device(object_slices, positions, probe_field, propagator_phase, measured):
    depth, dp = lax.axis_size("depth"), lax.axis_size("dp")
    clusters = depth // positions.shape[0]
    members = dp // clusters
    rows, cols = object_slices.shape[-2:]

    all_positions = lax.all_to_all(jnp.tile(positions, (dp, 1)), "dp", 0, 0, tiled=True)
    windows, kern = take_windows(all_positions, object_slices[0], propagator_phase, depth, members)
    windows = lax.all_to_all(windows, "depth", 0, 0, tiled=True)
    targets = [measured] + [swap(measured, m * members) for m in range(1, clusters)]
    terms = run_waves(probe_field, kern, windows, targets, members)

    groups = [
        [d * dp + w * members + i for d in range(depth) for i in range(core, members, 2)]
        for w in range(clusters)
        for core in range(2)
    ]
    terms = lax.all_to_all(terms, ("depth", "dp"), 0, 0, axis_index_groups=groups, tiled=True)
    return place_windows(all_positions, terms, swap(terms, 1), members, rows // dp, cols)[None]


def solution(mesh):
    placed = (P("depth", None, None, None), P("dp", None), P(), P(), P("dp", None, None))
    return jax.shard_map(
        on_device,
        mesh=mesh,
        in_specs=placed,
        out_specs=P("depth", None, "dp", None),
        check_vma=False,
    )
```

```python
import functools
import math

import jax
import jax.numpy as jnp
import numpy as np
from jax import lax
from jax.experimental import pallas as pl
from jax.experimental.pallas import tpu as pltpu
from jax.sharding import PartitionSpec as P

grad_scale = 0.03125
f32 = jnp.float32
bf16 = jnp.bfloat16


def dft_matrices(size):
    k = np.arange(size)
    angles = 2.0 * np.pi * ((k[:, None] * k[None, :]) % size) / size
    c = np.cos(angles) / math.sqrt(size)
    s = np.sin(angles) / math.sqrt(size)
    plus = np.block([[c, s], [-s, c]]).astype(np.float32)
    minus = np.block([[c, -s], [s, c]]).astype(np.float32)
    parts = []
    for full in (plus, minus):
        high = full.astype(bf16)
        low = (full - high.astype(np.float32)).astype(bf16)
        parts.append((high, low))
    (ph, plo), (mh, mlo) = parts
    right = np.stack([np.concatenate([ph, ph, plo], 0), np.concatenate([mh, mh, mlo], 0)])
    left = np.stack([np.concatenate([mh, mh, mlo], 1), np.concatenate([ph, ph, plo], 1)])
    return left, right


def indices(clusters):
    dp_index = lax.axis_index("dp")
    return lax.axis_index("depth"), lax.div(dp_index, lax.axis_size("dp") // clusters), dp_index


def window_kernel(obj_ref, phase_ref, *rest):
    buf, sems = rest[-2:]
    depth = buf.shape[0]
    clusters = len(rest) - 4 - depth
    pos_refs = rest[:clusters]
    out_refs = rest[clusters : clusters + depth]
    table_ref, kern_ref = rest[clusters + depth : -2]
    own, cluster, _ = indices(clusters)
    per_home = depth // clusters
    window = out_refs[0].shape[-1]
    rows, cols = obj_ref.shape[-2:]
    tall, wide = buf.shape[-2:]

    for home in range(clusters):
        for q in range(per_home):
            for axis in range(2):
                value = pos_refs[0][q, axis]
                for m in range(1, clusters):
                    value = jnp.where(home ^ cluster == m, pos_refs[m][q, axis], value)
                table_ref[home * per_home + q, axis] = value

    def corner(m):
        at = own ^ m
        row, col = table_ref[at, 0], table_ref[at, 1]
        row_base = pl.multiple_of(jnp.minimum(row >> 3, (rows - tall) // 8) * 8, 8)
        col_base = pl.multiple_of(jnp.minimum(col >> 7, (cols - wide) // 128) * 128, 128)
        return row_base, col_base, row - row_base, col - col_base

    def copy(m):
        row_base, col_base, _, _ = corner(m)
        return pltpu.make_async_copy(
            obj_ref.at[:, pl.ds(row_base, tall), pl.ds(col_base, wide)], buf.at[m], sems.at[m]
        )

    for m in range(depth):
        copy(m).start()
    kern_ref[0] = jnp.cos(phase_ref[...])
    kern_ref[1] = jnp.sin(phase_ref[...])
    for m in range(depth):
        copy(m).wait()
        _, _, row_off, col_off = corner(m)
        lift = jnp.where(row_off == 0, 0, tall - row_off)
        shift = jnp.where(col_off == 0, 0, wide - col_off)
        for part in range(2):
            block = pltpu.roll(buf[m, part], shift, 1)[:, :window]
            block = pltpu.roll(block, lift, 0)[:window]
            out_refs[m][part] = block.astype(bf16)


def take_windows(obj, phase, positions, depth):
    window = phase.shape[-1]
    tall, wide = window + 8, window + 128
    smem = pl.BlockSpec(memory_space=pltpu.SMEM)
    vmem = pl.BlockSpec(memory_space=pltpu.VMEM)
    out = pl.pallas_call(
        window_kernel,
        out_shape=[jax.ShapeDtypeStruct((2, window, window), bf16)] * depth
        + [
            jax.ShapeDtypeStruct((depth, 2), jnp.int32),
            jax.ShapeDtypeStruct((2, window, window), f32),
        ],
        in_specs=[pl.BlockSpec(memory_space=pl.ANY), vmem] + [smem] * len(positions),
        out_specs=[vmem] * depth + [smem, vmem],
        scratch_shapes=[
            pltpu.VMEM((depth, 2, tall, wide), f32),
            pltpu.SemaphoreType.DMA((depth,)),
        ],
        name="take_windows",
    )(obj, phase, *positions)
    return list(out[:depth]), out[depth], out[depth + 1]


def split(x):
    high = x.astype(bf16)
    return high, (x - high.astype(f32)).astype(bf16)


def cmul(a, b):
    return a[0] * b[0] - a[1] * b[1], a[0] * b[1] + a[1] * b[0]


def cmul_conj(a, b):
    return a[0] * b[0] + a[1] * b[1], a[0] * b[1] - a[1] * b[0]


def wave_kernel(slices, clusters, probe_ref, kern_ref, left_ref, right_ref, *rest):
    t_refs, rest = rest[:slices], rest[slices:]
    meas_refs = rest[:clusters]
    out_ref, trans, meas = rest[-3:]
    own, cluster, _ = indices(clusters)
    per_home = slices // clusters
    window = probe_ref.shape[-1]

    for m in range(slices):
        trans[own ^ m] = t_refs[m][...]
    home = lax.div(own, per_home)
    for m, meas_ref in enumerate(meas_refs):

        @pl.when(home ^ cluster == m)
        def _():
            meas[...] = meas_ref[lax.rem(own, per_home)]

    def t_of(k):
        return trans[k, 0].astype(f32), trans[k, 1].astype(f32)

    def passes(x, axis, exact):
        if not exact:
            return x.astype(bf16)
        high, low = split(x)
        return jnp.concatenate([high, low, high], axis=axis)

    def rows(field, sign, exact):
        x = passes(jnp.concatenate(field, axis=0), 0, exact)
        y = jnp.dot(left_ref[sign, :, : x.shape[0]], x, preferred_element_type=f32)
        return y[:window], y[window:]

    def cols(field, sign, exact):
        x = passes(jnp.concatenate(field, axis=1), 1, exact)
        y = jnp.dot(x, right_ref[sign, : x.shape[1]], preferred_element_type=f32)
        return y[:, :window], y[:, window:]

    plus, minus = 0, 1

    def transform(field, sign, exact):
        return cols(rows(field, sign, exact), sign, exact)

    kern = (kern_ref[0], kern_ref[1])
    psi = (probe_ref[0], probe_ref[1])
    kept = []
    for k in range(slices):
        kept.append(psi)
        spectrum = transform(cmul(t_of(k), psi), minus, True)
        if k < slices - 1:
            psi = transform(cmul(kern, spectrum), plus, True)

    re, im = spectrum
    scale = 2.0 * (re * re + im * im - meas[...])
    returned = transform((scale * re, scale * im), plus, False)
    for k in reversed(range(slices)):
        re, im = cmul_conj(kept[k], returned)
        out_ref[own ^ k, 0] = (re * grad_scale).astype(bf16)
        out_ref[own ^ k, 1] = (im * grad_scale).astype(bf16)
        if k > 0:
            spectrum = transform(cmul_conj(t_of(k), returned), minus, False)
            returned = transform(cmul_conj(kern, spectrum), plus, False)


def run_waves(probe, kern, windows, measured, tables):
    slices = len(windows)
    window = probe.shape[-1]
    left, right = dft_matrices(window)
    vmem = pl.BlockSpec(memory_space=pltpu.VMEM)
    smem = pl.BlockSpec(memory_space=pltpu.SMEM)
    return pl.pallas_call(
        functools.partial(wave_kernel, slices, len(measured)),
        out_shape=jax.ShapeDtypeStruct((slices, 2, window, window), bf16),
        in_specs=[vmem] * (4 + slices + len(measured)) + [smem] * len(tables),
        out_specs=vmem,
        scratch_shapes=[
            pltpu.VMEM((slices, 2, window, window), bf16),
            pltpu.VMEM((window, window), f32),
        ],
        compiler_params=pltpu.CompilerParams(vmem_limit_bytes=40 * 1024 * 1024),
        name="run_waves",
    )(probe, kern, jnp.asarray(left), jnp.asarray(right), *windows, *measured, *tables)


def pack_kernel(own_ref, other_ref, *out_refs):
    for m, out_ref in enumerate(out_refs):
        out_ref[0] = own_ref[m]
        out_ref[1] = other_ref[m]


def pack(own, other):
    vmem = pl.BlockSpec(memory_space=pltpu.VMEM)
    return pl.pallas_call(
        pack_kernel,
        out_shape=[jax.ShapeDtypeStruct((2,) + own.shape[1:], own.dtype)] * own.shape[0],
        in_specs=[vmem, vmem],
        out_specs=[vmem] * own.shape[0],
        name="pack_terms",
    )(own, other)


def place_kernel(depth, planes, *rest):
    out_ref, canvas = rest[-2:]
    table_refs = rest[: 2 * planes]
    own_block, *blocks = rest[2 * planes : -2]
    _, stripe, cols = out_ref.shape
    window = own_block.shape[-1]
    wide = window + 128
    own, dp_index = lax.axis_index("depth"), lax.axis_index("dp")
    core = lax.rem(dp_index, 2)
    first_row = dp_index * stripe
    canvas[:, window : window + stripe, :] = jnp.zeros((2, stripe, canvas.shape[2]), f32)

    def place(block_ref, n, at, valid):
        row, col = at
        row = row - first_row + window
        row_base = pl.multiple_of((row >> 3) << 3, 8)
        col_base = pl.multiple_of((col >> 7) << 7, 128)

        @pl.when((row > 0) & (row < window + stripe) & valid)
        def _():
            for part in range(2):
                block = block_ref[n, part].astype(f32)
                block = jnp.concatenate([block, jnp.zeros((8, window), f32)], axis=0)
                block = pltpu.roll(block, row - row_base, 0)
                block = jnp.concatenate([block, jnp.zeros((window + 8, 128), f32)], axis=1)
                block = pltpu.roll(block, col - col_base, 1)
                put = (part, pl.ds(row_base, window + 8), pl.ds(col_base, wide))
                canvas[put] = canvas[put] + block

    def position(plane, other, d):
        return [table_refs[2 * plane + other][d, axis] for axis in range(2)]

    for n in range(2):
        place(own_block, n, position(0, n, own), True)
    for held in range(2):
        for r in range(planes // 2):
            for m in range(depth):
                block_ref = blocks[(held * (planes // 2) + r) * depth + m]
                for n in range(2):
                    choice = []
                    for h in range(2):
                        first = position(2 * r + h, held ^ n, own ^ m)
                        choice.append(first)
                    by = core ^ held
                    at = [jnp.where(by == 0, choice[0][axis], choice[1][axis]) for axis in range(2)]
                    place(block_ref, n, at, (by == 1) if r == m == 0 else True)

    out_ref[...] = canvas[:, window : window + stripe, :cols]


def place_windows(tables, own_block, blocks, depth, stripe, cols):
    window = own_block.shape[-1]
    vmem = pl.BlockSpec(memory_space=pltpu.VMEM)
    smem = pl.BlockSpec(memory_space=pltpu.SMEM)
    tall = window + (stripe + 7) // 8 * 8 + window + 8
    return pl.pallas_call(
        functools.partial(place_kernel, depth, len(tables) // 2),
        out_shape=jax.ShapeDtypeStruct((2, stripe, cols), f32),
        in_specs=[smem] * len(tables) + [vmem] * (1 + len(blocks)),
        out_specs=vmem,
        scratch_shapes=[pltpu.VMEM((2, tall, cols + 128), f32)],
        compiler_params=pltpu.CompilerParams(vmem_limit_bytes=48 * 1024 * 1024),
        name="place_windows",
    )(*tables, own_block, *blocks)


def swap(block, depth_distance, dp_distances):
    depth, dp = lax.axis_size("depth"), lax.axis_size("dp")
    route = [
        (d * dp + j, (d ^ depth_distance) * dp + (j ^ dp_distances[j % 2]))
        for d in range(depth)
        for j in range(dp)
        if depth_distance or dp_distances[j % 2]
    ]
    return lax.ppermute(block, ("depth", "dp"), route)


def on_device(object_slices, positions, probe_field, propagator_phase, measured):
    depth, dp = lax.axis_size("depth"), lax.axis_size("dp")
    clusters = depth // positions.shape[0]
    members = dp // clusters
    planes = members // 2
    rows, cols = object_slices.shape[-2:]
    across = (1, 1)

    homes = [(m * members, m * members) for m in range(1, clusters)]
    all_homes = [positions] + [swap(positions, 0, home) for home in homes]
    windows, table, kern = take_windows(object_slices[0], propagator_phase, all_homes, depth)
    windows = [windows[0]] + [swap(windows[m], m, (0, 0)) for m in range(1, depth)]
    late, kern = lax.optimization_barrier((measured, kern))
    targets = [measured] + [swap(late, 0, home) for home in homes]
    tables = []
    for plane in range(planes):
        near = swap(table, 0, (2 * plane, 2 * plane)) if plane else table
        tables += [near, swap(near, 0, across)]
    terms = run_waves(probe_field, kern, windows, targets, tables)

    packed = pack(terms, swap(terms, 0, across))
    arrived = [
        swap(packed[m], m, (4 * r, 4 * r + 2)) for r in range(planes // 2) for m in range(depth)
    ]
    passed = [swap(block, 0, across) for block in arrived]
    out = place_windows(tables, packed[0], arrived + passed, depth, rows // dp, cols)
    return out[None]


def solution(mesh):
    placed = (P("depth", None, None, None), P("dp", None), P(), P(), P("dp", None, None))
    return jax.shard_map(
        on_device,
        mesh=mesh,
        in_specs=placed,
        out_specs=P("depth", None, "dp", None),
        check_vma=False,
    )
```

```python
import functools
import math

import jax
import jax.numpy as jnp
import numpy as np
from jax import lax
from jax.experimental import pallas as pl
from jax.experimental.pallas import tpu as pltpu
from jax.sharding import PartitionSpec as P

grad_scale = 0.03125
f32 = jnp.float32
bf16 = jnp.bfloat16


def dft_matrices(size):
    k = np.arange(size)
    angles = 2.0 * np.pi * ((k[:, None] * k[None, :]) % size) / size
    c = np.cos(angles) / math.sqrt(size)
    s = np.sin(angles) / math.sqrt(size)
    plus = np.block([[c, s], [-s, c]]).astype(np.float32)
    minus = np.block([[c, -s], [s, c]]).astype(np.float32)
    parts = []
    for full in (plus, minus):
        high = full.astype(bf16)
        low = (full - high.astype(np.float32)).astype(bf16)
        parts.append((high, low))
    (ph, plo), (mh, mlo) = parts
    right = np.stack([np.concatenate([ph, ph, plo], 0), np.concatenate([mh, mh, mlo], 0)])
    left = np.stack([np.concatenate([mh, mh, mlo], 1), np.concatenate([ph, ph, plo], 1)])
    return left, right


code_rows = 16


def window_kernel(members, obj_ref, *rest):
    table, buf, table_sems, sems = rest[-4:]
    clusters, count = buf.shape[:2]
    pos_refs, out_refs, code_ref = rest[:clusters], rest[clusters:-5], rest[-5]
    window = out_refs[0].shape[-1]
    rows, cols = obj_ref.shape[-2:]
    tall, wide = buf.shape[-2:]
    cluster = lax.div(lax.axis_index("dp"), members)
    home = lax.div(lax.axis_index("depth"), 2)

    fetches = [
        pltpu.make_async_copy(pos_refs[m], table.at[m], table_sems.at[m]) for m in range(clusters)
    ]
    for fetch in fetches:
        fetch.start()
    for fetch in fetches:
        fetch.wait()

    def corner(m, p):
        at = home ^ cluster ^ m
        row, col = table[at, p, 0], table[at, p, 1]
        row_base = pl.multiple_of(jnp.minimum(row >> 3, (rows - tall) // 8) * 8, 8)
        col_base = pl.multiple_of(jnp.minimum(col >> 7, (cols - wide) // 128) * 128, 128)
        return row_base, col_base, row - row_base, col - col_base

    def copy(m, p):
        row_base, col_base, _, _ = corner(m, p)
        return pltpu.make_async_copy(
            obj_ref.at[:, pl.ds(row_base, tall), pl.ds(col_base, wide)], buf.at[m, p], sems.at[m, p]
        )

    order = [(m, p) for m in reversed(range(clusters)) for p in range(count)]
    for m, p in order:
        copy(m, p).start()
    line = lax.broadcasted_iota(jnp.int32, (code_rows, window), 0)
    for p in range(count):
        row, col = table[home ^ cluster, p, 0], table[home ^ cluster, p, 1]
        code = jnp.where(line == 0, row >> 3, jnp.where(line == 1, row & 7, 0))
        code = jnp.where(line == 2, col >> 3, jnp.where(line == 3, col & 7, code))
        code_ref[p] = code.astype(f32).astype(bf16)
    for m, p in order:
        copy(m, p).wait()
        _, _, row_off, col_off = corner(m, p)
        lift = jnp.where(row_off == 0, 0, tall - row_off)
        shift = jnp.where(col_off == 0, 0, wide - col_off)
        for part in range(2):
            block = pltpu.roll(buf[m, p, part], shift, 1)[:, :window]
            block = pltpu.roll(block, lift, 0)[:window]
            out_refs[m][p, part] = block.astype(bf16)


def take_windows(obj, positions, window, members):
    clusters, count = len(positions), positions[0].shape[0]
    tall, wide = window + 8, window + 128
    any_space = pl.BlockSpec(memory_space=pl.ANY)
    vmem = pl.BlockSpec(memory_space=pltpu.VMEM)
    out = pl.pallas_call(
        functools.partial(window_kernel, members),
        out_shape=[jax.ShapeDtypeStruct((count, 2, window, window), bf16)] * clusters
        + [jax.ShapeDtypeStruct((count, code_rows, window), bf16)],
        in_specs=[any_space] * (1 + clusters),
        out_specs=[vmem] * (clusters + 1),
        scratch_shapes=[
            pltpu.SMEM((clusters, count, 2), jnp.int32),
            pltpu.VMEM((clusters, count, 2, tall, wide), f32),
            pltpu.SemaphoreType.DMA((clusters,)),
            pltpu.SemaphoreType.DMA((clusters, count)),
        ],
        compiler_params=pltpu.CompilerParams(vmem_limit_bytes=24 * 1024 * 1024),
        name="take_windows",
    )(obj, *positions)
    return out[:clusters], out[clusters]


def split(x):
    high = x.astype(bf16)
    return high, (x - high.astype(f32)).astype(bf16)


def cmul(a, b):
    return a[0] * b[0] - a[1] * b[1], a[0] * b[1] + a[1] * b[0]


def cmul_conj(a, b):
    return a[0] * b[0] + a[1] * b[1], a[0] * b[1] - a[1] * b[0]


def wave_kernel(members, clusters, probe_ref, kern_ref, left_ref, right_ref, code_ref, *rest):
    trans, terms, meas = rest[-3:]
    slices, count, _, _, window = trans.shape
    meas_refs, t_refs, out_refs = rest[:clusters], rest[clusters : clusters + slices], rest[clusters + slices : -3]
    own, cluster = lax.axis_index("depth"), lax.div(lax.axis_index("dp"), members)
    everyone = range(count)

    for m in range(slices):
        trans[own ^ m] = t_refs[m][...]
    for m, meas_ref in enumerate(meas_refs):

        @pl.when(lax.div(own, 2) ^ cluster == m)
        def _():
            meas[...] = meas_ref[...]

    def t_of(k, p):
        return trans[k, p, 0].astype(f32), trans[k, p, 1].astype(f32)

    def passes(x, axis, exact):
        if not exact:
            return x.astype(bf16)
        high, low = split(x)
        return jnp.concatenate([high, low, high], axis=axis)

    def rows(fields, sign, exact):
        x = jnp.concatenate([jnp.concatenate(f, axis=0) for f in fields], axis=1)
        x = passes(x, 0, exact)
        y = jnp.dot(left_ref[sign, :, : x.shape[0]], x, preferred_element_type=f32)
        cut = [y[:, p * window : (p + 1) * window] for p in everyone]
        return [(c[:window], c[window:]) for c in cut]

    def cols(fields, sign, exact):
        x = jnp.concatenate([jnp.concatenate(f, axis=1) for f in fields], axis=0)
        x = passes(x, 1, exact)
        y = jnp.dot(x, right_ref[sign, : x.shape[1]], preferred_element_type=f32)
        cut = [y[p * window : (p + 1) * window] for p in everyone]
        return [(c[:, :window], c[:, window:]) for c in cut]

    plus, minus = 0, 1

    def transform(fields, sign, exact):
        return cols(rows(fields, sign, exact), sign, exact)

    kern = (kern_ref[0], kern_ref[1])
    psi = [(probe_ref[0], probe_ref[1])] * count
    kept = []
    for k in range(slices):
        kept.append(psi)
        spectrum = transform([cmul(t_of(k, p), psi[p]) for p in everyone], minus, True)
        if k < slices - 1:
            psi = transform([cmul(kern, s) for s in spectrum], plus, True)

    def source(p):
        re, im = spectrum[p]
        scale = 2.0 * (re * re + im * im - meas[p])
        return scale * re, scale * im

    returned = transform([source(p) for p in everyone], plus, False)
    for k in reversed(range(slices)):
        for p in everyone:
            re, im = cmul_conj(kept[k][p], returned[p])
            terms[own ^ k, p, :window] = (re * grad_scale).astype(bf16)
            terms[own ^ k, p, window:] = (im * grad_scale).astype(bf16)
        if k > 0:
            chi = [cmul_conj(t_of(k, p), returned[p]) for p in everyone]
            spectrum = transform(chi, minus, False)
            returned = transform([cmul_conj(kern, s) for s in spectrum], plus, False)
    for n, out_ref in enumerate(out_refs):
        out_ref[:, : 2 * window] = terms[2 * n]
        out_ref[:, 2 * window :] = code_ref[...]


def run_waves(probe, kern, code, measured, windows, members):
    slices, count, window = len(windows), code.shape[0], code.shape[-1]
    left, right = dft_matrices(window)
    vmem = pl.BlockSpec(memory_space=pltpu.VMEM)
    block = jax.ShapeDtypeStruct((count, 2 * window + code_rows, window), bf16)
    return pl.pallas_call(
        functools.partial(wave_kernel, members, len(measured)),
        out_shape=[block] * (slices // 2),
        in_specs=[vmem] * (5 + len(measured) + slices),
        out_specs=[vmem] * (slices // 2),
        scratch_shapes=[
            pltpu.VMEM((slices, count, 2, window, window), bf16),
            pltpu.VMEM((slices, count, 2 * window, window), bf16),
            pltpu.VMEM((count, window, window), f32),
        ],
        compiler_params=pltpu.CompilerParams(vmem_limit_bytes=40 * 1024 * 1024),
        name="run_waves",
    )(probe, kern, jnp.asarray(left), jnp.asarray(right), code, *measured, *windows)


def place_kernel(*refs):
    block_refs, (out_ref, canvas) = refs[:-2], refs[-2:]
    _, stripe, cols = out_ref.shape
    count, _, window = block_refs[0].shape
    wide = window + 128
    first_row = lax.axis_index("dp") * stripe
    canvas[:, window : window + stripe, :] = jnp.zeros((2, stripe, canvas.shape[2]), f32)
    corners = []
    for block_ref in block_refs:
        for p in range(count):
            code = block_ref[p, 2 * window :].astype(f32)
            row = (8.0 * code[0:1] + code[1:2]).astype(jnp.int32)
            col = (8.0 * code[2:3] + code[3:4]).astype(jnp.int32)
            corners.append((row[0, 0], col[0, 0]))
    for n, (row, col) in enumerate(corners):
        block_ref, p = block_refs[n // count], n % count
        row = row - first_row + window
        row_base = pl.multiple_of((row >> 3) << 3, 8)
        col_base = pl.multiple_of((col >> 7) << 7, 128)

        @pl.when((row > 0) & (row < window + stripe))
        def _():
            for part in range(2):
                block = block_ref[p, part * window : (part + 1) * window].astype(f32)
                block = jnp.concatenate([block, jnp.zeros((8, window), f32)], axis=0)
                block = pltpu.roll(block, row - row_base, 0)
                block = jnp.concatenate([block, jnp.zeros((window + 8, 128), f32)], axis=1)
                block = pltpu.roll(block, col - col_base, 1)
                put = (part, pl.ds(row_base, window + 8), pl.ds(col_base, wide))
                canvas[put] = canvas[put] + block

    out_ref[...] = canvas[:, window : window + stripe, :cols]


def place_windows(blocks, stripe, cols):
    window = blocks[0].shape[-1]
    vmem = pl.BlockSpec(memory_space=pltpu.VMEM)
    tall = window + (stripe + 7) // 8 * 8 + window + 8
    return pl.pallas_call(
        place_kernel,
        out_shape=jax.ShapeDtypeStruct((2, stripe, cols), f32),
        in_specs=[vmem] * len(blocks),
        out_specs=vmem,
        scratch_shapes=[pltpu.VMEM((2, tall, cols + 128), f32)],
        compiler_params=pltpu.CompilerParams(vmem_limit_bytes=48 * 1024 * 1024),
        name="place_windows",
    )(*blocks)


def swap(block, depth_distance, dp_distance):
    depth, dp = lax.axis_size("depth"), lax.axis_size("dp")
    route = [
        (d * dp + j, (d ^ depth_distance) * dp + (j ^ dp_distance))
        for d in range(depth)
        for j in range(dp)
    ]
    return lax.ppermute(block, ("depth", "dp"), route)


def on_device(object_slices, positions, probe_field, propagator_phase, measured):
    depth, dp = lax.axis_size("depth"), lax.axis_size("dp")
    clusters = depth // 2
    members = dp // clusters
    rows, cols = object_slices.shape[-2:]
    window = probe_field.shape[-1]

    homes = [m * members for m in range(1, clusters)]
    all_positions = [positions] + [swap(positions, 0, home) for home in homes]
    windows, code = take_windows(object_slices[0], all_positions, window, members)
    measured, phase, code = lax.optimization_barrier((measured, propagator_phase, code))
    windows = [windows[0]] + [swap(windows[m // 2], m, 0) for m in range(1, depth)]
    targets = [measured] + [swap(measured, 0, home) for home in homes]
    kern = jnp.stack([jnp.cos(phase), jnp.sin(phase)])
    terms = run_waves(probe_field, kern, code, targets, windows, members)

    blocks = [
        swap(terms[m // 2], m, plane) if m or plane else terms[0]
        for plane in range(0, members, 2)
        for m in range(0, depth, 2)
    ]
    blocks += [swap(block, 0, 1) for block in blocks]
    return place_windows(blocks, rows // dp, cols)[None]


def solution(mesh):
    placed = (P("depth", None, None, None), P("dp", None), P(), P(), P("dp", None, None))
    return jax.shard_map(
        on_device,
        mesh=mesh,
        in_specs=placed,
        out_specs=P("depth", None, "dp", None),
        check_vma=False,
    )
```

```python
import functools
import math

import jax
import jax.numpy as jnp
import numpy as np
from jax import lax
from jax.experimental import pallas as pl
from jax.experimental.pallas import tpu as pltpu
from jax.sharding import PartitionSpec as P

grad_scale = 0.03125
f32 = jnp.float32
bf16 = jnp.bfloat16


def dft_matrices(size):
    k = np.arange(size)
    angles = 2.0 * np.pi * ((k[:, None] * k[None, :]) % size) / size
    c = np.cos(angles) / math.sqrt(size)
    s = np.sin(angles) / math.sqrt(size)
    plus = np.block([[c, s], [-s, c]]).astype(np.float32)
    minus = np.block([[c, -s], [s, c]]).astype(np.float32)
    parts = []
    for full in (plus, minus):
        high = full.astype(bf16)
        low = (full - high.astype(np.float32)).astype(bf16)
        parts.append((high, low))
    (ph, plo), (mh, mlo) = parts
    right = np.stack([np.concatenate([ph, ph, plo], 0), np.concatenate([mh, mh, mlo], 0)])
    left = np.stack([np.concatenate([mh, mh, mlo], 1), np.concatenate([ph, ph, plo], 1)])
    return left, right


code_rows = 16


def fetch_kernel(obj_ref, out_ref, sem):
    copy = pltpu.make_async_copy(obj_ref, out_ref, sem)
    copy.start()
    copy.wait()


def fetch(obj):
    size = 4 * math.prod(obj.shape)
    return pl.pallas_call(
        fetch_kernel,
        out_shape=jax.ShapeDtypeStruct(obj.shape, obj.dtype),
        in_specs=[pl.BlockSpec(memory_space=pltpu.HBM)],
        out_specs=pl.BlockSpec(memory_space=pltpu.VMEM),
        scratch_shapes=[pltpu.SemaphoreType.DMA],
        compiler_params=pltpu.CompilerParams(vmem_limit_bytes=16 * 1024 * 1024),
        cost_estimate=pl.CostEstimate(flops=0, bytes_accessed=2 * size, transcendentals=0),
        name="fetch_slice",
    )(obj)


def window_kernel(members, obj_ref, *rest):
    table, table_sems = rest[-2:]
    clusters, count = table.shape[:2]
    pos_refs, out_refs, code_ref = rest[:clusters], rest[clusters:-3], rest[-3]
    window = out_refs[0].shape[-1]
    rows, cols = obj_ref.shape[-2:]
    tall, wide = window + 8, window + 128
    cluster = lax.div(lax.axis_index("dp"), members)
    home = lax.div(lax.axis_index("depth"), 2)

    fetches = [
        pltpu.make_async_copy(pos_refs[m], table.at[m], table_sems.at[m])
        for m in range(1, clusters)
    ]
    for fetch in fetches:
        fetch.start()
    for p in range(count):
        for axis in range(2):
            table[0, p, axis] = pos_refs[0][p, axis]
    for fetch in fetches:
        fetch.wait()

    def corner(m, p):
        at = home ^ cluster ^ m
        row, col = table[at, p, 0], table[at, p, 1]
        row_base = pl.multiple_of(jnp.minimum(row >> 3, (rows - tall) // 8) * 8, 8)
        col_base = pl.multiple_of(jnp.minimum(col >> 7, (cols - wide) // 128) * 128, 128)
        return row_base, col_base, row - row_base, col - col_base

    line = lax.broadcasted_iota(jnp.int32, (code_rows, window), 0)
    for p in range(count):
        row, col = table[home ^ cluster, p, 0], table[home ^ cluster, p, 1]
        code = jnp.where(line == 0, row >> 3, jnp.where(line == 1, row & 7, 0))
        code = jnp.where(line == 2, col >> 3, jnp.where(line == 3, col & 7, code))
        code_ref[p] = code.astype(f32).astype(bf16)
    for m in reversed(range(clusters)):
        for p in range(count):
            row_base, col_base, row_off, col_off = corner(m, p)
            lift = jnp.where(row_off == 0, 0, tall - row_off)
            shift = jnp.where(col_off == 0, 0, wide - col_off)
            for part in range(2):
                block = obj_ref[part, pl.ds(row_base, tall), pl.ds(col_base, wide)]
                block = pltpu.roll(block, shift, 1)[:, :window]
                block = pltpu.roll(block, lift, 0)[:window]
                out_refs[m][p, part] = block.astype(bf16)


def take_windows(obj, positions, window, members):
    clusters, count = len(positions), positions[0].shape[0]
    any_space = pl.BlockSpec(memory_space=pl.ANY)
    smem = pl.BlockSpec(memory_space=pltpu.SMEM)
    vmem = pl.BlockSpec(memory_space=pltpu.VMEM)
    out = pl.pallas_call(
        functools.partial(window_kernel, members),
        out_shape=[jax.ShapeDtypeStruct((count, 2, window, window), bf16)] * clusters
        + [jax.ShapeDtypeStruct((count, code_rows, window), bf16)],
        in_specs=[vmem, smem] + [any_space] * (clusters - 1),
        out_specs=[vmem] * (clusters + 1),
        scratch_shapes=[
            pltpu.SMEM((clusters, count, 2), jnp.int32),
            pltpu.SemaphoreType.DMA((clusters,)),
        ],
        compiler_params=pltpu.CompilerParams(vmem_limit_bytes=16 * 1024 * 1024),
        name="take_windows",
    )(obj, *positions)
    return out[:clusters], out[clusters]


def split(x):
    high = x.astype(bf16)
    return high, (x - high.astype(f32)).astype(bf16)


def cmul(a, b):
    return a[0] * b[0] - a[1] * b[1], a[0] * b[1] + a[1] * b[0]


def cmul_conj(a, b):
    return a[0] * b[0] + a[1] * b[1], a[0] * b[1] - a[1] * b[0]


def wave_kernel(members, clusters, probe_ref, kern_ref, left_ref, right_ref, code_ref, *rest):
    trans, terms, meas = rest[-3:]
    slices, count, _, _, window = trans.shape
    meas_refs, t_refs, out_refs = rest[:clusters], rest[clusters : clusters + slices], rest[clusters + slices : -3]
    own, cluster = lax.axis_index("depth"), lax.div(lax.axis_index("dp"), members)
    everyone = range(count)

    for m in range(slices):
        trans[own ^ m] = t_refs[m][...]
    for m, meas_ref in enumerate(meas_refs):

        @pl.when(lax.div(own, 2) ^ cluster == m)
        def _():
            meas[...] = meas_ref[...]

    def t_of(k, p):
        return trans[k, p, 0].astype(f32), trans[k, p, 1].astype(f32)

    def passes(x, axis, exact):
        if not exact:
            return x.astype(bf16)
        high, low = split(x)
        return jnp.concatenate([high, low, high], axis=axis)

    def rows(fields, sign, exact):
        x = jnp.concatenate([jnp.concatenate(f, axis=0) for f in fields], axis=1)
        x = passes(x, 0, exact)
        y = jnp.dot(left_ref[sign, :, : x.shape[0]], x, preferred_element_type=f32)
        cut = [y[:, p * window : (p + 1) * window] for p in everyone]
        return [(c[:window], c[window:]) for c in cut]

    def cols(fields, sign, exact):
        x = jnp.concatenate([jnp.concatenate(f, axis=1) for f in fields], axis=0)
        x = passes(x, 1, exact)
        y = jnp.dot(x, right_ref[sign, : x.shape[1]], preferred_element_type=f32)
        cut = [y[p * window : (p + 1) * window] for p in everyone]
        return [(c[:, :window], c[:, window:]) for c in cut]

    plus, minus = 0, 1

    def transform(fields, sign, exact):
        return cols(rows(fields, sign, exact), sign, exact)

    kern = (kern_ref[0], kern_ref[1])
    psi = [(probe_ref[0], probe_ref[1])] * count
    kept = []
    for k in range(slices):
        kept.append(psi)
        spectrum = transform([cmul(t_of(k, p), psi[p]) for p in everyone], minus, True)
        if k < slices - 1:
            psi = transform([cmul(kern, s) for s in spectrum], plus, True)

    def source(p):
        re, im = spectrum[p]
        scale = 2.0 * (re * re + im * im - meas[p])
        return scale * re, scale * im

    returned = transform([source(p) for p in everyone], plus, False)
    for k in reversed(range(slices)):
        for p in everyone:
            re, im = cmul_conj(kept[k][p], returned[p])
            terms[own ^ k, p, :window] = (re * grad_scale).astype(bf16)
            terms[own ^ k, p, window:] = (im * grad_scale).astype(bf16)
        if k > 0:
            chi = [cmul_conj(t_of(k, p), returned[p]) for p in everyone]
            spectrum = transform(chi, minus, False)
            returned = transform([cmul_conj(kern, s) for s in spectrum], plus, False)
    for n, out_ref in enumerate(out_refs):
        out_ref[:, : 2 * window] = terms[2 * n]
        out_ref[:, 2 * window :] = code_ref[...]


def run_waves(probe, kern, code, measured, windows, members):
    slices, count, window = len(windows), code.shape[0], code.shape[-1]
    left, right = dft_matrices(window)
    vmem = pl.BlockSpec(memory_space=pltpu.VMEM)
    block = jax.ShapeDtypeStruct((count, 2 * window + code_rows, window), bf16)
    return pl.pallas_call(
        functools.partial(wave_kernel, members, len(measured)),
        out_shape=[block] * (slices // 2),
        in_specs=[vmem] * (5 + len(measured) + slices),
        out_specs=[vmem] * (slices // 2),
        scratch_shapes=[
            pltpu.VMEM((slices, count, 2, window, window), bf16),
            pltpu.VMEM((slices, count, 2 * window, window), bf16),
            pltpu.VMEM((count, window, window), f32),
        ],
        compiler_params=pltpu.CompilerParams(vmem_limit_bytes=40 * 1024 * 1024),
        name="run_waves",
    )(probe, kern, jnp.asarray(left), jnp.asarray(right), code, *measured, *windows)


def place_kernel(*refs):
    block_refs, (out_ref, canvas) = refs[:-2], refs[-2:]
    _, stripe, cols = out_ref.shape
    count, _, window = block_refs[0].shape
    wide = window + 128
    first_row = lax.axis_index("dp") * stripe
    canvas[:, window : window + stripe, :] = jnp.zeros((2, stripe, canvas.shape[2]), f32)
    corners = []
    for block_ref in block_refs:
        for p in range(count):
            code = block_ref[p, 2 * window :].astype(f32)
            row = (8.0 * code[0:1] + code[1:2]).astype(jnp.int32)
            col = (8.0 * code[2:3] + code[3:4]).astype(jnp.int32)
            corners.append((row[0, 0], col[0, 0]))
    for n, (row, col) in enumerate(corners):
        block_ref, p = block_refs[n // count], n % count
        row = row - first_row + window
        row_base = pl.multiple_of((row >> 3) << 3, 8)
        col_base = pl.multiple_of((col >> 7) << 7, 128)

        @pl.when((row > 0) & (row < window + stripe))
        def _():
            for part in range(2):
                block = block_ref[p, part * window : (part + 1) * window].astype(f32)
                block = jnp.concatenate([block, jnp.zeros((8, window), f32)], axis=0)
                block = pltpu.roll(block, row - row_base, 0)
                block = jnp.concatenate([block, jnp.zeros((window + 8, 128), f32)], axis=1)
                block = pltpu.roll(block, col - col_base, 1)
                put = (part, pl.ds(row_base, window + 8), pl.ds(col_base, wide))
                canvas[put] = canvas[put] + block

    out_ref[...] = canvas[:, window : window + stripe, :cols]


def place_windows(blocks, stripe, cols):
    window = blocks[0].shape[-1]
    vmem = pl.BlockSpec(memory_space=pltpu.VMEM)
    tall = window + (stripe + 7) // 8 * 8 + window + 8
    return pl.pallas_call(
        place_kernel,
        out_shape=jax.ShapeDtypeStruct((2, stripe, cols), f32),
        in_specs=[vmem] * len(blocks),
        out_specs=vmem,
        scratch_shapes=[pltpu.VMEM((2, tall, cols + 128), f32)],
        compiler_params=pltpu.CompilerParams(vmem_limit_bytes=48 * 1024 * 1024),
        name="place_windows",
    )(*blocks)


def swap(block, depth_distance, dp_distance):
    depth, dp = lax.axis_size("depth"), lax.axis_size("dp")
    route = [
        (d * dp + j, (d ^ depth_distance) * dp + (j ^ dp_distance))
        for d in range(depth)
        for j in range(dp)
    ]
    return lax.ppermute(block, ("depth", "dp"), route)


def on_device(object_slices, positions, probe_field, propagator_phase, measured):
    depth, dp = lax.axis_size("depth"), lax.axis_size("dp")
    clusters = depth // 2
    members = dp // clusters
    rows, cols = object_slices.shape[-2:]
    window = probe_field.shape[-1]

    homes = [m * members for m in range(1, clusters)]
    all_positions = [positions] + [swap(positions, 0, home) for home in homes]
    windows, code = take_windows(fetch(object_slices[0]), all_positions, window, members)
    phase, code = lax.optimization_barrier((propagator_phase, code))
    windows = [windows[0]] + [swap(windows[m // 2], m, 0) for m in range(1, depth)]
    targets = [measured] + [swap(measured, 0, home) for home in homes]
    kern = jnp.stack([jnp.cos(phase), jnp.sin(phase)])
    terms = run_waves(probe_field, kern, code, targets, windows, members)

    blocks = [
        swap(terms[m // 2], m, plane) if m or plane else terms[0]
        for plane in range(0, members, 2)
        for m in range(0, depth, 2)
    ]
    blocks += [swap(block, 0, 1) for block in blocks]
    return place_windows(blocks, rows // dp, cols)[None]


def solution(mesh):
    placed = (P("depth", None, None, None), P("dp", None), P(), P(), P("dp", None, None))
    return jax.shard_map(
        on_device,
        mesh=mesh,
        in_specs=placed,
        out_specs=P("depth", None, "dp", None),
        check_vma=False,
    )
```

```python
import functools
import math

import jax
import jax.numpy as jnp
import numpy as np
from jax import lax
from jax.experimental import pallas as pl
from jax.experimental.pallas import tpu as pltpu
from jax.sharding import PartitionSpec as P

grad_scale = 0.03125
f32 = jnp.float32
bf16 = jnp.bfloat16


def dft_matrices(size):
    k = np.arange(size)
    angles = 2.0 * np.pi * ((k[:, None] * k[None, :]) % size) / size
    c = np.cos(angles) / math.sqrt(size)
    s = np.sin(angles) / math.sqrt(size)
    plus = np.block([[c, s], [-s, c]]).astype(np.float32)
    minus = np.block([[c, -s], [s, c]]).astype(np.float32)
    parts = []
    for full in (plus, minus):
        high = full.astype(bf16)
        low = (full - high.astype(np.float32)).astype(bf16)
        parts.append((high, low))
    (ph, plo), (mh, mlo) = parts
    right = np.stack([np.concatenate([ph, ph, plo], 0), np.concatenate([mh, mh, mlo], 0)])
    left = np.stack([np.concatenate([mh, mh, mlo], 1), np.concatenate([ph, ph, plo], 1)])
    return left, right


code_rows = 16


def fetch_kernel(obj_ref, meas_ref, out_ref, rounded_ref, sem):
    copy = pltpu.make_async_copy(obj_ref, out_ref, sem)
    copy.start()
    rounded_ref[...] = meas_ref[...].astype(bf16)
    copy.wait()


def fetch(obj, measured):
    vmem = pl.BlockSpec(memory_space=pltpu.VMEM)
    size = 4 * math.prod(obj.shape)
    return pl.pallas_call(
        fetch_kernel,
        out_shape=[
            jax.ShapeDtypeStruct(obj.shape, obj.dtype),
            jax.ShapeDtypeStruct(measured.shape, bf16),
        ],
        in_specs=[pl.BlockSpec(memory_space=pltpu.HBM), vmem],
        out_specs=[vmem, vmem],
        scratch_shapes=[pltpu.SemaphoreType.DMA],
        compiler_params=pltpu.CompilerParams(vmem_limit_bytes=16 * 1024 * 1024),
        cost_estimate=pl.CostEstimate(flops=0, bytes_accessed=2 * size, transcendentals=0),
        name="fetch_slice",
    )(obj, measured)


def window_kernel(members, obj_ref, *rest):
    table, table_sems = rest[-2:]
    clusters, count = table.shape[:2]
    pos_refs, out_refs, code_ref = rest[:clusters], rest[clusters:-3], rest[-3]
    window = out_refs[0].shape[-1]
    rows, cols = obj_ref.shape[-2:]
    tall, wide = window + 8, window + 128
    cluster = lax.div(lax.axis_index("dp"), members)
    home = lax.div(lax.axis_index("depth"), 2)

    fetches = [
        pltpu.make_async_copy(pos_refs[m], table.at[m], table_sems.at[m])
        for m in range(1, clusters)
    ]
    for fetch in fetches:
        fetch.start()
    for p in range(count):
        for axis in range(2):
            table[0, p, axis] = pos_refs[0][p, axis]
    for fetch in fetches:
        fetch.wait()

    def corner(m, p):
        at = home ^ cluster ^ m
        row, col = table[at, p, 0], table[at, p, 1]
        row_base = pl.multiple_of(jnp.minimum(row >> 3, (rows - tall) // 8) * 8, 8)
        col_base = pl.multiple_of(jnp.minimum(col >> 7, (cols - wide) // 128) * 128, 128)
        return row_base, col_base, row - row_base, col - col_base

    line = lax.broadcasted_iota(jnp.int32, (code_rows, window), 0)
    for p in range(count):
        row, col = table[home ^ cluster, p, 0], table[home ^ cluster, p, 1]
        code = jnp.where(line == 0, row >> 3, jnp.where(line == 1, row & 7, 0))
        code = jnp.where(line == 2, col >> 3, jnp.where(line == 3, col & 7, code))
        code_ref[p] = code.astype(f32).astype(bf16)
    for m in reversed(range(clusters)):
        for p in range(count):
            row_base, col_base, row_off, col_off = corner(m, p)
            lift = jnp.where(row_off == 0, 0, tall - row_off)
            shift = jnp.where(col_off == 0, 0, wide - col_off)
            for part in range(2):
                block = obj_ref[part, pl.ds(row_base, tall), pl.ds(col_base, wide)]
                block = pltpu.roll(block, shift, 1)[:, :window]
                block = pltpu.roll(block, lift, 0)[:window]
                out_refs[m][p, part] = block.astype(bf16)


def take_windows(obj, positions, window, members):
    clusters, count = len(positions), positions[0].shape[0]
    any_space = pl.BlockSpec(memory_space=pl.ANY)
    smem = pl.BlockSpec(memory_space=pltpu.SMEM)
    vmem = pl.BlockSpec(memory_space=pltpu.VMEM)
    out = pl.pallas_call(
        functools.partial(window_kernel, members),
        out_shape=[jax.ShapeDtypeStruct((count, 2, window, window), bf16)] * clusters
        + [jax.ShapeDtypeStruct((count, code_rows, window), bf16)],
        in_specs=[vmem, smem] + [any_space] * (clusters - 1),
        out_specs=[vmem] * (clusters + 1),
        scratch_shapes=[
            pltpu.SMEM((clusters, count, 2), jnp.int32),
            pltpu.SemaphoreType.DMA((clusters,)),
        ],
        compiler_params=pltpu.CompilerParams(vmem_limit_bytes=16 * 1024 * 1024),
        name="take_windows",
    )(obj, *positions)
    return out[:clusters], out[clusters]


def split(x):
    high = x.astype(bf16)
    return high, (x - high.astype(f32)).astype(bf16)


def cmul(a, b):
    return a[0] * b[0] - a[1] * b[1], a[0] * b[1] + a[1] * b[0]


def cmul_conj(a, b):
    return a[0] * b[0] + a[1] * b[1], a[0] * b[1] - a[1] * b[0]


def wave_kernel(members, clusters, probe_ref, kern_ref, left_ref, right_ref, code_ref, *rest):
    trans, terms, meas = rest[-3:]
    slices, count, _, _, window = trans.shape
    meas_refs, t_refs, out_refs = rest[:clusters], rest[clusters : clusters + slices], rest[clusters + slices : -3]
    own, cluster = lax.axis_index("depth"), lax.div(lax.axis_index("dp"), members)
    everyone = range(count)

    for m in range(slices):
        trans[own ^ m] = t_refs[m][...]
    for m, meas_ref in enumerate(meas_refs):

        @pl.when(lax.div(own, 2) ^ cluster == m)
        def _():
            meas[...] = meas_ref[...].astype(f32)

    def t_of(k, p):
        return trans[k, p, 0].astype(f32), trans[k, p, 1].astype(f32)

    def passes(x, axis, exact):
        if not exact:
            return x.astype(bf16)
        high, low = split(x)
        return jnp.concatenate([high, low, high], axis=axis)

    def rows(fields, sign, exact):
        x = jnp.concatenate([jnp.concatenate(f, axis=0) for f in fields], axis=1)
        x = passes(x, 0, exact)
        y = jnp.dot(left_ref[sign, :, : x.shape[0]], x, preferred_element_type=f32)
        cut = [y[:, p * window : (p + 1) * window] for p in everyone]
        return [(c[:window], c[window:]) for c in cut]

    def cols(fields, sign, exact):
        x = jnp.concatenate([jnp.concatenate(f, axis=1) for f in fields], axis=0)
        x = passes(x, 1, exact)
        y = jnp.dot(x, right_ref[sign, : x.shape[1]], preferred_element_type=f32)
        cut = [y[p * window : (p + 1) * window] for p in everyone]
        return [(c[:, :window], c[:, window:]) for c in cut]

    plus, minus = 0, 1

    def transform(fields, sign, exact):
        return cols(rows(fields, sign, exact), sign, exact)

    kern = (kern_ref[0], kern_ref[1])
    psi = [(probe_ref[0], probe_ref[1])] * count
    kept = []
    for k in range(slices):
        kept.append(psi)
        spectrum = transform([cmul(t_of(k, p), psi[p]) for p in everyone], minus, True)
        if k < slices - 1:
            psi = transform([cmul(kern, s) for s in spectrum], plus, True)

    def source(p):
        re, im = spectrum[p]
        scale = 2.0 * (re * re + im * im - meas[p])
        return scale * re, scale * im

    returned = transform([source(p) for p in everyone], plus, False)
    for k in reversed(range(slices)):
        for p in everyone:
            re, im = cmul_conj(kept[k][p], returned[p])
            terms[own ^ k, p, :window] = (re * grad_scale).astype(bf16)
            terms[own ^ k, p, window:] = (im * grad_scale).astype(bf16)
        if k > 0:
            chi = [cmul_conj(t_of(k, p), returned[p]) for p in everyone]
            spectrum = transform(chi, minus, False)
            returned = transform([cmul_conj(kern, s) for s in spectrum], plus, False)
    for n, out_ref in enumerate(out_refs):
        out_ref[:, : 2 * window] = terms[2 * n]
        out_ref[:, 2 * window :] = code_ref[...]


def run_waves(probe, kern, code, measured, windows, members):
    slices, count, window = len(windows), code.shape[0], code.shape[-1]
    left, right = dft_matrices(window)
    vmem = pl.BlockSpec(memory_space=pltpu.VMEM)
    block = jax.ShapeDtypeStruct((count, 2 * window + code_rows, window), bf16)
    return pl.pallas_call(
        functools.partial(wave_kernel, members, len(measured)),
        out_shape=[block] * (slices // 2),
        in_specs=[vmem] * (5 + len(measured) + slices),
        out_specs=[vmem] * (slices // 2),
        scratch_shapes=[
            pltpu.VMEM((slices, count, 2, window, window), bf16),
            pltpu.VMEM((slices, count, 2 * window, window), bf16),
            pltpu.VMEM((count, window, window), f32),
        ],
        compiler_params=pltpu.CompilerParams(vmem_limit_bytes=40 * 1024 * 1024),
        name="run_waves",
    )(probe, kern, jnp.asarray(left), jnp.asarray(right), code, *measured, *windows)


def place_kernel(*refs):
    block_refs, (out_ref, canvas) = refs[:-2], refs[-2:]
    _, stripe, cols = out_ref.shape
    count, _, window = block_refs[0].shape
    wide = window + 128
    first_row = lax.axis_index("dp") * stripe
    canvas[:, window : window + stripe, :] = jnp.zeros((2, stripe, canvas.shape[2]), f32)
    corners = []
    for block_ref in block_refs:
        for p in range(count):
            code = block_ref[p, 2 * window :].astype(f32)
            row = (8.0 * code[0:1] + code[1:2]).astype(jnp.int32)
            col = (8.0 * code[2:3] + code[3:4]).astype(jnp.int32)
            corners.append((row[0, 0], col[0, 0]))
    for n, (row, col) in enumerate(corners):
        block_ref, p = block_refs[n // count], n % count
        row = row - first_row + window
        row_base = pl.multiple_of((row >> 3) << 3, 8)
        col_base = pl.multiple_of((col >> 7) << 7, 128)

        @pl.when((row > 0) & (row < window + stripe))
        def _():
            for part in range(2):
                block = block_ref[p, part * window : (part + 1) * window].astype(f32)
                block = jnp.concatenate([block, jnp.zeros((8, window), f32)], axis=0)
                block = pltpu.roll(block, row - row_base, 0)
                block = jnp.concatenate([block, jnp.zeros((window + 8, 128), f32)], axis=1)
                block = pltpu.roll(block, col - col_base, 1)
                put = (part, pl.ds(row_base, window + 8), pl.ds(col_base, wide))
                canvas[put] = canvas[put] + block

    out_ref[...] = canvas[:, window : window + stripe, :cols]


def place_windows(blocks, stripe, cols):
    window = blocks[0].shape[-1]
    vmem = pl.BlockSpec(memory_space=pltpu.VMEM)
    tall = window + (stripe + 7) // 8 * 8 + window + 8
    return pl.pallas_call(
        place_kernel,
        out_shape=jax.ShapeDtypeStruct((2, stripe, cols), f32),
        in_specs=[vmem] * len(blocks),
        out_specs=vmem,
        scratch_shapes=[pltpu.VMEM((2, tall, cols + 128), f32)],
        compiler_params=pltpu.CompilerParams(vmem_limit_bytes=48 * 1024 * 1024),
        name="place_windows",
    )(*blocks)


def swap(block, depth_distance, dp_distance):
    depth, dp = lax.axis_size("depth"), lax.axis_size("dp")
    route = [
        (d * dp + j, (d ^ depth_distance) * dp + (j ^ dp_distance))
        for d in range(depth)
        for j in range(dp)
    ]
    return lax.ppermute(block, ("depth", "dp"), route)


def on_device(object_slices, positions, probe_field, propagator_phase, measured):
    depth, dp = lax.axis_size("depth"), lax.axis_size("dp")
    clusters = depth // 2
    members = dp // clusters
    rows, cols = object_slices.shape[-2:]
    window = probe_field.shape[-1]

    homes = [m * members for m in range(1, clusters)]
    all_positions = [positions] + [swap(positions, 0, home) for home in homes]
    obj, measured = fetch(object_slices[0], measured)
    windows, code = take_windows(obj, all_positions, window, members)
    phase, code = lax.optimization_barrier((propagator_phase, code))
    windows = [windows[0]] + [swap(windows[m // 2], m, 0) for m in range(1, depth)]
    kern = jnp.stack([jnp.cos(phase), jnp.sin(phase)])
    kern, measured = lax.optimization_barrier((kern, measured))
    targets = [measured] + [swap(measured, 0, home) for home in homes]
    terms = run_waves(probe_field, kern, code, targets, windows, members)

    blocks = [
        swap(terms[m // 2], m, plane) if m or plane else terms[0]
        for plane in range(0, members, 2)
        for m in range(0, depth, 2)
    ]
    blocks += [swap(block, 0, 1) for block in blocks]
    return place_windows(blocks, rows // dp, cols)[None]


def solution(mesh):
    placed = (P("depth", None, None, None), P("dp", None), P(), P(), P("dp", None, None))
    return jax.shard_map(
        on_device,
        mesh=mesh,
        in_specs=placed,
        out_specs=P("depth", None, "dp", None),
        check_vma=False,
    )
```

```python
import functools
import math

import jax
import jax.numpy as jnp
import numpy as np
from jax import lax
from jax.experimental import pallas as pl
from jax.experimental.pallas import tpu as pltpu
from jax.sharding import PartitionSpec as P

grad_scale = 0.03125
f32 = jnp.float32
bf16 = jnp.bfloat16


def dft_matrices(size):
    k = np.arange(size)
    angles = 2.0 * np.pi * ((k[:, None] * k[None, :]) % size) / size
    c = np.cos(angles) / math.sqrt(size)
    s = np.sin(angles) / math.sqrt(size)
    plus = np.block([[c, s], [-s, c]]).astype(np.float32)
    minus = np.block([[c, -s], [s, c]]).astype(np.float32)
    parts = []
    for full in (plus, minus):
        high = full.astype(bf16)
        low = (full - high.astype(np.float32)).astype(bf16)
        parts.append((high, low))
    (ph, plo), (mh, mlo) = parts
    right = np.stack([np.concatenate([ph, ph, plo], 0), np.concatenate([mh, mh, mlo], 0)])
    left = np.stack([mh, ph])
    thin = np.concatenate([minus[:, :size] for minus in (mh, mh, mlo)], 1)
    return jnp.asarray(thin), jnp.asarray(left), jnp.asarray(right)


code_rows = 16


def fetch_kernel(obj_ref, out_ref, sem):
    copy = pltpu.make_async_copy(obj_ref, out_ref, sem)
    copy.start()
    copy.wait()


def fetch(obj):
    size = 4 * math.prod(obj.shape)
    return pl.pallas_call(
        fetch_kernel,
        out_shape=jax.ShapeDtypeStruct(obj.shape, obj.dtype),
        in_specs=[pl.BlockSpec(memory_space=pltpu.HBM)],
        out_specs=pl.BlockSpec(memory_space=pltpu.VMEM),
        scratch_shapes=[pltpu.SemaphoreType.DMA],
        compiler_params=pltpu.CompilerParams(vmem_limit_bytes=16 * 1024 * 1024),
        cost_estimate=pl.CostEstimate(flops=0, bytes_accessed=2 * size, transcendentals=0),
        name="fetch_slice",
    )(obj)


def window_kernel(members, obj_ref, *rest):
    table, table_sems = rest[-2:]
    clusters, count = table.shape[:2]
    pos_refs, out_refs, code_ref = rest[:clusters], rest[clusters:-3], rest[-3]
    window = out_refs[0].shape[-1]
    rows, cols = obj_ref.shape[-2:]
    tall, wide = window + 8, window + 128
    cluster = lax.div(lax.axis_index("dp"), members)
    home = lax.div(lax.axis_index("depth"), 2)

    fetches = [
        pltpu.make_async_copy(pos_refs[m], table.at[m], table_sems.at[m])
        for m in range(1, clusters)
    ]
    for fetch in fetches:
        fetch.start()
    for p in range(count):
        for axis in range(2):
            table[0, p, axis] = pos_refs[0][p, axis]
    for fetch in fetches:
        fetch.wait()

    def corner(m, p):
        at = home ^ cluster ^ m
        row, col = table[at, p, 0], table[at, p, 1]
        row_base = pl.multiple_of(jnp.minimum(row >> 3, (rows - tall) // 8) * 8, 8)
        col_base = pl.multiple_of(jnp.minimum(col >> 7, (cols - wide) // 128) * 128, 128)
        return row_base, col_base, row - row_base, col - col_base

    line = lax.broadcasted_iota(jnp.int32, (code_rows, window), 0)
    for p in range(count):
        row, col = table[home ^ cluster, p, 0], table[home ^ cluster, p, 1]
        code = jnp.where(line == 0, row >> 3, jnp.where(line == 1, row & 7, 0))
        code = jnp.where(line == 2, col >> 3, jnp.where(line == 3, col & 7, code))
        code_ref[p] = code.astype(f32).astype(bf16)
    for m in reversed(range(clusters)):
        for p in range(count):
            row_base, col_base, row_off, col_off = corner(m, p)
            lift = jnp.where(row_off == 0, 0, tall - row_off)
            shift = jnp.where(col_off == 0, 0, wide - col_off)
            for part in range(2):
                block = obj_ref[part, pl.ds(row_base, tall), pl.ds(col_base, wide)]
                block = pltpu.roll(block, shift, 1)[:, :window]
                block = pltpu.roll(block, lift, 0)[:window]
                out_refs[m][p, part] = block.astype(bf16)


def take_windows(obj, positions, window, members):
    clusters, count = len(positions), positions[0].shape[0]
    any_space = pl.BlockSpec(memory_space=pl.ANY)
    smem = pl.BlockSpec(memory_space=pltpu.SMEM)
    vmem = pl.BlockSpec(memory_space=pltpu.VMEM)
    out = pl.pallas_call(
        functools.partial(window_kernel, members),
        out_shape=[jax.ShapeDtypeStruct((count, 2, window, window), bf16)] * clusters
        + [jax.ShapeDtypeStruct((count, code_rows, window), bf16)],
        in_specs=[vmem, smem] + [any_space] * (clusters - 1),
        out_specs=[vmem] * (clusters + 1),
        scratch_shapes=[
            pltpu.SMEM((clusters, count, 2), jnp.int32),
            pltpu.SemaphoreType.DMA((clusters,)),
        ],
        compiler_params=pltpu.CompilerParams(vmem_limit_bytes=16 * 1024 * 1024),
        name="take_windows",
    )(obj, *positions)
    return out[:clusters], out[clusters]


def split(x):
    high = x.astype(bf16)
    return high, (x - high.astype(f32)).astype(bf16)


def cmul(a, b):
    return a[0] * b[0] - a[1] * b[1], a[0] * b[1] + a[1] * b[0]


def cmul_conj(a, b):
    return a[0] * b[0] + a[1] * b[1], a[0] * b[1] - a[1] * b[0]


def transform(field, sign, tables, exact):
    thin_ref, left_ref, right_ref = tables
    re, im = field
    size = re.shape[0]
    if exact:
        high, low = split(jnp.concatenate([re, im], axis=1))
        x = jnp.concatenate([high, low, high], axis=0)
        y = jnp.dot(thin_ref[...], x, preferred_element_type=f32)
        cr, ci, sr, si = y[:size, :size], y[:size, size:], y[size:, :size], y[size:, size:]
        re, im = (cr - si, ci + sr) if sign == 0 else (cr + si, ci - sr)
        high, low = split(jnp.concatenate([re, im], axis=1))
        x = jnp.concatenate([high, low, high], axis=1)
        y = jnp.dot(x, right_ref[sign], preferred_element_type=f32)
    else:
        x = jnp.concatenate([re, im], axis=0).astype(bf16)
        y = jnp.dot(left_ref[sign], x, preferred_element_type=f32)
        x = jnp.concatenate([y[:size], y[size:]], axis=1).astype(bf16)
        y = jnp.dot(x, right_ref[sign, : 2 * size], preferred_element_type=f32)
    return y[:, :size], y[:, size:]


def forward_kernel(probe_ref, kern_ref, *rest):
    tables, t_refs, (trans, waves) = rest[:3], rest[3:-2], rest[-2:]
    slices, count = trans.shape[:2]
    own = lax.axis_index("depth")
    everyone = range(count)
    for m in range(slices):
        trans[own ^ m] = t_refs[m][...]
    kern = (kern_ref[0], kern_ref[1])
    psi = [(probe_ref[0], probe_ref[1])] * count
    for k in range(slices):
        field = [cmul((trans[k, p, 0].astype(f32), trans[k, p, 1].astype(f32)), psi[p]) for p in everyone]
        psi = [transform(f, 1, tables, True) for f in field]
        if k < slices - 1:
            psi = [transform(cmul(kern, s), 0, tables, True) for s in psi]
        for p in everyone:
            waves[k, p, 0] = psi[p][0]
            waves[k, p, 1] = psi[p][1]


def backward_kernel(members, clusters, probe_ref, kern_ref, code_ref, trans, waves, *rest):
    tables, meas_refs, out_refs, (terms, meas) = rest[:3], rest[3 : 3 + clusters], rest[3 + clusters : -2], rest[-2:]
    slices, count, _, window, _ = trans.shape
    own, cluster = lax.axis_index("depth"), lax.div(lax.axis_index("dp"), members)
    everyone = range(count)
    for m, meas_ref in enumerate(meas_refs):

        @pl.when(lax.div(own, 2) ^ cluster == m)
        def _():
            meas[...] = meas_ref[...]

    kern = (kern_ref[0], kern_ref[1])

    def source(p):
        re, im = waves[slices - 1, p, 0], waves[slices - 1, p, 1]
        scale = 2.0 * (re * re + im * im - meas[p])
        return scale * re, scale * im

    returned = [transform(source(p), 0, tables, False) for p in everyone]
    for k in reversed(range(slices)):
        for p in everyone:
            wave = (waves[k - 1, p, 0], waves[k - 1, p, 1]) if k else (probe_ref[0], probe_ref[1])
            re, im = cmul_conj(wave, returned[p])
            terms[own ^ k, p, :window] = (re * grad_scale).astype(bf16)
            terms[own ^ k, p, window:] = (im * grad_scale).astype(bf16)
        if k > 0:
            chi = [
                cmul_conj((trans[k, p, 0].astype(f32), trans[k, p, 1].astype(f32)), returned[p])
                for p in everyone
            ]
            chi = [transform(c, 1, tables, False) for c in chi]
            returned = [transform(cmul_conj(kern, c), 0, tables, False) for c in chi]
    for n, out_ref in enumerate(out_refs):
        out_ref[:, : 2 * window] = terms[2 * n]
        out_ref[:, 2 * window :] = code_ref[...]


limit = pltpu.CompilerParams(vmem_limit_bytes=32 * 1024 * 1024)
vmem = pl.BlockSpec(memory_space=pltpu.VMEM)


def run_forward(probe, kern, tables, windows):
    slices, shape = len(windows), windows[0].shape
    return pl.pallas_call(
        forward_kernel,
        out_shape=[
            jax.ShapeDtypeStruct((slices,) + shape, bf16),
            jax.ShapeDtypeStruct((slices,) + shape, f32),
        ],
        in_specs=[vmem] * (5 + slices),
        out_specs=[vmem, vmem],
        compiler_params=limit,
        name="run_forward",
    )(probe, kern, *tables, *windows)


def run_backward(probe, kern, code, trans, waves, tables, measured, members):
    slices, count, _, window, _ = trans.shape
    block = jax.ShapeDtypeStruct((count, 2 * window + code_rows, window), bf16)
    return pl.pallas_call(
        functools.partial(backward_kernel, members, len(measured)),
        out_shape=[block] * (slices // 2),
        in_specs=[vmem] * (8 + len(measured)),
        out_specs=[vmem] * (slices // 2),
        scratch_shapes=[
            pltpu.VMEM((slices, count, 2 * window, window), bf16),
            pltpu.VMEM((count, window, window), f32),
        ],
        compiler_params=limit,
        name="run_backward",
    )(probe, kern, code, trans, waves, *tables, *measured)


def place_kernel(*refs):
    block_refs, (out_ref, canvas) = refs[:-2], refs[-2:]
    _, stripe, cols = out_ref.shape
    count, _, window = block_refs[0].shape
    wide = window + 128
    first_row = lax.axis_index("dp") * stripe
    canvas[:, window : window + stripe, :] = jnp.zeros((2, stripe, canvas.shape[2]), f32)
    corners = []
    for block_ref in block_refs:
        for p in range(count):
            code = block_ref[p, 2 * window :].astype(f32)
            row = (8.0 * code[0:1] + code[1:2]).astype(jnp.int32)
            col = (8.0 * code[2:3] + code[3:4]).astype(jnp.int32)
            corners.append((row[0, 0], col[0, 0]))
    for n, (row, col) in enumerate(corners):
        block_ref, p = block_refs[n // count], n % count
        row = row - first_row + window
        row_base = pl.multiple_of((row >> 3) << 3, 8)
        col_base = pl.multiple_of((col >> 7) << 7, 128)

        @pl.when((row > 0) & (row < window + stripe))
        def _():
            for part in range(2):
                block = block_ref[p, part * window : (part + 1) * window].astype(f32)
                block = jnp.concatenate([block, jnp.zeros((8, window), f32)], axis=0)
                block = pltpu.roll(block, row - row_base, 0)
                block = jnp.concatenate([block, jnp.zeros((window + 8, 128), f32)], axis=1)
                block = pltpu.roll(block, col - col_base, 1)
                put = (part, pl.ds(row_base, window + 8), pl.ds(col_base, wide))
                canvas[put] = canvas[put] + block

    out_ref[...] = canvas[:, window : window + stripe, :cols]


def place_windows(blocks, stripe, cols):
    window = blocks[0].shape[-1]
    vmem = pl.BlockSpec(memory_space=pltpu.VMEM)
    tall = window + (stripe + 7) // 8 * 8 + window + 8
    return pl.pallas_call(
        place_kernel,
        out_shape=jax.ShapeDtypeStruct((2, stripe, cols), f32),
        in_specs=[vmem] * len(blocks),
        out_specs=vmem,
        scratch_shapes=[pltpu.VMEM((2, tall, cols + 128), f32)],
        compiler_params=pltpu.CompilerParams(vmem_limit_bytes=48 * 1024 * 1024),
        name="place_windows",
    )(*blocks)


def swap(block, depth_distance, dp_distance):
    depth, dp = lax.axis_size("depth"), lax.axis_size("dp")
    route = [
        (d * dp + j, (d ^ depth_distance) * dp + (j ^ dp_distance))
        for d in range(depth)
        for j in range(dp)
    ]
    return lax.ppermute(block, ("depth", "dp"), route)


def on_device(object_slices, positions, probe_field, propagator_phase, measured):
    depth, dp = lax.axis_size("depth"), lax.axis_size("dp")
    clusters = depth // 2
    members = dp // clusters
    rows, cols = object_slices.shape[-2:]
    window = probe_field.shape[-1]

    homes = [m * members for m in range(1, clusters)]
    all_positions = [positions] + [swap(positions, 0, home) for home in homes]
    windows, code = take_windows(fetch(object_slices[0]), all_positions, window, members)
    phase, code = lax.optimization_barrier((propagator_phase, code))
    windows = [windows[0]] + [swap(windows[m // 2], m, 0) for m in range(1, depth)]
    kern = jnp.stack([jnp.cos(phase), jnp.sin(phase)])
    kern, late = lax.optimization_barrier((kern, measured))
    targets = [measured] + [swap(late, 0, home) for home in homes]
    tables = dft_matrices(window)
    trans, waves = run_forward(probe_field, kern, tables, windows)
    terms = run_backward(probe_field, kern, code, trans, waves, tables, targets, members)

    blocks = [
        swap(terms[m // 2], m, plane) if m or plane else terms[0]
        for plane in range(0, members, 2)
        for m in range(0, depth, 2)
    ]
    blocks += [swap(block, 0, 1) for block in blocks]
    return place_windows(blocks, rows // dp, cols)[None]


def solution(mesh):
    placed = (P("depth", None, None, None), P("dp", None), P(), P(), P("dp", None, None))
    return jax.shard_map(
        on_device,
        mesh=mesh,
        in_specs=placed,
        out_specs=P("depth", None, "dp", None),
        check_vma=False,
    )
```

```python
import functools
import math

import jax
import jax.numpy as jnp
import numpy as np
from jax import lax
from jax.experimental import pallas as pl
from jax.experimental.pallas import tpu as pltpu
from jax.sharding import PartitionSpec as P

grad_scale = 0.03125
f32 = jnp.float32
bf16 = jnp.bfloat16


def dft_matrices(size):
    k = np.arange(size)
    angles = 2.0 * np.pi * ((k[:, None] * k[None, :]) % size) / size
    c = np.cos(angles) / math.sqrt(size)
    s = np.sin(angles) / math.sqrt(size)
    plus = np.block([[c, s], [-s, c]]).astype(np.float32)
    minus = np.block([[c, -s], [s, c]]).astype(np.float32)
    parts = []
    for full in (plus, minus):
        high = full.astype(bf16)
        low = (full - high.astype(np.float32)).astype(bf16)
        parts.append((high, low))
    (ph, plo), (mh, mlo) = parts
    right = np.stack([np.concatenate([ph, ph, plo], 0), np.concatenate([mh, mh, mlo], 0)])
    left = np.stack([np.concatenate([mh, mh, mlo], 1), np.concatenate([ph, ph, plo], 1)])
    return jnp.asarray(left), jnp.asarray(right)


code_rows = 16

small = pltpu.CompilerParams(vmem_limit_bytes=16 * 1024 * 1024)
limit = pltpu.CompilerParams(vmem_limit_bytes=32 * 1024 * 1024)
vmem = pl.BlockSpec(memory_space=pltpu.VMEM)
smem = pl.BlockSpec(memory_space=pltpu.SMEM)


def cut(obj_ref, row, col, out_ref, window):
    rows, cols = obj_ref.shape[-2:]
    tall, wide = window + 8, window + 128
    row_base = pl.multiple_of(jnp.minimum(row >> 3, (rows - tall) // 8) * 8, 8)
    col_base = pl.multiple_of(jnp.minimum(col >> 7, (cols - wide) // 128) * 128, 128)
    lift = jnp.where(row == row_base, 0, tall - (row - row_base))
    shift = jnp.where(col == col_base, 0, wide - (col - col_base))
    for part in range(2):
        block = obj_ref[part, pl.ds(row_base, tall), pl.ds(col_base, wide)]
        block = pltpu.roll(block, shift, 1)[:, :window]
        block = pltpu.roll(block, lift, 0)[:window]
        out_ref[part] = block.astype(bf16)


def near_kernel(pos_ref, obj_ref, out_ref):
    for p in range(out_ref.shape[0]):
        cut(obj_ref, pos_ref[p, 0], pos_ref[p, 1], out_ref.at[p], out_ref.shape[-1])


def near_windows(obj, positions, window):
    return pl.pallas_call(
        near_kernel,
        out_shape=jax.ShapeDtypeStruct((positions.shape[0], 2, window, window), bf16),
        in_specs=[smem, vmem],
        out_specs=vmem,
        compiler_params=small,
        cost_estimate=pl.CostEstimate(flops=0, bytes_accessed=4 * math.prod(obj.shape), transcendentals=0),
        name="near_windows",
    )(positions, obj)


def far_kernel(members, obj_ref, near_ref, *rest):
    table, table_sems = rest[-2:]
    clusters, count = table.shape[:2]
    pos_refs, out_refs, code_ref = rest[:clusters], rest[clusters:-3], rest[-3]
    window = near_ref.shape[-1]
    cluster = lax.div(lax.axis_index("dp"), members)
    home = lax.div(lax.axis_index("depth"), 2)

    arrivals = [
        pltpu.make_async_copy(pos_refs[m], table.at[m], table_sems.at[m])
        for m in range(1, clusters)
    ]
    for arrival in arrivals:
        arrival.start()
    for p in range(count):
        for axis in range(2):
            table[0, p, axis] = pos_refs[0][p, axis]
    for m in range(clusters):

        @pl.when(home ^ cluster == m)
        def _():
            out_refs[m][...] = near_ref[...]

    for arrival in arrivals:
        arrival.wait()
    line = lax.broadcasted_iota(jnp.int32, (code_rows, window), 0)
    for p in range(count):
        row, col = table[home ^ cluster, p, 0], table[home ^ cluster, p, 1]
        code = jnp.where(line == 0, row >> 3, jnp.where(line == 1, row & 7, 0))
        code = jnp.where(line == 2, col >> 3, jnp.where(line == 3, col & 7, code))
        code_ref[p] = code.astype(f32).astype(bf16)
    for m in range(clusters):
        at = home ^ cluster ^ m

        @pl.when(at > 0)
        def _():
            for p in range(count):
                cut(obj_ref, table[at, p, 0], table[at, p, 1], out_refs[m].at[p], window)


def take_windows(obj, positions, window, members):
    clusters, count = len(positions), positions[0].shape[0]
    near = near_windows(obj, positions[0], window)
    out = pl.pallas_call(
        functools.partial(far_kernel, members),
        out_shape=[jax.ShapeDtypeStruct(near.shape, bf16)] * clusters
        + [jax.ShapeDtypeStruct((count, code_rows, window), bf16)],
        in_specs=[vmem, vmem, smem] + [pl.BlockSpec(memory_space=pl.ANY)] * (clusters - 1),
        out_specs=[vmem] * (clusters + 1),
        scratch_shapes=[
            pltpu.SMEM((clusters, count, 2), jnp.int32),
            pltpu.SemaphoreType.DMA((clusters,)),
        ],
        compiler_params=small,
        name="far_windows",
    )(obj, near, *positions)
    return out[:clusters], out[clusters]


def split(x):
    high = x.astype(bf16)
    return high, (x - high.astype(f32)).astype(bf16)


def cmul(a, b):
    return a[0] * b[0] - a[1] * b[1], a[0] * b[1] + a[1] * b[0]


def cmul_conj(a, b):
    return a[0] * b[0] + a[1] * b[1], a[0] * b[1] - a[1] * b[0]


def transform(fields, sign, tables, exact):
    left_ref, right_ref = tables
    size = fields[0][0].shape[0]

    def passes(x, axis):
        if not exact:
            return x.astype(bf16)
        high, low = split(x)
        return jnp.concatenate([high, low, high], axis=axis)

    x = passes(jnp.concatenate([jnp.concatenate(f, axis=0) for f in fields], axis=1), 0)
    y = jnp.dot(left_ref[sign, :, : x.shape[0]], x, preferred_element_type=f32)
    fields = [y[:, n * size : (n + 1) * size] for n in range(len(fields))]
    fields = [jnp.concatenate([f[:size], f[size:]], axis=1) for f in fields]
    x = passes(jnp.concatenate(fields, axis=0), 1)
    y = jnp.dot(x, right_ref[sign, : x.shape[1]], preferred_element_type=f32)
    fields = [y[n * size : (n + 1) * size] for n in range(len(fields))]
    return [(f[:, :size], f[:, size:]) for f in fields]


def forward_kernel(probe_ref, kern_ref, *rest):
    tables, t_refs, (trans, waves) = rest[:2], rest[2:-2], rest[-2:]
    slices, count = trans.shape[:2]
    own = lax.axis_index("depth")
    everyone = range(count)
    for m in range(slices):
        trans[own ^ m] = t_refs[m][...]
    kern = (kern_ref[0], kern_ref[1])
    psi = [(probe_ref[0], probe_ref[1])] * count
    for k in range(slices):
        field = [cmul((trans[k, p, 0].astype(f32), trans[k, p, 1].astype(f32)), psi[p]) for p in everyone]
        psi = transform(field, 1, tables, True)
        if k < slices - 1:
            psi = transform([cmul(kern, s) for s in psi], 0, tables, True)
        for p in everyone:
            waves[k, p, 0] = psi[p][0]
            waves[k, p, 1] = psi[p][1]


def backward_kernel(members, clusters, probe_ref, kern_ref, code_ref, trans, waves, *rest):
    tables, meas_refs = rest[:2], rest[2 : 2 + clusters]
    out_refs, (terms, meas) = rest[2 + clusters : -2], rest[-2:]
    slices, count, _, window, _ = trans.shape
    own, cluster = lax.axis_index("depth"), lax.div(lax.axis_index("dp"), members)
    everyone = range(count)
    for m, meas_ref in enumerate(meas_refs):

        @pl.when(lax.div(own, 2) ^ cluster == m)
        def _():
            meas[...] = meas_ref[...]

    kern = (kern_ref[0], kern_ref[1])

    def source(p):
        re, im = waves[slices - 1, p, 0], waves[slices - 1, p, 1]
        scale = 2.0 * (re * re + im * im - meas[p])
        return scale * re, scale * im

    returned = transform([source(p) for p in everyone], 0, tables, False)
    for k in reversed(range(slices)):
        for p in everyone:
            wave = (waves[k - 1, p, 0], waves[k - 1, p, 1]) if k else (probe_ref[0], probe_ref[1])
            re, im = cmul_conj(wave, returned[p])
            terms[own ^ k, p, :window] = (re * grad_scale).astype(bf16)
            terms[own ^ k, p, window:] = (im * grad_scale).astype(bf16)
        if k > 0:
            chi = [
                cmul_conj((trans[k, p, 0].astype(f32), trans[k, p, 1].astype(f32)), returned[p])
                for p in everyone
            ]
            chi = transform(chi, 1, tables, False)
            returned = transform([cmul_conj(kern, c) for c in chi], 0, tables, False)
    for n, out_ref in enumerate(out_refs):
        out_ref[:, : 2 * window] = terms[2 * n]
        out_ref[:, 2 * window :] = code_ref[...]


def run_forward(probe, kern, tables, windows):
    slices, shape = len(windows), windows[0].shape
    return pl.pallas_call(
        forward_kernel,
        out_shape=[
            jax.ShapeDtypeStruct((slices,) + shape, bf16),
            jax.ShapeDtypeStruct((slices,) + shape, f32),
        ],
        in_specs=[vmem] * (4 + slices),
        out_specs=[vmem, vmem],
        compiler_params=limit,
        name="run_forward",
    )(probe, kern, *tables, *windows)


def run_backward(probe, kern, code, trans, waves, tables, measured, members):
    slices, count, _, window, _ = trans.shape
    block = jax.ShapeDtypeStruct((count, 2 * window + code_rows, window), bf16)
    return pl.pallas_call(
        functools.partial(backward_kernel, members, len(measured)),
        out_shape=[block] * (slices // 2),
        in_specs=[vmem] * (7 + len(measured)),
        out_specs=[vmem] * (slices // 2),
        scratch_shapes=[
            pltpu.VMEM((slices, count, 2 * window, window), bf16),
            pltpu.VMEM((count, window, window), f32),
        ],
        compiler_params=limit,
        name="run_backward",
    )(probe, kern, code, trans, waves, *tables, *measured)


def place_kernel(*refs):
    block_refs, (out_ref, canvas) = refs[:-2], refs[-2:]
    _, stripe, cols = out_ref.shape
    count, _, window = block_refs[0].shape
    wide = window + 128
    first_row = lax.axis_index("dp") * stripe
    canvas[:, window : window + stripe, :] = jnp.zeros((2, stripe, canvas.shape[2]), f32)
    corners = []
    for block_ref in block_refs:
        for p in range(count):
            code = block_ref[p, 2 * window :].astype(f32)
            row = (8.0 * code[0:1] + code[1:2]).astype(jnp.int32)
            col = (8.0 * code[2:3] + code[3:4]).astype(jnp.int32)
            corners.append((row[0, 0], col[0, 0]))
    for n, (row, col) in enumerate(corners):
        block_ref, p = block_refs[n // count], n % count
        row = row - first_row + window
        row_base = pl.multiple_of((row >> 3) << 3, 8)
        col_base = pl.multiple_of((col >> 7) << 7, 128)

        @pl.when((row > 0) & (row < window + stripe))
        def _():
            for part in range(2):
                block = block_ref[p, part * window : (part + 1) * window].astype(f32)
                block = jnp.concatenate([block, jnp.zeros((8, window), f32)], axis=0)
                block = pltpu.roll(block, row - row_base, 0)
                block = jnp.concatenate([block, jnp.zeros((window + 8, 128), f32)], axis=1)
                block = pltpu.roll(block, col - col_base, 1)
                put = (part, pl.ds(row_base, window + 8), pl.ds(col_base, wide))
                canvas[put] = canvas[put] + block

    out_ref[...] = canvas[:, window : window + stripe, :cols]


def place_windows(blocks, stripe, cols):
    window = blocks[0].shape[-1]
    vmem = pl.BlockSpec(memory_space=pltpu.VMEM)
    tall = window + (stripe + 7) // 8 * 8 + window + 8
    return pl.pallas_call(
        place_kernel,
        out_shape=jax.ShapeDtypeStruct((2, stripe, cols), f32),
        in_specs=[vmem] * len(blocks),
        out_specs=vmem,
        scratch_shapes=[pltpu.VMEM((2, tall, cols + 128), f32)],
        compiler_params=pltpu.CompilerParams(vmem_limit_bytes=48 * 1024 * 1024),
        name="place_windows",
    )(*blocks)


def swap(block, depth_distance, dp_distance):
    depth, dp = lax.axis_size("depth"), lax.axis_size("dp")
    route = [
        (d * dp + j, (d ^ depth_distance) * dp + (j ^ dp_distance))
        for d in range(depth)
        for j in range(dp)
    ]
    return lax.ppermute(block, ("depth", "dp"), route)


def on_device(object_slices, positions, probe_field, propagator_phase, measured):
    depth, dp = lax.axis_size("depth"), lax.axis_size("dp")
    clusters = depth // 2
    members = dp // clusters
    rows, cols = object_slices.shape[-2:]
    window = probe_field.shape[-1]

    homes = [m * members for m in range(1, clusters)]
    all_positions = [positions] + [swap(positions, 0, home) for home in homes]
    windows, code = take_windows(object_slices[0], all_positions, window, members)
    phase, code = lax.optimization_barrier((propagator_phase, code))
    windows = [windows[0]] + [swap(windows[m // 2], m, 0) for m in range(1, depth)]
    kern = jnp.stack([jnp.cos(phase), jnp.sin(phase)])
    kern, late = lax.optimization_barrier((kern, measured))
    targets = [measured] + [swap(late, 0, home) for home in homes]
    tables = dft_matrices(window)
    trans, waves = run_forward(probe_field, kern, tables, windows)
    terms = run_backward(probe_field, kern, code, trans, waves, tables, targets, members)

    blocks = [
        swap(terms[m // 2], m, plane) if m or plane else terms[0]
        for plane in range(0, members, 2)
        for m in range(0, depth, 2)
    ]
    blocks += [swap(block, 0, 1) for block in blocks]
    return place_windows(blocks, rows // dp, cols)[None]


def solution(mesh):
    placed = (P("depth", None, None, None), P("dp", None), P(), P(), P("dp", None, None))
    return jax.shard_map(
        on_device,
        mesh=mesh,
        in_specs=placed,
        out_specs=P("depth", None, "dp", None),
        check_vma=False,
    )
```

```python
import functools
import math

import jax
import jax.numpy as jnp
import numpy as np
from jax import lax
from jax.experimental import pallas as pl
from jax.experimental.pallas import tpu as pltpu
from jax.sharding import PartitionSpec as P

grad_scale = 0.03125
f32 = jnp.float32
bf16 = jnp.bfloat16


def dft_matrices(size):
    k = np.arange(size)
    angles = 2.0 * np.pi * ((k[:, None] * k[None, :]) % size) / size
    c = np.cos(angles) / math.sqrt(size)
    s = np.sin(angles) / math.sqrt(size)
    plus = np.block([[c, s], [-s, c]]).astype(np.float32)
    minus = np.block([[c, -s], [s, c]]).astype(np.float32)
    parts = []
    for full in (plus, minus):
        high = full.astype(bf16)
        low = (full - high.astype(np.float32)).astype(bf16)
        parts.append((high, low))
    (ph, plo), (mh, mlo) = parts
    right = np.stack([np.concatenate([ph, ph, plo], 0), np.concatenate([mh, mh, mlo], 0)])
    left = np.stack([np.concatenate([mh, mh, mlo], 1), np.concatenate([ph, ph, plo], 1)])
    return left, right


code_rows = 16


def window_kernel(members, obj_ref, *rest):
    table, buf, cut, table_sems, sems = rest[-5:]
    clusters, count, _, tall, wide = buf.shape
    pos_refs, out_refs, code_ref = rest[:clusters], rest[clusters:-6], rest[-6]
    window = cut.shape[-1]
    rows, cols = obj_ref.shape[-2:]
    cluster = lax.div(lax.axis_index("dp"), members)
    home = lax.div(lax.axis_index("depth"), 2)

    def corner(a, p):
        row, col = table[a, p, 0], table[a, p, 1]
        row_base = pl.multiple_of(jnp.minimum(row >> 3, (rows - tall) // 8) * 8, 8)
        col_base = pl.multiple_of(jnp.minimum(col >> 7, (cols - wide) // 128) * 128, 128)
        return row_base, col_base, row - row_base, col - col_base

    def copy(a, p):
        row_base, col_base, _, _ = corner(a, p)
        return pltpu.make_async_copy(
            obj_ref.at[:, pl.ds(row_base, tall), pl.ds(col_base, wide)], buf.at[a, p], sems.at[a, p]
        )

    arrivals = [
        pltpu.make_async_copy(pos_refs[a], table.at[a], table_sems.at[a])
        for a in range(1, clusters)
    ]
    for arrival in arrivals:
        arrival.start()
    for p in range(count):
        for axis in range(2):
            table[0, p, axis] = pos_refs[0][p, axis]
        copy(0, p).start()
    for a in range(1, clusters):
        arrivals[a - 1].wait()
        for p in range(count):
            copy(a, p).start()
    line = lax.broadcasted_iota(jnp.int32, (code_rows, window), 0)
    for p in range(count):
        row, col = table[home ^ cluster, p, 0], table[home ^ cluster, p, 1]
        code = jnp.where(line == 0, row >> 3, jnp.where(line == 1, row & 7, 0))
        code = jnp.where(line == 2, col >> 3, jnp.where(line == 3, col & 7, code))
        code_ref[p] = code.astype(f32).astype(bf16)
    for a in range(clusters):
        for p in range(count):
            copy(a, p).wait()
            _, _, row_off, col_off = corner(a, p)
            lift = jnp.where(row_off == 0, 0, tall - row_off)
            shift = jnp.where(col_off == 0, 0, wide - col_off)
            for part in range(2):
                block = pltpu.roll(buf[a, p, part], shift, 1)[:, :window]
                block = pltpu.roll(block, lift, 0)[:window]
                cut[home ^ cluster ^ a, p, part] = block.astype(bf16)
    for m, out_ref in enumerate(out_refs):
        out_ref[...] = cut[m]


def take_windows(obj, positions, window, members):
    clusters, count = len(positions), positions[0].shape[0]
    any_space = pl.BlockSpec(memory_space=pl.ANY)
    smem = pl.BlockSpec(memory_space=pltpu.SMEM)
    vmem = pl.BlockSpec(memory_space=pltpu.VMEM)
    out = pl.pallas_call(
        functools.partial(window_kernel, members),
        out_shape=[jax.ShapeDtypeStruct((count, 2, window, window), bf16)] * clusters
        + [jax.ShapeDtypeStruct((count, code_rows, window), bf16)],
        in_specs=[any_space, smem] + [any_space] * (clusters - 1),
        out_specs=[vmem] * (clusters + 1),
        scratch_shapes=[
            pltpu.SMEM((clusters, count, 2), jnp.int32),
            pltpu.VMEM((clusters, count, 2, window + 8, window + 128), f32),
            pltpu.VMEM((clusters, count, 2, window, window), bf16),
            pltpu.SemaphoreType.DMA((clusters,)),
            pltpu.SemaphoreType.DMA((clusters, count)),
        ],
        name="take_windows",
    )(obj, *positions)
    return out[:clusters], out[clusters]


def split(x):
    high = x.astype(bf16)
    return high, (x - high.astype(f32)).astype(bf16)


def cmul(a, b):
    return a[0] * b[0] - a[1] * b[1], a[0] * b[1] + a[1] * b[0]


def cmul_conj(a, b):
    return a[0] * b[0] + a[1] * b[1], a[0] * b[1] - a[1] * b[0]


def wave_kernel(members, clusters, probe_ref, kern_ref, left_ref, right_ref, code_ref, *rest):
    trans, terms, meas = rest[-3:]
    slices, count, _, _, window = trans.shape
    meas_refs, t_refs, out_refs = rest[:clusters], rest[clusters : clusters + slices], rest[clusters + slices : -3]
    own, cluster = lax.axis_index("depth"), lax.div(lax.axis_index("dp"), members)
    everyone = range(count)

    for m in range(slices):
        trans[own ^ m] = t_refs[m][...]
    for m, meas_ref in enumerate(meas_refs):

        @pl.when(lax.div(own, 2) ^ cluster == m)
        def _():
            meas[...] = meas_ref[...]

    def t_of(k, p):
        return trans[k, p, 0].astype(f32), trans[k, p, 1].astype(f32)

    def passes(x, axis, exact):
        if not exact:
            return x.astype(bf16)
        high, low = split(x)
        return jnp.concatenate([high, low, high], axis=axis)

    def rows(fields, sign, exact):
        x = jnp.concatenate([jnp.concatenate(f, axis=0) for f in fields], axis=1)
        x = passes(x, 0, exact)
        y = jnp.dot(left_ref[sign, :, : x.shape[0]], x, preferred_element_type=f32)
        cut = [y[:, p * window : (p + 1) * window] for p in everyone]
        return [(c[:window], c[window:]) for c in cut]

    def cols(fields, sign, exact):
        x = jnp.concatenate([jnp.concatenate(f, axis=1) for f in fields], axis=0)
        x = passes(x, 1, exact)
        y = jnp.dot(x, right_ref[sign, : x.shape[1]], preferred_element_type=f32)
        cut = [y[p * window : (p + 1) * window] for p in everyone]
        return [(c[:, :window], c[:, window:]) for c in cut]

    plus, minus = 0, 1

    def transform(fields, sign, exact):
        return cols(rows(fields, sign, exact), sign, exact)

    kern = (kern_ref[0], kern_ref[1])
    psi = [(probe_ref[0], probe_ref[1])] * count
    kept = []
    for k in range(slices):
        kept.append(psi)
        spectrum = transform([cmul(t_of(k, p), psi[p]) for p in everyone], minus, True)
        if k < slices - 1:
            psi = transform([cmul(kern, s) for s in spectrum], plus, True)

    def source(p):
        re, im = spectrum[p]
        scale = 2.0 * (re * re + im * im - meas[p])
        return scale * re, scale * im

    returned = transform([source(p) for p in everyone], plus, False)
    for k in reversed(range(slices)):
        for p in everyone:
            re, im = cmul_conj(kept[k][p], returned[p])
            terms[own ^ k, p, :window] = (re * grad_scale).astype(bf16)
            terms[own ^ k, p, window:] = (im * grad_scale).astype(bf16)
        if k > 0:
            chi = [cmul_conj(t_of(k, p), returned[p]) for p in everyone]
            spectrum = transform(chi, minus, False)
            returned = transform([cmul_conj(kern, s) for s in spectrum], plus, False)
    for n, out_ref in enumerate(out_refs):
        out_ref[:, : 2 * window] = terms[2 * n]
        out_ref[:, 2 * window :] = code_ref[...]


def run_waves(probe, kern, code, measured, windows, members):
    slices, count, window = len(windows), code.shape[0], code.shape[-1]
    left, right = dft_matrices(window)
    vmem = pl.BlockSpec(memory_space=pltpu.VMEM)
    block = jax.ShapeDtypeStruct((count, 2 * window + code_rows, window), bf16)
    return pl.pallas_call(
        functools.partial(wave_kernel, members, len(measured)),
        out_shape=[block] * (slices // 2),
        in_specs=[vmem] * (5 + len(measured) + slices),
        out_specs=[vmem] * (slices // 2),
        scratch_shapes=[
            pltpu.VMEM((slices, count, 2, window, window), bf16),
            pltpu.VMEM((slices, count, 2 * window, window), bf16),
            pltpu.VMEM((count, window, window), f32),
        ],
        compiler_params=pltpu.CompilerParams(vmem_limit_bytes=40 * 1024 * 1024),
        name="run_waves",
    )(probe, kern, jnp.asarray(left), jnp.asarray(right), code, *measured, *windows)


def place_kernel(*refs):
    block_refs, (out_ref, canvas) = refs[:-2], refs[-2:]
    _, stripe, cols = out_ref.shape
    count, _, window = block_refs[0].shape
    wide = window + 128
    first_row = lax.axis_index("dp") * stripe
    canvas[:, window : window + stripe, :] = jnp.zeros((2, stripe, canvas.shape[2]), f32)
    corners = []
    for block_ref in block_refs:
        for p in range(count):
            code = block_ref[p, 2 * window :].astype(f32)
            row = (8.0 * code[0:1] + code[1:2]).astype(jnp.int32)
            col = (8.0 * code[2:3] + code[3:4]).astype(jnp.int32)
            corners.append((row[0, 0], col[0, 0]))
    for n, (row, col) in enumerate(corners):
        block_ref, p = block_refs[n // count], n % count
        row = row - first_row + window
        row_base = pl.multiple_of((row >> 3) << 3, 8)
        col_base = pl.multiple_of((col >> 7) << 7, 128)

        @pl.when((row > 0) & (row < window + stripe))
        def _():
            for part in range(2):
                block = block_ref[p, part * window : (part + 1) * window].astype(f32)
                block = jnp.concatenate([block, jnp.zeros((8, window), f32)], axis=0)
                block = pltpu.roll(block, row - row_base, 0)
                block = jnp.concatenate([block, jnp.zeros((window + 8, 128), f32)], axis=1)
                block = pltpu.roll(block, col - col_base, 1)
                put = (part, pl.ds(row_base, window + 8), pl.ds(col_base, wide))
                canvas[put] = canvas[put] + block

    out_ref[...] = canvas[:, window : window + stripe, :cols]


def place_windows(blocks, stripe, cols):
    window = blocks[0].shape[-1]
    vmem = pl.BlockSpec(memory_space=pltpu.VMEM)
    tall = window + (stripe + 7) // 8 * 8 + window + 8
    return pl.pallas_call(
        place_kernel,
        out_shape=jax.ShapeDtypeStruct((2, stripe, cols), f32),
        in_specs=[vmem] * len(blocks),
        out_specs=vmem,
        scratch_shapes=[pltpu.VMEM((2, tall, cols + 128), f32)],
        compiler_params=pltpu.CompilerParams(vmem_limit_bytes=48 * 1024 * 1024),
        name="place_windows",
    )(*blocks)


def swap(block, depth_distance, dp_distance):
    depth, dp = lax.axis_size("depth"), lax.axis_size("dp")
    route = [
        (d * dp + j, (d ^ depth_distance) * dp + (j ^ dp_distance))
        for d in range(depth)
        for j in range(dp)
    ]
    return lax.ppermute(block, ("depth", "dp"), route)


def on_device(object_slices, positions, probe_field, propagator_phase, measured):
    depth, dp = lax.axis_size("depth"), lax.axis_size("dp")
    clusters = depth // 2
    members = dp // clusters
    rows, cols = object_slices.shape[-2:]
    window = probe_field.shape[-1]

    homes = [m * members for m in range(1, clusters)]
    all_positions = [positions] + [swap(positions, 0, home) for home in homes]
    windows, code = take_windows(object_slices[0], all_positions, window, members)
    phase, code = lax.optimization_barrier((propagator_phase, code))
    windows = [windows[0]] + [swap(windows[m // 2], m, 0) for m in range(1, depth)]
    targets = [measured] + [swap(measured, 0, home) for home in homes]
    kern = jnp.stack([jnp.cos(phase), jnp.sin(phase)])
    terms = run_waves(probe_field, kern, code, targets, windows, members)

    blocks = [
        swap(terms[m // 2], m, plane) if m or plane else terms[0]
        for plane in range(0, members, 2)
        for m in range(0, depth, 2)
    ]
    blocks += [swap(block, 0, 1) for block in blocks]
    return place_windows(blocks, rows // dp, cols)[None]


def solution(mesh):
    placed = (P("depth", None, None, None), P("dp", None), P(), P(), P("dp", None, None))
    return jax.shard_map(
        on_device,
        mesh=mesh,
        in_specs=placed,
        out_specs=P("depth", None, "dp", None),
        check_vma=False,
    )
```

```python
import functools
import math

import jax
import jax.numpy as jnp
import numpy as np
from jax import lax
from jax.experimental import pallas as pl
from jax.experimental.pallas import tpu as pltpu
from jax.sharding import PartitionSpec as P

grad_scale = 0.03125
f32 = jnp.float32
bf16 = jnp.bfloat16


def dft_matrices(size):
    k = np.arange(size)
    angles = 2.0 * np.pi * ((k[:, None] * k[None, :]) % size) / size
    c = np.cos(angles) / math.sqrt(size)
    s = np.sin(angles) / math.sqrt(size)
    plus = np.block([[c, s], [-s, c]]).astype(np.float32)
    minus = np.block([[c, -s], [s, c]]).astype(np.float32)
    parts = []
    for full in (plus, minus):
        high = full.astype(bf16)
        low = (full - high.astype(np.float32)).astype(bf16)
        parts.append((high, low))
    (ph, plo), (mh, mlo) = parts
    right = np.stack([np.concatenate([ph, ph, plo], 0), np.concatenate([mh, mh, mlo], 0)])
    left = np.stack([np.concatenate([mh, mh, mlo], 1), np.concatenate([ph, ph, plo], 1)])
    return left, right


code_rows = 16


def fetch_kernel(obj_ref, out_ref, sem):
    copy = pltpu.make_async_copy(obj_ref, out_ref, sem)
    copy.start()
    copy.wait()


def fetch(obj):
    size = 4 * math.prod(obj.shape)
    return pl.pallas_call(
        fetch_kernel,
        out_shape=jax.ShapeDtypeStruct(obj.shape, obj.dtype),
        in_specs=[pl.BlockSpec(memory_space=pltpu.HBM)],
        out_specs=pl.BlockSpec(memory_space=pltpu.VMEM),
        scratch_shapes=[pltpu.SemaphoreType.DMA],
        compiler_params=pltpu.CompilerParams(vmem_limit_bytes=16 * 1024 * 1024),
        cost_estimate=pl.CostEstimate(flops=0, bytes_accessed=2 * size, transcendentals=0),
        name="fetch_slice",
    )(obj)


def window_kernel(members, obj_ref, *rest):
    table, table_sems = rest[-2:]
    clusters, count = table.shape[:2]
    pos_refs, out_refs, code_ref = rest[:clusters], rest[clusters:-3], rest[-3]
    window = out_refs[0].shape[-1]
    rows, cols = obj_ref.shape[-2:]
    tall, wide = window + 8, window + 128
    cluster = lax.div(lax.axis_index("dp"), members)
    home = lax.div(lax.axis_index("depth"), 2)

    fetches = [
        pltpu.make_async_copy(pos_refs[m], table.at[m], table_sems.at[m])
        for m in range(1, clusters)
    ]
    for fetch in fetches:
        fetch.start()
    for p in range(count):
        for axis in range(2):
            table[0, p, axis] = pos_refs[0][p, axis]
    for fetch in fetches:
        fetch.wait()

    def corner(m, p):
        at = home ^ cluster ^ m
        row, col = table[at, p, 0], table[at, p, 1]
        row_base = pl.multiple_of(jnp.minimum(row >> 3, (rows - tall) // 8) * 8, 8)
        col_base = pl.multiple_of(jnp.minimum(col >> 7, (cols - wide) // 128) * 128, 128)
        return row_base, col_base, row - row_base, col - col_base

    line = lax.broadcasted_iota(jnp.int32, (code_rows, window), 0)
    for p in range(count):
        row, col = table[home ^ cluster, p, 0], table[home ^ cluster, p, 1]
        code = jnp.where(line == 0, row >> 3, jnp.where(line == 1, row & 7, 0))
        code = jnp.where(line == 2, col >> 3, jnp.where(line == 3, col & 7, code))
        code_ref[p] = code.astype(f32).astype(bf16)
    for m in reversed(range(clusters)):
        for p in range(count):
            row_base, col_base, row_off, col_off = corner(m, p)
            lift = jnp.where(row_off == 0, 0, tall - row_off)
            shift = jnp.where(col_off == 0, 0, wide - col_off)
            for part in range(2):
                block = obj_ref[part, pl.ds(row_base, tall), pl.ds(col_base, wide)]
                block = pltpu.roll(block, shift, 1)[:, :window]
                block = pltpu.roll(block, lift, 0)[:window]
                out_refs[m][p, part] = block.astype(bf16)


def take_windows(obj, positions, window, members):
    clusters, count = len(positions), positions[0].shape[0]
    any_space = pl.BlockSpec(memory_space=pl.ANY)
    smem = pl.BlockSpec(memory_space=pltpu.SMEM)
    vmem = pl.BlockSpec(memory_space=pltpu.VMEM)
    out = pl.pallas_call(
        functools.partial(window_kernel, members),
        out_shape=[jax.ShapeDtypeStruct((count, 2, window, window), bf16)] * clusters
        + [jax.ShapeDtypeStruct((count, code_rows, window), bf16)],
        in_specs=[vmem, smem] + [any_space] * (clusters - 1),
        out_specs=[vmem] * (clusters + 1),
        scratch_shapes=[
            pltpu.SMEM((clusters, count, 2), jnp.int32),
            pltpu.SemaphoreType.DMA((clusters,)),
        ],
        compiler_params=pltpu.CompilerParams(vmem_limit_bytes=16 * 1024 * 1024),
        name="take_windows",
    )(obj, *positions)
    return out[:clusters], out[clusters]


def split(x):
    high = x.astype(bf16)
    return high, (x - high.astype(f32)).astype(bf16)


def cmul(a, b):
    return a[0] * b[0] - a[1] * b[1], a[0] * b[1] + a[1] * b[0]


def cmul_conj(a, b):
    return a[0] * b[0] + a[1] * b[1], a[0] * b[1] - a[1] * b[0]


def wave_kernel(members, clusters, probe_ref, kern_ref, left_ref, right_ref, code_ref, *rest):
    trans, terms, meas = rest[-3:]
    slices, count, _, _, window = trans.shape
    meas_refs, t_refs, out_refs = rest[:clusters], rest[clusters : clusters + slices], rest[clusters + slices : -3]
    own, cluster = lax.axis_index("depth"), lax.div(lax.axis_index("dp"), members)
    everyone = range(count)

    for m in range(slices):
        trans[own ^ m] = t_refs[m][...]
    for m, meas_ref in enumerate(meas_refs):

        @pl.when(lax.div(own, 2) ^ cluster == m)
        def _():
            meas[...] = meas_ref[...]

    def t_of(k, p):
        return trans[k, p, 0].astype(f32), trans[k, p, 1].astype(f32)

    def passes(x, axis, exact):
        if not exact:
            return x.astype(bf16)
        high, low = split(x)
        return jnp.concatenate([high, low, high], axis=axis)

    def rows(fields, sign, exact):
        x = jnp.concatenate([jnp.concatenate(f, axis=0) for f in fields], axis=1)
        x = passes(x, 0, exact)
        y = jnp.dot(left_ref[sign, :, : x.shape[0]], x, preferred_element_type=f32)
        cut = [y[:, p * window : (p + 1) * window] for p in everyone]
        return [(c[:window], c[window:]) for c in cut]

    def cols(fields, sign, exact):
        x = jnp.concatenate([jnp.concatenate(f, axis=1) for f in fields], axis=0)
        x = passes(x, 1, exact)
        y = jnp.dot(x, right_ref[sign, : x.shape[1]], preferred_element_type=f32)
        cut = [y[p * window : (p + 1) * window] for p in everyone]
        return [(c[:, :window], c[:, window:]) for c in cut]

    plus, minus = 0, 1

    def transform(fields, sign, exact):
        return cols(rows(fields, sign, exact), sign, exact)

    kern = (kern_ref[0], kern_ref[1])
    psi = [(probe_ref[0], probe_ref[1])] * count
    kept = []
    for k in range(slices):
        kept.append(psi)
        spectrum = transform([cmul(t_of(k, p), psi[p]) for p in everyone], minus, True)
        if k < slices - 1:
            psi = transform([cmul(kern, s) for s in spectrum], plus, True)

    def source(p):
        re, im = spectrum[p]
        scale = 2.0 * (re * re + im * im - meas[p])
        return scale * re, scale * im

    returned = transform([source(p) for p in everyone], plus, False)
    for k in reversed(range(slices)):
        for p in everyone:
            re, im = cmul_conj(kept[k][p], returned[p])
            terms[own ^ k, p, :window] = (re * grad_scale).astype(bf16)
            terms[own ^ k, p, window:] = (im * grad_scale).astype(bf16)
        if k > 0:
            chi = [cmul_conj(t_of(k, p), returned[p]) for p in everyone]
            spectrum = transform(chi, minus, False)
            returned = transform([cmul_conj(kern, s) for s in spectrum], plus, False)
    for n, out_ref in enumerate(out_refs):
        out_ref[:, : 2 * window] = terms[2 * n]
        out_ref[:, 2 * window :] = code_ref[...]


def run_waves(probe, kern, code, measured, windows, members):
    slices, count, window = len(windows), code.shape[0], code.shape[-1]
    left, right = dft_matrices(window)
    vmem = pl.BlockSpec(memory_space=pltpu.VMEM)
    block = jax.ShapeDtypeStruct((count, 2 * window + code_rows, window), bf16)
    return pl.pallas_call(
        functools.partial(wave_kernel, members, len(measured)),
        out_shape=[block] * (slices // 2),
        in_specs=[vmem] * (5 + len(measured) + slices),
        out_specs=[vmem] * (slices // 2),
        scratch_shapes=[
            pltpu.VMEM((slices, count, 2, window, window), bf16),
            pltpu.VMEM((slices, count, 2 * window, window), bf16),
            pltpu.VMEM((count, window, window), f32),
        ],
        compiler_params=pltpu.CompilerParams(vmem_limit_bytes=40 * 1024 * 1024),
        name="run_waves",
    )(probe, kern, jnp.asarray(left), jnp.asarray(right), code, *measured, *windows)


def place_kernel(*refs):
    block_refs, (out_ref, canvas) = refs[:-2], refs[-2:]
    _, stripe, cols = out_ref.shape
    count, _, window = block_refs[0].shape
    wide = window + 128
    first_row = lax.axis_index("dp") * stripe
    canvas[:, window : window + stripe, :] = jnp.zeros((2, stripe, canvas.shape[2]), f32)
    corners = []
    for block_ref in block_refs:
        for p in range(count):
            code = block_ref[p, 2 * window :].astype(f32)
            row = (8.0 * code[0:1] + code[1:2]).astype(jnp.int32)
            col = (8.0 * code[2:3] + code[3:4]).astype(jnp.int32)
            corners.append((row[0, 0], col[0, 0]))
    for n, (row, col) in enumerate(corners):
        block_ref, p = block_refs[n // count], n % count
        row = row - first_row + window
        row_base = pl.multiple_of((row >> 3) << 3, 8)
        col_base = pl.multiple_of((col >> 7) << 7, 128)

        @pl.when((row > 0) & (row < window + stripe))
        def _():
            for part in range(2):
                block = block_ref[p, part * window : (part + 1) * window].astype(f32)
                block = jnp.concatenate([block, jnp.zeros((8, window), f32)], axis=0)
                block = pltpu.roll(block, row - row_base, 0)
                block = jnp.concatenate([block, jnp.zeros((window + 8, 128), f32)], axis=1)
                block = pltpu.roll(block, col - col_base, 1)
                put = (part, pl.ds(row_base, window + 8), pl.ds(col_base, wide))
                canvas[put] = canvas[put] + block

    out_ref[...] = canvas[:, window : window + stripe, :cols]


def place_windows(blocks, stripe, cols):
    window = blocks[0].shape[-1]
    vmem = pl.BlockSpec(memory_space=pltpu.VMEM)
    tall = window + (stripe + 7) // 8 * 8 + window + 8
    return pl.pallas_call(
        place_kernel,
        out_shape=jax.ShapeDtypeStruct((2, stripe, cols), f32),
        in_specs=[vmem] * len(blocks),
        out_specs=vmem,
        scratch_shapes=[pltpu.VMEM((2, tall, cols + 128), f32)],
        compiler_params=pltpu.CompilerParams(vmem_limit_bytes=48 * 1024 * 1024),
        name="place_windows",
    )(*blocks)


def swap(block, depth_distance, dp_distance):
    depth, dp = lax.axis_size("depth"), lax.axis_size("dp")
    route = [
        (d * dp + j, (d ^ depth_distance) * dp + (j ^ dp_distance))
        for d in range(depth)
        for j in range(dp)
    ]
    return lax.ppermute(block, ("depth", "dp"), route)


def on_device(object_slices, positions, probe_field, propagator_phase, measured):
    depth, dp = lax.axis_size("depth"), lax.axis_size("dp")
    clusters = depth // 2
    members = dp // clusters
    rows, cols = object_slices.shape[-2:]
    window = probe_field.shape[-1]

    homes = [m * members for m in range(1, clusters)]
    all_positions = [positions] + [swap(positions, 0, home) for home in homes]
    obj, late = lax.optimization_barrier((fetch(object_slices[0]), measured))
    windows, code = take_windows(obj, all_positions, window, members)
    phase, code = lax.optimization_barrier((propagator_phase, code))
    windows = [windows[0]] + [swap(windows[m // 2], m, 0) for m in range(1, depth)]
    targets = [measured] + [swap(late, 0, home) for home in homes]
    kern = jnp.stack([jnp.cos(phase), jnp.sin(phase)])
    terms = run_waves(probe_field, kern, code, targets, windows, members)

    blocks = [
        swap(terms[m // 2], m, plane) if m or plane else terms[0]
        for plane in range(0, members, 2)
        for m in range(0, depth, 2)
    ]
    blocks += [swap(block, 0, 1) for block in blocks]
    return place_windows(blocks, rows // dp, cols)[None]


def solution(mesh):
    placed = (P("depth", None, None, None), P("dp", None), P(), P(), P("dp", None, None))
    return jax.shard_map(
        on_device,
        mesh=mesh,
        in_specs=placed,
        out_specs=P("depth", None, "dp", None),
        check_vma=False,
    )
```

```python
import functools
import math

import jax
import jax.numpy as jnp
import numpy as np
from jax import lax
from jax.experimental import pallas as pl
from jax.experimental.pallas import tpu as pltpu
from jax.sharding import PartitionSpec as P

grad_scale = 0.03125
f32 = jnp.float32
bf16 = jnp.bfloat16


def dft_matrices(size):
    k = np.arange(size)
    angles = 2.0 * np.pi * ((k[:, None] * k[None, :]) % size) / size
    c = np.cos(angles) / math.sqrt(size)
    s = np.sin(angles) / math.sqrt(size)
    plus = np.block([[c, s], [-s, c]]).astype(np.float32)
    minus = np.block([[c, -s], [s, c]]).astype(np.float32)
    parts = []
    for full in (plus, minus):
        high = full.astype(bf16)
        low = (full - high.astype(np.float32)).astype(bf16)
        parts.append((high, low))
    (ph, plo), (mh, mlo) = parts
    right = np.stack([np.concatenate([ph, ph, plo], 0), np.concatenate([mh, mh, mlo], 0)])
    left = np.stack([np.concatenate([mh, mh, mlo], 1), np.concatenate([ph, ph, plo], 1)])
    return left, right


code_rows = 16


def fetch_kernel(obj_ref, out_ref, sem):
    copy = pltpu.make_async_copy(obj_ref, out_ref, sem)
    copy.start()
    copy.wait()


def fetch(obj):
    size = 4 * math.prod(obj.shape)
    return pl.pallas_call(
        fetch_kernel,
        out_shape=jax.ShapeDtypeStruct(obj.shape, obj.dtype),
        in_specs=[pl.BlockSpec(memory_space=pltpu.HBM)],
        out_specs=pl.BlockSpec(memory_space=pltpu.VMEM),
        scratch_shapes=[pltpu.SemaphoreType.DMA],
        compiler_params=pltpu.CompilerParams(vmem_limit_bytes=16 * 1024 * 1024),
        cost_estimate=pl.CostEstimate(flops=0, bytes_accessed=2 * size, transcendentals=0),
        name="fetch_slice",
    )(obj)


def window_kernel(members, obj_ref, *rest):
    table, table_sems = rest[-2:]
    clusters, count = table.shape[:2]
    pos_refs, out_refs, code_ref = rest[:clusters], rest[clusters:-3], rest[-3]
    window = out_refs[0].shape[-1]
    rows, cols = obj_ref.shape[-2:]
    tall, wide = window + 8, window + 128
    cluster = lax.div(lax.axis_index("dp"), members)
    home = lax.div(lax.axis_index("depth"), 2)

    fetches = [
        pltpu.make_async_copy(pos_refs[m], table.at[m], table_sems.at[m])
        for m in range(1, clusters)
    ]
    for fetch in fetches:
        fetch.start()
    for p in range(count):
        for axis in range(2):
            table[0, p, axis] = pos_refs[0][p, axis]
    for fetch in fetches:
        fetch.wait()

    def corner(m, p):
        at = home ^ cluster ^ m
        row, col = table[at, p, 0], table[at, p, 1]
        row_base = pl.multiple_of(jnp.minimum(row >> 3, (rows - tall) // 8) * 8, 8)
        col_base = pl.multiple_of(jnp.minimum(col >> 7, (cols - wide) // 128) * 128, 128)
        return row_base, col_base, row - row_base, col - col_base

    line = lax.broadcasted_iota(jnp.int32, (code_rows, window), 0)
    for p in range(count):
        row, col = table[home ^ cluster, p, 0], table[home ^ cluster, p, 1]
        code = jnp.where(line == 0, row >> 3, jnp.where(line == 1, row & 7, 0))
        code = jnp.where(line == 2, col >> 3, jnp.where(line == 3, col & 7, code))
        code_ref[p] = code.astype(f32).astype(bf16)
    for m in reversed(range(clusters)):
        for p in range(count):
            row_base, col_base, row_off, col_off = corner(m, p)
            lift = jnp.where(row_off == 0, 0, tall - row_off)
            shift = jnp.where(col_off == 0, 0, wide - col_off)
            for part in range(2):
                block = obj_ref[part, pl.ds(row_base, tall), pl.ds(col_base, wide)]
                block = pltpu.roll(block, shift, 1)[:, :window]
                block = pltpu.roll(block, lift, 0)[:window]
                out_refs[m][p, part] = block.astype(bf16)


def take_windows(obj, positions, window, members):
    clusters, count = len(positions), positions[0].shape[0]
    any_space = pl.BlockSpec(memory_space=pl.ANY)
    smem = pl.BlockSpec(memory_space=pltpu.SMEM)
    vmem = pl.BlockSpec(memory_space=pltpu.VMEM)
    out = pl.pallas_call(
        functools.partial(window_kernel, members),
        out_shape=[jax.ShapeDtypeStruct((count, 2, window, window), bf16)] * clusters
        + [jax.ShapeDtypeStruct((count, code_rows, window), bf16)],
        in_specs=[vmem, smem] + [any_space] * (clusters - 1),
        out_specs=[vmem] * (clusters + 1),
        scratch_shapes=[
            pltpu.SMEM((clusters, count, 2), jnp.int32),
            pltpu.SemaphoreType.DMA((clusters,)),
        ],
        compiler_params=pltpu.CompilerParams(vmem_limit_bytes=16 * 1024 * 1024),
        name="take_windows",
    )(obj, *positions)
    return out[:clusters], out[clusters]


def split(x):
    high = x.astype(bf16)
    return high, (x - high.astype(f32)).astype(bf16)


def cmul(a, b):
    return a[0] * b[0] - a[1] * b[1], a[0] * b[1] + a[1] * b[0]


def cmul_conj(a, b):
    return a[0] * b[0] + a[1] * b[1], a[0] * b[1] - a[1] * b[0]


def wave_kernel(members, clusters, probe_ref, kern_ref, left_ref, right_ref, code_ref, *rest):
    trans, terms, meas = rest[-3:]
    slices, count, _, _, window = trans.shape
    meas_refs, t_refs, out_refs = rest[:clusters], rest[clusters : clusters + slices], rest[clusters + slices : -3]
    own, cluster = lax.axis_index("depth"), lax.div(lax.axis_index("dp"), members)
    everyone = range(count)

    for m in range(slices):
        trans[own ^ m] = t_refs[m][...]
    for m, meas_ref in enumerate(meas_refs):

        @pl.when(lax.div(own, 2) ^ cluster == m)
        def _():
            meas[...] = meas_ref[...]

    def t_of(k, p):
        return trans[k, p, 0].astype(f32), trans[k, p, 1].astype(f32)

    def passes(x, axis, exact):
        if not exact:
            return x.astype(bf16)
        high, low = split(x)
        return jnp.concatenate([high, low, high], axis=axis)

    def rows(fields, sign, exact):
        x = jnp.concatenate([jnp.concatenate(f, axis=0) for f in fields], axis=1)
        x = passes(x, 0, exact)
        y = jnp.dot(left_ref[sign, :, : x.shape[0]], x, preferred_element_type=f32)
        cut = [y[:, p * window : (p + 1) * window] for p in everyone]
        return [(c[:window], c[window:]) for c in cut]

    def cols(fields, sign, exact):
        x = jnp.concatenate([jnp.concatenate(f, axis=1) for f in fields], axis=0)
        x = passes(x, 1, exact)
        y = jnp.dot(x, right_ref[sign, : x.shape[1]], preferred_element_type=f32)
        cut = [y[p * window : (p + 1) * window] for p in everyone]
        return [(c[:, :window], c[:, window:]) for c in cut]

    plus, minus = 0, 1

    def transform(fields, sign, exact):
        return cols(rows(fields, sign, exact), sign, exact)

    kern = (kern_ref[0], kern_ref[1])
    psi = [(probe_ref[0], probe_ref[1])] * count
    kept = []
    for k in range(slices):
        kept.append(psi)
        spectrum = transform([cmul(t_of(k, p), psi[p]) for p in everyone], minus, True)
        if k < slices - 1:
            psi = transform([cmul(kern, s) for s in spectrum], plus, True)

    def source(p):
        re, im = spectrum[p]
        scale = 2.0 * (re * re + im * im - meas[p])
        return scale * re, scale * im

    returned = transform([source(p) for p in everyone], plus, False)
    for k in reversed(range(slices)):
        for p in everyone:
            re, im = cmul_conj(kept[k][p], returned[p])
            terms[own ^ k, p, :window] = (re * grad_scale).astype(bf16)
            terms[own ^ k, p, window:] = (im * grad_scale).astype(bf16)
        if k > 0:
            chi = [cmul_conj(t_of(k, p), returned[p]) for p in everyone]
            spectrum = transform(chi, minus, False)
            returned = transform([cmul_conj(kern, s) for s in spectrum], plus, False)
    for n, out_ref in enumerate(out_refs):
        out_ref[:, : 2 * window] = terms[2 * n]
        out_ref[:, 2 * window :] = code_ref[...]


def run_waves(probe, kern, code, measured, windows, members):
    slices, count, window = len(windows), code.shape[0], code.shape[-1]
    left, right = dft_matrices(window)
    vmem = pl.BlockSpec(memory_space=pltpu.VMEM)
    block = jax.ShapeDtypeStruct((count, 2 * window + code_rows, window), bf16)
    return pl.pallas_call(
        functools.partial(wave_kernel, members, len(measured)),
        out_shape=[block] * (slices // 2),
        in_specs=[vmem] * (5 + len(measured) + slices),
        out_specs=[vmem] * (slices // 2),
        scratch_shapes=[
            pltpu.VMEM((slices, count, 2, window, window), bf16),
            pltpu.VMEM((slices, count, 2 * window, window), bf16),
            pltpu.VMEM((count, window, window), f32),
        ],
        compiler_params=pltpu.CompilerParams(vmem_limit_bytes=40 * 1024 * 1024),
        name="run_waves",
    )(probe, kern, jnp.asarray(left), jnp.asarray(right), code, *measured, *windows)


def add_blocks(block_refs, canvas, stripe):
    count, _, window = block_refs[0].shape
    cols = canvas.shape[-1] - 128
    wide = window + 128
    first_row = lax.axis_index("dp") * stripe
    corners = []
    for block_ref in block_refs:
        for p in range(count):
            code = block_ref[p, 2 * window :].astype(f32)
            row = (8.0 * code[0:1] + code[1:2]).astype(jnp.int32)
            col = (8.0 * code[2:3] + code[3:4]).astype(jnp.int32)
            corners.append((row[0, 0], col[0, 0]))
    for n, (row, col) in enumerate(corners):
        block_ref, p = block_refs[n // count], n % count
        row = row - first_row + window
        row_base = pl.multiple_of((row >> 3) << 3, 8)
        col_base = pl.multiple_of((col >> 7) << 7, 128)

        @pl.when((row > 0) & (row < window + stripe))
        def _():
            for part in range(2):
                block = block_ref[p, part * window : (part + 1) * window].astype(f32)
                block = jnp.concatenate([block, jnp.zeros((8, window), f32)], axis=0)
                block = pltpu.roll(block, row - row_base, 0)
                block = jnp.concatenate([block, jnp.zeros((window + 8, 128), f32)], axis=1)
                block = pltpu.roll(block, col - col_base, 1)
                put = (part, pl.ds(row_base, window + 8), pl.ds(col_base, wide))
                canvas[put] = canvas[put] + block


def first_kernel(stripe, *refs):
    block_refs, canvas = refs[:-1], refs[-1]
    window = block_refs[0].shape[-1]
    canvas[:, window : window + stripe, :] = jnp.zeros((2, stripe, canvas.shape[2]), f32)
    add_blocks(block_refs, canvas, stripe)


def second_kernel(start_ref, *refs):
    block_refs, (out_ref, canvas) = refs[:-2], refs[-2:]
    _, stripe, cols = out_ref.shape
    window = block_refs[0].shape[-1]
    canvas[:, window : window + stripe, :] = start_ref[:, window : window + stripe, :]
    add_blocks(block_refs, canvas, stripe)
    out_ref[...] = canvas[:, window : window + stripe, :cols]


def place_windows(near, far, stripe, cols):
    window = near[0].shape[-1]
    vmem = pl.BlockSpec(memory_space=pltpu.VMEM)
    tall = window + (stripe + 7) // 8 * 8 + window + 8
    canvas = (2, tall, cols + 128)
    limit = pltpu.CompilerParams(vmem_limit_bytes=24 * 1024 * 1024)
    start = pl.pallas_call(
        functools.partial(first_kernel, stripe),
        out_shape=jax.ShapeDtypeStruct(canvas, f32),
        in_specs=[vmem] * len(near),
        out_specs=vmem,
        compiler_params=limit,
        name="place_near",
    )(*near)
    return pl.pallas_call(
        second_kernel,
        out_shape=jax.ShapeDtypeStruct((2, stripe, cols), f32),
        in_specs=[vmem] * (1 + len(far)),
        out_specs=vmem,
        scratch_shapes=[pltpu.VMEM(canvas, f32)],
        compiler_params=limit,
        name="place_far",
    )(start, *far)


def swap(block, depth_distance, dp_distance):
    depth, dp = lax.axis_size("depth"), lax.axis_size("dp")
    route = [
        (d * dp + j, (d ^ depth_distance) * dp + (j ^ dp_distance))
        for d in range(depth)
        for j in range(dp)
    ]
    return lax.ppermute(block, ("depth", "dp"), route)


def on_device(object_slices, positions, probe_field, propagator_phase, measured):
    depth, dp = lax.axis_size("depth"), lax.axis_size("dp")
    clusters = depth // 2
    members = dp // clusters
    rows, cols = object_slices.shape[-2:]
    window = probe_field.shape[-1]

    homes = [m * members for m in range(1, clusters)]
    all_positions = [positions] + [swap(positions, 0, home) for home in homes]
    windows, code = take_windows(fetch(object_slices[0]), all_positions, window, members)
    phase, code = lax.optimization_barrier((propagator_phase, code))
    windows = [windows[0]] + [swap(windows[m // 2], m, 0) for m in range(1, depth)]
    targets = [measured] + [swap(measured, 0, home) for home in homes]
    kern = jnp.stack([jnp.cos(phase), jnp.sin(phase)])
    terms = run_waves(probe_field, kern, code, targets, windows, members)

    blocks = [
        swap(terms[m // 2], m, plane) if m or plane else terms[0]
        for plane in range(0, members, 2)
        for m in range(0, depth, 2)
    ]
    return place_windows(blocks, [swap(block, 0, 1) for block in blocks], rows // dp, cols)[None]


def solution(mesh):
    placed = (P("depth", None, None, None), P("dp", None), P(), P(), P("dp", None, None))
    return jax.shard_map(
        on_device,
        mesh=mesh,
        in_specs=placed,
        out_specs=P("depth", None, "dp", None),
        check_vma=False,
    )
```

```python
import functools
import math

import jax
import jax.numpy as jnp
import numpy as np
from jax import lax
from jax.experimental import pallas as pl
from jax.experimental.pallas import tpu as pltpu
from jax.sharding import PartitionSpec as P

grad_scale = 0.03125
f32 = jnp.float32
bf16 = jnp.bfloat16


def dft_matrices(size):
    k = np.arange(size)
    angles = 2.0 * np.pi * ((k[:, None] * k[None, :]) % size) / size
    c = np.cos(angles) / math.sqrt(size)
    s = np.sin(angles) / math.sqrt(size)
    plus = np.block([[c, s], [-s, c]]).astype(np.float32)
    minus = np.block([[c, -s], [s, c]]).astype(np.float32)
    parts = []
    for full in (plus, minus):
        high = full.astype(bf16)
        low = (full - high.astype(np.float32)).astype(bf16)
        parts.append((high, low))
    (ph, plo), (mh, mlo) = parts
    right = np.stack([np.concatenate([ph, ph, plo], 0), np.concatenate([mh, mh, mlo], 0)])
    left = np.stack([np.concatenate([mh, mh, mlo], 1), np.concatenate([ph, ph, plo], 1)])
    return jnp.asarray(left), jnp.asarray(right)


code_rows = 16

limit = pltpu.CompilerParams(vmem_limit_bytes=32 * 1024 * 1024)
vmem = pl.BlockSpec(memory_space=pltpu.VMEM)


def fetch_kernel(obj_ref, out_ref, sem):
    copy = pltpu.make_async_copy(obj_ref, out_ref, sem)
    copy.start()
    copy.wait()


def fetch(obj):
    size = 4 * math.prod(obj.shape)
    return pl.pallas_call(
        fetch_kernel,
        out_shape=jax.ShapeDtypeStruct(obj.shape, obj.dtype),
        in_specs=[pl.BlockSpec(memory_space=pltpu.HBM)],
        out_specs=pl.BlockSpec(memory_space=pltpu.VMEM),
        scratch_shapes=[pltpu.SemaphoreType.DMA],
        compiler_params=pltpu.CompilerParams(vmem_limit_bytes=16 * 1024 * 1024),
        cost_estimate=pl.CostEstimate(flops=0, bytes_accessed=2 * size, transcendentals=0),
        name="fetch_slice",
    )(obj)


def window_kernel(members, obj_ref, *rest):
    table, table_sems = rest[-2:]
    clusters, count = table.shape[:2]
    pos_refs, out_refs, code_ref = rest[:clusters], rest[clusters:-3], rest[-3]
    window = out_refs[0].shape[-1]
    rows, cols = obj_ref.shape[-2:]
    tall, wide = window + 8, window + 128
    cluster = lax.div(lax.axis_index("dp"), members)
    home = lax.div(lax.axis_index("depth"), 2)

    fetches = [
        pltpu.make_async_copy(pos_refs[m], table.at[m], table_sems.at[m])
        for m in range(1, clusters)
    ]
    for fetch in fetches:
        fetch.start()
    for p in range(count):
        for axis in range(2):
            table[0, p, axis] = pos_refs[0][p, axis]
    for fetch in fetches:
        fetch.wait()

    def corner(m, p):
        at = home ^ cluster ^ m
        row, col = table[at, p, 0], table[at, p, 1]
        row_base = pl.multiple_of(jnp.minimum(row >> 3, (rows - tall) // 8) * 8, 8)
        col_base = pl.multiple_of(jnp.minimum(col >> 7, (cols - wide) // 128) * 128, 128)
        return row_base, col_base, row - row_base, col - col_base

    line = lax.broadcasted_iota(jnp.int32, (code_rows, window), 0)
    for p in range(count):
        row, col = table[home ^ cluster, p, 0], table[home ^ cluster, p, 1]
        code = jnp.where(line == 0, row >> 3, jnp.where(line == 1, row & 7, 0))
        code = jnp.where(line == 2, col >> 3, jnp.where(line == 3, col & 7, code))
        code_ref[p] = code.astype(f32).astype(bf16)
    for m in reversed(range(clusters)):
        for p in range(count):
            row_base, col_base, row_off, col_off = corner(m, p)
            lift = jnp.where(row_off == 0, 0, tall - row_off)
            shift = jnp.where(col_off == 0, 0, wide - col_off)
            for part in range(2):
                block = obj_ref[part, pl.ds(row_base, tall), pl.ds(col_base, wide)]
                block = pltpu.roll(block, shift, 1)[:, :window]
                block = pltpu.roll(block, lift, 0)[:window]
                out_refs[m][p, part] = block.astype(bf16)


def take_windows(obj, positions, window, members):
    clusters, count = len(positions), positions[0].shape[0]
    any_space = pl.BlockSpec(memory_space=pl.ANY)
    smem = pl.BlockSpec(memory_space=pltpu.SMEM)
    vmem = pl.BlockSpec(memory_space=pltpu.VMEM)
    out = pl.pallas_call(
        functools.partial(window_kernel, members),
        out_shape=[jax.ShapeDtypeStruct((count, 2, window, window), bf16)] * clusters
        + [jax.ShapeDtypeStruct((count, code_rows, window), bf16)],
        in_specs=[vmem, smem] + [any_space] * (clusters - 1),
        out_specs=[vmem] * (clusters + 1),
        scratch_shapes=[
            pltpu.SMEM((clusters, count, 2), jnp.int32),
            pltpu.SemaphoreType.DMA((clusters,)),
        ],
        compiler_params=pltpu.CompilerParams(vmem_limit_bytes=16 * 1024 * 1024),
        name="take_windows",
    )(obj, *positions)
    return out[:clusters], out[clusters]


def split(x):
    high = x.astype(bf16)
    return high, (x - high.astype(f32)).astype(bf16)


def cmul(a, b):
    return a[0] * b[0] - a[1] * b[1], a[0] * b[1] + a[1] * b[0]


def cmul_conj(a, b):
    return a[0] * b[0] + a[1] * b[1], a[0] * b[1] - a[1] * b[0]


def transform(fields, sign, tables, exact):
    left_ref, right_ref = tables
    size = fields[0][0].shape[0]

    def passes(x, axis):
        if not exact:
            return x.astype(bf16)
        high, low = split(x)
        return jnp.concatenate([high, low, high], axis=axis)

    x = passes(jnp.concatenate([jnp.concatenate(f, axis=0) for f in fields], axis=1), 0)
    y = jnp.dot(left_ref[sign, :, : x.shape[0]], x, preferred_element_type=f32)
    fields = [y[:, n * size : (n + 1) * size] for n in range(len(fields))]
    fields = [jnp.concatenate([f[:size], f[size:]], axis=1) for f in fields]
    x = passes(jnp.concatenate(fields, axis=0), 1)
    y = jnp.dot(x, right_ref[sign, : x.shape[1]], preferred_element_type=f32)
    fields = [y[n * size : (n + 1) * size] for n in range(len(fields))]
    return [(f[:, :size], f[:, size:]) for f in fields]


def forward_kernel(probe_ref, kern_ref, *rest):
    tables, t_refs, (trans, waves) = rest[:2], rest[2:-2], rest[-2:]
    slices, count = trans.shape[:2]
    own = lax.axis_index("depth")
    everyone = range(count)
    for m in range(slices):
        trans[own ^ m] = t_refs[m][...]
    kern = (kern_ref[0], kern_ref[1])
    psi = [(probe_ref[0], probe_ref[1])] * count
    for k in range(slices):
        field = [cmul((trans[k, p, 0].astype(f32), trans[k, p, 1].astype(f32)), psi[p]) for p in everyone]
        psi = transform(field, 1, tables, True)
        if k < slices - 1:
            psi = transform([cmul(kern, s) for s in psi], 0, tables, True)
        for p in everyone:
            waves[k, p, 0] = psi[p][0]
            waves[k, p, 1] = psi[p][1]


def backward_kernel(members, clusters, probe_ref, kern_ref, code_ref, trans, waves, *rest):
    tables, meas_refs = rest[:2], rest[2 : 2 + clusters]
    out_refs, (terms, meas) = rest[2 + clusters : -2], rest[-2:]
    slices, count, _, window, _ = trans.shape
    own, cluster = lax.axis_index("depth"), lax.div(lax.axis_index("dp"), members)
    everyone = range(count)
    for m, meas_ref in enumerate(meas_refs):

        @pl.when(lax.div(own, 2) ^ cluster == m)
        def _():
            meas[...] = meas_ref[...]

    kern = (kern_ref[0], kern_ref[1])

    def source(p):
        re, im = waves[slices - 1, p, 0], waves[slices - 1, p, 1]
        scale = 2.0 * (re * re + im * im - meas[p])
        return scale * re, scale * im

    returned = transform([source(p) for p in everyone], 0, tables, False)
    for k in reversed(range(slices)):
        for p in everyone:
            wave = (waves[k - 1, p, 0], waves[k - 1, p, 1]) if k else (probe_ref[0], probe_ref[1])
            re, im = cmul_conj(wave, returned[p])
            terms[own ^ k, p, :window] = (re * grad_scale).astype(bf16)
            terms[own ^ k, p, window:] = (im * grad_scale).astype(bf16)
        if k > 0:
            chi = [
                cmul_conj((trans[k, p, 0].astype(f32), trans[k, p, 1].astype(f32)), returned[p])
                for p in everyone
            ]
            chi = transform(chi, 1, tables, False)
            returned = transform([cmul_conj(kern, c) for c in chi], 0, tables, False)
    for n, out_ref in enumerate(out_refs):
        out_ref[:, : 2 * window] = terms[2 * n]
        out_ref[:, 2 * window :] = code_ref[...]


def run_forward(probe, kern, tables, windows):
    slices, shape = len(windows), windows[0].shape
    return pl.pallas_call(
        forward_kernel,
        out_shape=[
            jax.ShapeDtypeStruct((slices,) + shape, bf16),
            jax.ShapeDtypeStruct((slices,) + shape, f32),
        ],
        in_specs=[vmem] * (4 + slices),
        out_specs=[vmem, vmem],
        compiler_params=limit,
        name="run_forward",
    )(probe, kern, *tables, *windows)


def run_backward(probe, kern, code, trans, waves, tables, measured, members):
    slices, count, _, window, _ = trans.shape
    block = jax.ShapeDtypeStruct((count, 2 * window + code_rows, window), bf16)
    return pl.pallas_call(
        functools.partial(backward_kernel, members, len(measured)),
        out_shape=[block] * (slices // 2),
        in_specs=[vmem] * (7 + len(measured)),
        out_specs=[vmem] * (slices // 2),
        scratch_shapes=[
            pltpu.VMEM((slices, count, 2 * window, window), bf16),
            pltpu.VMEM((count, window, window), f32),
        ],
        compiler_params=limit,
        name="run_backward",
    )(probe, kern, code, trans, waves, *tables, *measured)


def add_blocks(block_refs, canvas, stripe):
    count, _, window = block_refs[0].shape
    cols = canvas.shape[-1] - 128
    wide = window + 128
    first_row = lax.axis_index("dp") * stripe
    corners = []
    for block_ref in block_refs:
        for p in range(count):
            code = block_ref[p, 2 * window :].astype(f32)
            row = (8.0 * code[0:1] + code[1:2]).astype(jnp.int32)
            col = (8.0 * code[2:3] + code[3:4]).astype(jnp.int32)
            corners.append((row[0, 0], col[0, 0]))
    for n, (row, col) in enumerate(corners):
        block_ref, p = block_refs[n // count], n % count
        row = row - first_row + window
        row_base = pl.multiple_of((row >> 3) << 3, 8)
        col_base = pl.multiple_of((col >> 7) << 7, 128)

        @pl.when((row > 0) & (row < window + stripe))
        def _():
            for part in range(2):
                block = block_ref[p, part * window : (part + 1) * window].astype(f32)
                block = jnp.concatenate([block, jnp.zeros((8, window), f32)], axis=0)
                block = pltpu.roll(block, row - row_base, 0)
                block = jnp.concatenate([block, jnp.zeros((window + 8, 128), f32)], axis=1)
                block = pltpu.roll(block, col - col_base, 1)
                put = (part, pl.ds(row_base, window + 8), pl.ds(col_base, wide))
                canvas[put] = canvas[put] + block


def first_kernel(stripe, *refs):
    block_refs, canvas = refs[:-1], refs[-1]
    window = block_refs[0].shape[-1]
    canvas[:, window : window + stripe, :] = jnp.zeros((2, stripe, canvas.shape[2]), f32)
    add_blocks(block_refs, canvas, stripe)


def second_kernel(start_ref, *refs):
    block_refs, (out_ref, canvas) = refs[:-2], refs[-2:]
    _, stripe, cols = out_ref.shape
    window = block_refs[0].shape[-1]
    canvas[:, window : window + stripe, :] = start_ref[:, window : window + stripe, :]
    add_blocks(block_refs, canvas, stripe)
    out_ref[...] = canvas[:, window : window + stripe, :cols]


def place_windows(near, far, stripe, cols):
    window = near[0].shape[-1]
    vmem = pl.BlockSpec(memory_space=pltpu.VMEM)
    tall = window + (stripe + 7) // 8 * 8 + window + 8
    canvas = (2, tall, cols + 128)
    limit = pltpu.CompilerParams(vmem_limit_bytes=24 * 1024 * 1024)
    start = pl.pallas_call(
        functools.partial(first_kernel, stripe),
        out_shape=jax.ShapeDtypeStruct(canvas, f32),
        in_specs=[vmem] * len(near),
        out_specs=vmem,
        compiler_params=limit,
        name="place_near",
    )(*near)
    return pl.pallas_call(
        second_kernel,
        out_shape=jax.ShapeDtypeStruct((2, stripe, cols), f32),
        in_specs=[vmem] * (1 + len(far)),
        out_specs=vmem,
        scratch_shapes=[pltpu.VMEM(canvas, f32)],
        compiler_params=limit,
        name="place_far",
    )(start, *far)


def swap(block, depth_distance, dp_distance):
    depth, dp = lax.axis_size("depth"), lax.axis_size("dp")
    route = [
        (d * dp + j, (d ^ depth_distance) * dp + (j ^ dp_distance))
        for d in range(depth)
        for j in range(dp)
    ]
    return lax.ppermute(block, ("depth", "dp"), route)


def on_device(object_slices, positions, probe_field, propagator_phase, measured):
    depth, dp = lax.axis_size("depth"), lax.axis_size("dp")
    clusters = depth // 2
    members = dp // clusters
    rows, cols = object_slices.shape[-2:]
    window = probe_field.shape[-1]

    homes = [m * members for m in range(1, clusters)]
    all_positions = [positions] + [swap(positions, 0, home) for home in homes]
    windows, code = take_windows(fetch(object_slices[0]), all_positions, window, members)
    phase, code = lax.optimization_barrier((propagator_phase, code))
    windows = [windows[0]] + [swap(windows[m // 2], m, 0) for m in range(1, depth)]
    kern = jnp.stack([jnp.cos(phase), jnp.sin(phase)])
    kern, late = lax.optimization_barrier((kern, measured))
    targets = [measured] + [swap(late, 0, home) for home in homes]
    tables = dft_matrices(window)
    trans, waves = run_forward(probe_field, kern, tables, windows)
    terms = run_backward(probe_field, kern, code, trans, waves, tables, targets, members)

    blocks = [
        swap(terms[m // 2], m, plane) if m or plane else terms[0]
        for plane in range(0, members, 2)
        for m in range(0, depth, 2)
    ]
    return place_windows(blocks, [swap(block, 0, 1) for block in blocks], rows // dp, cols)[None]


def solution(mesh):
    placed = (P("depth", None, None, None), P("dp", None), P(), P(), P("dp", None, None))
    return jax.shard_map(
        on_device,
        mesh=mesh,
        in_specs=placed,
        out_specs=P("depth", None, "dp", None),
        check_vma=False,
    )
```

```python
import functools
import math

import jax
import jax.numpy as jnp
import numpy as np
from jax import lax
from jax.experimental import pallas as pl
from jax.experimental.pallas import tpu as pltpu
from jax.sharding import PartitionSpec as P

grad_scale = 0.03125
f32 = jnp.float32
bf16 = jnp.bfloat16


def dft_matrices(size):
    k = np.arange(size)
    angles = 2.0 * np.pi * ((k[:, None] * k[None, :]) % size) / size
    c = np.cos(angles) / math.sqrt(size)
    s = np.sin(angles) / math.sqrt(size)
    plus = np.block([[c, s], [-s, c]]).astype(np.float32)
    minus = np.block([[c, -s], [s, c]]).astype(np.float32)
    parts = []
    for full in (plus, minus):
        high = full.astype(bf16)
        low = (full - high.astype(np.float32)).astype(bf16)
        parts.append((high, low))
    (ph, plo), (mh, mlo) = parts
    right = np.stack([np.concatenate([ph, ph, plo], 0), np.concatenate([mh, mh, mlo], 0)])
    left = np.stack([np.concatenate([mh, mh, mlo], 1), np.concatenate([ph, ph, plo], 1)])
    return jnp.asarray(left), jnp.asarray(right)


code_rows = 16

limit = pltpu.CompilerParams(vmem_limit_bytes=32 * 1024 * 1024)
vmem = pl.BlockSpec(memory_space=pltpu.VMEM)


def fetch_kernel(obj_ref, out_ref, sem):
    copy = pltpu.make_async_copy(obj_ref, out_ref, sem)
    copy.start()
    copy.wait()


def fetch(obj):
    size = 4 * math.prod(obj.shape)
    return pl.pallas_call(
        fetch_kernel,
        out_shape=jax.ShapeDtypeStruct(obj.shape, obj.dtype),
        in_specs=[pl.BlockSpec(memory_space=pltpu.HBM)],
        out_specs=pl.BlockSpec(memory_space=pltpu.VMEM),
        scratch_shapes=[pltpu.SemaphoreType.DMA],
        compiler_params=pltpu.CompilerParams(vmem_limit_bytes=16 * 1024 * 1024),
        cost_estimate=pl.CostEstimate(flops=0, bytes_accessed=2 * size, transcendentals=0),
        name="fetch_slice",
    )(obj)


def window_kernel(members, obj_ref, *rest):
    table, table_sems = rest[-2:]
    clusters, count = table.shape[:2]
    pos_refs, out_refs, code_ref = rest[:clusters], rest[clusters:-3], rest[-3]
    window = out_refs[0].shape[-1]
    rows, cols = obj_ref.shape[-2:]
    tall, wide = window + 8, window + 128
    cluster = lax.div(lax.axis_index("dp"), members)
    home = lax.div(lax.axis_index("depth"), 2)

    fetches = [
        pltpu.make_async_copy(pos_refs[m], table.at[m], table_sems.at[m])
        for m in range(1, clusters)
    ]
    for fetch in fetches:
        fetch.start()
    for p in range(count):
        for axis in range(2):
            table[0, p, axis] = pos_refs[0][p, axis]
    for fetch in fetches:
        fetch.wait()

    def corner(m, p):
        at = home ^ cluster ^ m
        row, col = table[at, p, 0], table[at, p, 1]
        row_base = pl.multiple_of(jnp.minimum(row >> 3, (rows - tall) // 8) * 8, 8)
        col_base = pl.multiple_of(jnp.minimum(col >> 7, (cols - wide) // 128) * 128, 128)
        return row_base, col_base, row - row_base, col - col_base

    line = lax.broadcasted_iota(jnp.int32, (code_rows, window), 0)
    for p in range(count):
        row, col = table[home ^ cluster, p, 0], table[home ^ cluster, p, 1]
        code = jnp.where(line == 0, row >> 3, jnp.where(line == 1, row & 7, 0))
        code = jnp.where(line == 2, col >> 3, jnp.where(line == 3, col & 7, code))
        code_ref[p] = code.astype(f32).astype(bf16)
    for m in reversed(range(clusters)):
        for p in range(count):
            row_base, col_base, row_off, col_off = corner(m, p)
            lift = jnp.where(row_off == 0, 0, tall - row_off)
            shift = jnp.where(col_off == 0, 0, wide - col_off)
            for part in range(2):
                block = obj_ref[part, pl.ds(row_base, tall), pl.ds(col_base, wide)]
                block = pltpu.roll(block, shift, 1)[:, :window]
                block = pltpu.roll(block, lift, 0)[:window]
                out_refs[m][p, part] = block.astype(bf16)


def take_windows(obj, positions, window, members):
    clusters, count = len(positions), positions[0].shape[0]
    any_space = pl.BlockSpec(memory_space=pl.ANY)
    smem = pl.BlockSpec(memory_space=pltpu.SMEM)
    vmem = pl.BlockSpec(memory_space=pltpu.VMEM)
    out = pl.pallas_call(
        functools.partial(window_kernel, members),
        out_shape=[jax.ShapeDtypeStruct((count, 2, window, window), bf16)] * clusters
        + [jax.ShapeDtypeStruct((count, code_rows, window), bf16)],
        in_specs=[vmem, smem] + [any_space] * (clusters - 1),
        out_specs=[vmem] * (clusters + 1),
        scratch_shapes=[
            pltpu.SMEM((clusters, count, 2), jnp.int32),
            pltpu.SemaphoreType.DMA((clusters,)),
        ],
        compiler_params=pltpu.CompilerParams(vmem_limit_bytes=16 * 1024 * 1024),
        name="take_windows",
    )(obj, *positions)
    return out[:clusters], out[clusters]


def split(x):
    high = x.astype(bf16)
    return high, (x - high.astype(f32)).astype(bf16)


def cmul(a, b):
    return a[0] * b[0] - a[1] * b[1], a[0] * b[1] + a[1] * b[0]


def cmul_conj(a, b):
    return a[0] * b[0] + a[1] * b[1], a[0] * b[1] - a[1] * b[0]


def transform(fields, sign, tables, exact):
    left_ref, right_ref = tables
    size = fields[0][0].shape[0]

    def passes(x, axis):
        if not exact:
            return x.astype(bf16)
        high, low = split(x)
        return jnp.concatenate([high, low, high], axis=axis)

    x = passes(jnp.concatenate([jnp.concatenate(f, axis=0) for f in fields], axis=1), 0)
    y = jnp.dot(left_ref[sign, :, : x.shape[0]], x, preferred_element_type=f32)
    fields = [y[:, n * size : (n + 1) * size] for n in range(len(fields))]
    fields = [jnp.concatenate([f[:size], f[size:]], axis=1) for f in fields]
    x = passes(jnp.concatenate(fields, axis=0), 1)
    y = jnp.dot(x, right_ref[sign, : x.shape[1]], preferred_element_type=f32)
    fields = [y[n * size : (n + 1) * size] for n in range(len(fields))]
    return [(f[:, :size], f[:, size:]) for f in fields]


def forward_kernel(probe_ref, kern_ref, *rest):
    tables, t_refs, (trans, waves) = rest[:2], rest[2:-2], rest[-2:]
    slices, count = trans.shape[:2]
    own = lax.axis_index("depth")
    everyone = range(count)
    for m in range(slices):
        trans[own ^ m] = t_refs[m][...]
    kern = (kern_ref[0], kern_ref[1])
    psi = [(probe_ref[0], probe_ref[1])] * count
    for k in range(slices):
        field = [cmul((trans[k, p, 0].astype(f32), trans[k, p, 1].astype(f32)), psi[p]) for p in everyone]
        psi = transform(field, 1, tables, True)
        if k < slices - 1:
            psi = transform([cmul(kern, s) for s in psi], 0, tables, True)
        for p in everyone:
            waves[k, p, 0] = psi[p][0]
            waves[k, p, 1] = psi[p][1]


def backward_kernel(members, clusters, probe_ref, kern_ref, code_ref, trans, waves, *rest):
    tables, meas_refs = rest[:2], rest[2 : 2 + clusters]
    out_refs, (terms, meas) = rest[2 + clusters : -2], rest[-2:]
    slices, count, _, window, _ = trans.shape
    own, cluster = lax.axis_index("depth"), lax.div(lax.axis_index("dp"), members)
    everyone = range(count)
    for m, meas_ref in enumerate(meas_refs):

        @pl.when(lax.div(own, 2) ^ cluster == m)
        def _():
            meas[...] = meas_ref[...]

    kern = (kern_ref[0], kern_ref[1])

    def source(p):
        re, im = waves[slices - 1, p, 0], waves[slices - 1, p, 1]
        scale = 2.0 * (re * re + im * im - meas[p])
        return scale * re, scale * im

    returned = transform([source(p) for p in everyone], 0, tables, False)
    for k in reversed(range(slices)):
        for p in everyone:
            wave = (waves[k - 1, p, 0], waves[k - 1, p, 1]) if k else (probe_ref[0], probe_ref[1])
            re, im = cmul_conj(wave, returned[p])
            terms[own ^ k, p, :window] = (re * grad_scale).astype(bf16)
            terms[own ^ k, p, window:] = (im * grad_scale).astype(bf16)
        if k > 0:
            chi = [
                cmul_conj((trans[k, p, 0].astype(f32), trans[k, p, 1].astype(f32)), returned[p])
                for p in everyone
            ]
            chi = transform(chi, 1, tables, False)
            returned = transform([cmul_conj(kern, c) for c in chi], 0, tables, False)
    for n, out_ref in enumerate(out_refs):
        out_ref[:, : 2 * window] = terms[2 * n]
        out_ref[:, 2 * window :] = code_ref[...]


def run_forward(probe, kern, tables, windows):
    slices, shape = len(windows), windows[0].shape
    return pl.pallas_call(
        forward_kernel,
        out_shape=[
            jax.ShapeDtypeStruct((slices,) + shape, bf16),
            jax.ShapeDtypeStruct((slices,) + shape, f32),
        ],
        in_specs=[vmem] * (4 + slices),
        out_specs=[vmem, vmem],
        compiler_params=limit,
        name="run_forward",
    )(probe, kern, *tables, *windows)


def run_backward(probe, kern, code, trans, waves, tables, measured, members):
    slices, count, _, window, _ = trans.shape
    block = jax.ShapeDtypeStruct((count, 2 * window + code_rows, window), bf16)
    return pl.pallas_call(
        functools.partial(backward_kernel, members, len(measured)),
        out_shape=[block] * (slices // 2),
        in_specs=[vmem] * (7 + len(measured)),
        out_specs=[vmem] * (slices // 2),
        scratch_shapes=[
            pltpu.VMEM((slices, count, 2 * window, window), bf16),
            pltpu.VMEM((count, window, window), f32),
        ],
        compiler_params=limit,
        name="run_backward",
    )(probe, kern, code, trans, waves, *tables, *measured)


def add_blocks(block_refs, canvas, stripe):
    count, _, window = block_refs[0].shape
    cols = canvas.shape[-1] - 128
    wide = window + 128
    first_row = lax.axis_index("dp") * stripe
    corners = []
    for block_ref in block_refs:
        for p in range(count):
            code = block_ref[p, 2 * window :].astype(f32)
            row = (8.0 * code[0:1] + code[1:2]).astype(jnp.int32)
            col = (8.0 * code[2:3] + code[3:4]).astype(jnp.int32)
            corners.append((row[0, 0], col[0, 0]))
    for n, (row, col) in enumerate(corners):
        block_ref, p = block_refs[n // count], n % count
        row = row - first_row + window
        row_base = pl.multiple_of((row >> 3) << 3, 8)
        col_base = pl.multiple_of((col >> 7) << 7, 128)

        @pl.when((row > 0) & (row < window + stripe))
        def _():
            for part in range(2):
                block = block_ref[p, part * window : (part + 1) * window].astype(f32)
                block = jnp.concatenate([block, jnp.zeros((8, window), f32)], axis=0)
                block = pltpu.roll(block, row - row_base, 0)
                block = jnp.concatenate([block, jnp.zeros((window + 8, 128), f32)], axis=1)
                block = pltpu.roll(block, col - col_base, 1)
                put = (part, pl.ds(row_base, window + 8), pl.ds(col_base, wide))
                canvas[put] = canvas[put] + block


def first_kernel(stripe, *refs):
    block_refs, canvas = refs[:-1], refs[-1]
    window = block_refs[0].shape[-1]
    canvas[:, window : window + stripe, :] = jnp.zeros((2, stripe, canvas.shape[2]), f32)
    add_blocks(block_refs, canvas, stripe)


def second_kernel(start_ref, *refs):
    block_refs, (out_ref, canvas) = refs[:-2], refs[-2:]
    _, stripe, cols = out_ref.shape
    window = block_refs[0].shape[-1]
    canvas[:, window : window + stripe, :] = start_ref[:, window : window + stripe, :]
    add_blocks(block_refs, canvas, stripe)
    out_ref[...] = canvas[:, window : window + stripe, :cols]


def place_windows(near, far, stripe, cols):
    window = near[0].shape[-1]
    vmem = pl.BlockSpec(memory_space=pltpu.VMEM)
    tall = window + (stripe + 7) // 8 * 8 + window + 8
    canvas = (2, tall, cols + 128)
    limit = pltpu.CompilerParams(vmem_limit_bytes=24 * 1024 * 1024)
    start = pl.pallas_call(
        functools.partial(first_kernel, stripe),
        out_shape=jax.ShapeDtypeStruct(canvas, f32),
        in_specs=[vmem] * len(near),
        out_specs=vmem,
        compiler_params=limit,
        name="place_near",
    )(*near)
    return pl.pallas_call(
        second_kernel,
        out_shape=jax.ShapeDtypeStruct((2, stripe, cols), f32),
        in_specs=[vmem] * (1 + len(far)),
        out_specs=vmem,
        scratch_shapes=[pltpu.VMEM(canvas, f32)],
        compiler_params=limit,
        name="place_far",
    )(start, *far)


def swap(block, depth_distance, dp_distance):
    depth, dp = lax.axis_size("depth"), lax.axis_size("dp")
    route = [
        (d * dp + j, (d ^ depth_distance) * dp + (j ^ dp_distance))
        for d in range(depth)
        for j in range(dp)
    ]
    return lax.ppermute(block, ("depth", "dp"), route)


def on_device(object_slices, positions, probe_field, propagator_phase, measured):
    depth, dp = lax.axis_size("depth"), lax.axis_size("dp")
    clusters = depth // 2
    members = dp // clusters
    rows, cols = object_slices.shape[-2:]
    window = probe_field.shape[-1]

    homes = [m * members for m in range(1, clusters)]
    all_positions = [positions] + [swap(positions, 0, home) for home in homes]
    windows, code = take_windows(fetch(object_slices[0]), all_positions, window, members)
    phase, code = lax.optimization_barrier((propagator_phase, code))
    arrivals = [swap(windows[m // 2], m, 0) for m in reversed(range(1, depth))]
    windows = [windows[0]] + arrivals[::-1]
    kern = jnp.stack([jnp.cos(phase), jnp.sin(phase)])
    kern, late = lax.optimization_barrier((kern, measured))
    targets = [measured] + [swap(late, 0, home) for home in homes]
    tables = dft_matrices(window)
    trans, waves = run_forward(probe_field, kern, tables, windows)
    terms = run_backward(probe_field, kern, code, trans, waves, tables, targets, members)

    blocks = [
        swap(terms[m // 2], m, plane) if m or plane else terms[0]
        for plane in reversed(range(0, members, 2))
        for m in reversed(range(0, depth, 2))
    ]
    return place_windows(blocks, [swap(block, 0, 1) for block in blocks], rows // dp, cols)[None]


def solution(mesh):
    placed = (P("depth", None, None, None), P("dp", None), P(), P(), P("dp", None, None))
    return jax.shard_map(
        on_device,
        mesh=mesh,
        in_specs=placed,
        out_specs=P("depth", None, "dp", None),
        check_vma=False,
    )
```

```python
import functools
import math

import jax
import jax.numpy as jnp
import numpy as np
from jax import lax
from jax.experimental import pallas as pl
from jax.experimental.pallas import tpu as pltpu
from jax.sharding import PartitionSpec as P

grad_scale = 0.03125
f32 = jnp.float32
bf16 = jnp.bfloat16


def dft_matrices(size):
    k = np.arange(size)
    angles = 2.0 * np.pi * ((k[:, None] * k[None, :]) % size) / size
    c = np.cos(angles) / math.sqrt(size)
    s = np.sin(angles) / math.sqrt(size)
    plus = np.block([[c, s], [-s, c]]).astype(np.float32)
    minus = np.block([[c, -s], [s, c]]).astype(np.float32)
    parts = []
    for full in (plus, minus):
        high = full.astype(bf16)
        low = (full - high.astype(np.float32)).astype(bf16)
        parts.append((high, low))
    (ph, plo), (mh, mlo) = parts
    return jnp.asarray(np.stack([np.concatenate([ph, plo]), np.concatenate([mh, mlo])]))


code_rows = 16


def fetch_kernel(obj_ref, out_ref, sem):
    copy = pltpu.make_async_copy(obj_ref, out_ref, sem)
    copy.start()
    copy.wait()


def fetch(obj):
    size = 4 * math.prod(obj.shape)
    return pl.pallas_call(
        fetch_kernel,
        out_shape=jax.ShapeDtypeStruct(obj.shape, obj.dtype),
        in_specs=[pl.BlockSpec(memory_space=pltpu.HBM)],
        out_specs=pl.BlockSpec(memory_space=pltpu.VMEM),
        scratch_shapes=[pltpu.SemaphoreType.DMA],
        compiler_params=pltpu.CompilerParams(vmem_limit_bytes=16 * 1024 * 1024),
        cost_estimate=pl.CostEstimate(flops=0, bytes_accessed=2 * size, transcendentals=0),
        name="fetch_slice",
    )(obj)


def window_kernel(members, obj_ref, *rest):
    table, table_sems = rest[-2:]
    clusters, count = table.shape[:2]
    pos_refs, out_refs, code_ref = rest[:clusters], rest[clusters:-3], rest[-3]
    window = out_refs[0].shape[-1]
    rows, cols = obj_ref.shape[-2:]
    tall, wide = window + 8, window + 128
    cluster = lax.div(lax.axis_index("dp"), members)
    home = lax.div(lax.axis_index("depth"), 2)

    fetches = [
        pltpu.make_async_copy(pos_refs[m], table.at[m], table_sems.at[m])
        for m in range(1, clusters)
    ]
    for fetch in fetches:
        fetch.start()
    for p in range(count):
        for axis in range(2):
            table[0, p, axis] = pos_refs[0][p, axis]
    for fetch in fetches:
        fetch.wait()

    def corner(m, p):
        at = home ^ cluster ^ m
        row, col = table[at, p, 0], table[at, p, 1]
        row_base = pl.multiple_of(jnp.minimum(row >> 3, (rows - tall) // 8) * 8, 8)
        col_base = pl.multiple_of(jnp.minimum(col >> 7, (cols - wide) // 128) * 128, 128)
        return row_base, col_base, row - row_base, col - col_base

    line = lax.broadcasted_iota(jnp.int32, (code_rows, window), 0)
    for p in range(count):
        row, col = table[home ^ cluster, p, 0], table[home ^ cluster, p, 1]
        code = jnp.where(line == 0, row >> 3, jnp.where(line == 1, row & 7, 0))
        code = jnp.where(line == 2, col >> 3, jnp.where(line == 3, col & 7, code))
        code_ref[p] = code.astype(f32).astype(bf16)
    for m in reversed(range(clusters)):
        for p in range(count):
            row_base, col_base, row_off, col_off = corner(m, p)
            lift = jnp.where(row_off == 0, 0, tall - row_off)
            shift = jnp.where(col_off == 0, 0, wide - col_off)
            for part in range(2):
                block = obj_ref[part, pl.ds(row_base, tall), pl.ds(col_base, wide)]
                block = pltpu.roll(block, shift, 1)[:, :window]
                block = pltpu.roll(block, lift, 0)[:window]
                out_refs[m][p, part] = block.astype(bf16)


def take_windows(obj, positions, window, members):
    clusters, count = len(positions), positions[0].shape[0]
    any_space = pl.BlockSpec(memory_space=pl.ANY)
    smem = pl.BlockSpec(memory_space=pltpu.SMEM)
    vmem = pl.BlockSpec(memory_space=pltpu.VMEM)
    out = pl.pallas_call(
        functools.partial(window_kernel, members),
        out_shape=[jax.ShapeDtypeStruct((count, 2, window, window), bf16)] * clusters
        + [jax.ShapeDtypeStruct((count, code_rows, window), bf16)],
        in_specs=[vmem, smem] + [any_space] * (clusters - 1),
        out_specs=[vmem] * (clusters + 1),
        scratch_shapes=[
            pltpu.SMEM((clusters, count, 2), jnp.int32),
            pltpu.SemaphoreType.DMA((clusters,)),
        ],
        compiler_params=pltpu.CompilerParams(vmem_limit_bytes=16 * 1024 * 1024),
        name="take_windows",
    )(obj, *positions)
    return out[:clusters], out[clusters]


def split(x):
    high = x.astype(bf16)
    return high, (x - high.astype(f32)).astype(bf16)


def cmul(a, b):
    return a[0] * b[0] - a[1] * b[1], a[0] * b[1] + a[1] * b[0]


def cmul_conj(a, b):
    return a[0] * b[0] + a[1] * b[1], a[0] * b[1] - a[1] * b[0]


def wave_kernel(members, clusters, probe_ref, kern_ref, tables_ref, code_ref, *rest):
    trans, terms, meas = rest[-3:]
    slices, count, _, _, window = trans.shape
    meas_refs, t_refs, out_refs = rest[:clusters], rest[clusters : clusters + slices], rest[clusters + slices : -3]
    own, cluster = lax.axis_index("depth"), lax.div(lax.axis_index("dp"), members)
    everyone = range(count)

    for m in range(slices):
        trans[own ^ m] = t_refs[m][...]
    for m, meas_ref in enumerate(meas_refs):

        @pl.when(lax.div(own, 2) ^ cluster == m)
        def _():
            meas[...] = meas_ref[...]

    def t_of(k, p):
        return trans[k, p, 0].astype(f32), trans[k, p, 1].astype(f32)

    def dot(a, b):
        return jnp.dot(a, b, preferred_element_type=f32)

    def rows(fields, sign, exact):
        x = jnp.concatenate([jnp.concatenate(f, axis=0) for f in fields], axis=1)
        table_ref = tables_ref.at[1 - sign]
        if exact:
            high, low = split(x)
            y = dot(table_ref[...], high)
            y = y[: 2 * window] + y[2 * window :] + dot(table_ref[: 2 * window], low)
        else:
            y = dot(table_ref[: 2 * window], x.astype(bf16))
        cut = [y[:, p * window : (p + 1) * window] for p in everyone]
        return [(c[:window], c[window:]) for c in cut]

    def cols(fields, sign, exact):
        x = jnp.concatenate([jnp.concatenate(f, axis=1) for f in fields], axis=0)
        table_ref = tables_ref.at[sign]
        if exact:
            high, low = split(x)
            y = dot(jnp.concatenate([high, low], axis=0), table_ref[: 2 * window])
            y = y[: count * window] + y[count * window :] + dot(high, table_ref[2 * window :])
        else:
            y = dot(x.astype(bf16), table_ref[: 2 * window])
        cut = [y[p * window : (p + 1) * window] for p in everyone]
        return [(c[:, :window], c[:, window:]) for c in cut]

    plus, minus = 0, 1

    def transform(fields, sign, exact):
        return cols(rows(fields, sign, exact), sign, exact)

    kern = (kern_ref[0], kern_ref[1])
    psi = [(probe_ref[0], probe_ref[1])] * count
    kept = []
    for k in range(slices):
        kept.append(psi)
        spectrum = transform([cmul(t_of(k, p), psi[p]) for p in everyone], minus, True)
        if k < slices - 1:
            psi = transform([cmul(kern, s) for s in spectrum], plus, True)

    def source(p):
        re, im = spectrum[p]
        scale = 2.0 * (re * re + im * im - meas[p])
        return scale * re, scale * im

    returned = transform([source(p) for p in everyone], plus, False)
    for k in reversed(range(slices)):
        for p in everyone:
            re, im = cmul_conj(kept[k][p], returned[p])
            terms[own ^ k, p, :window] = (re * grad_scale).astype(bf16)
            terms[own ^ k, p, window:] = (im * grad_scale).astype(bf16)
        if k > 0:
            chi = [cmul_conj(t_of(k, p), returned[p]) for p in everyone]
            spectrum = transform(chi, minus, False)
            returned = transform([cmul_conj(kern, s) for s in spectrum], plus, False)
    for n, out_ref in enumerate(out_refs):
        out_ref[:, : 2 * window] = terms[2 * n]
        out_ref[:, 2 * window :] = code_ref[...]


def run_waves(probe, kern, code, measured, windows, members):
    slices, count, window = len(windows), code.shape[0], code.shape[-1]
    vmem = pl.BlockSpec(memory_space=pltpu.VMEM)
    block = jax.ShapeDtypeStruct((count, 2 * window + code_rows, window), bf16)
    return pl.pallas_call(
        functools.partial(wave_kernel, members, len(measured)),
        out_shape=[block] * (slices // 2),
        in_specs=[vmem] * (4 + len(measured) + slices),
        out_specs=[vmem] * (slices // 2),
        scratch_shapes=[
            pltpu.VMEM((slices, count, 2, window, window), bf16),
            pltpu.VMEM((slices, count, 2 * window, window), bf16),
            pltpu.VMEM((count, window, window), f32),
        ],
        compiler_params=pltpu.CompilerParams(vmem_limit_bytes=40 * 1024 * 1024),
        name="run_waves",
    )(probe, kern, dft_matrices(window), code, *measured, *windows)


def add_blocks(block_refs, canvas, stripe):
    count, _, window = block_refs[0].shape
    cols = canvas.shape[-1] - 128
    wide = window + 128
    first_row = lax.axis_index("dp") * stripe
    corners = []
    for block_ref in block_refs:
        for p in range(count):
            code = block_ref[p, 2 * window :].astype(f32)
            row = (8.0 * code[0:1] + code[1:2]).astype(jnp.int32)
            col = (8.0 * code[2:3] + code[3:4]).astype(jnp.int32)
            corners.append((row[0, 0], col[0, 0]))
    for n, (row, col) in enumerate(corners):
        block_ref, p = block_refs[n // count], n % count
        row = row - first_row + window
        row_base = pl.multiple_of((row >> 3) << 3, 8)
        col_base = pl.multiple_of((col >> 7) << 7, 128)

        @pl.when((row > 0) & (row < window + stripe))
        def _():
            for part in range(2):
                block = block_ref[p, part * window : (part + 1) * window].astype(f32)
                block = jnp.concatenate([block, jnp.zeros((8, window), f32)], axis=0)
                block = pltpu.roll(block, row - row_base, 0)
                block = jnp.concatenate([block, jnp.zeros((window + 8, 128), f32)], axis=1)
                block = pltpu.roll(block, col - col_base, 1)
                put = (part, pl.ds(row_base, window + 8), pl.ds(col_base, wide))
                canvas[put] = canvas[put] + block


def first_kernel(stripe, *refs):
    block_refs, canvas = refs[:-1], refs[-1]
    window = block_refs[0].shape[-1]
    canvas[:, window : window + stripe, :] = jnp.zeros((2, stripe, canvas.shape[2]), f32)
    add_blocks(block_refs, canvas, stripe)


def second_kernel(start_ref, *refs):
    block_refs, (out_ref, canvas) = refs[:-2], refs[-2:]
    _, stripe, cols = out_ref.shape
    window = block_refs[0].shape[-1]
    canvas[:, window : window + stripe, :] = start_ref[:, window : window + stripe, :]
    add_blocks(block_refs, canvas, stripe)
    out_ref[...] = canvas[:, window : window + stripe, :cols]


def place_windows(near, far, stripe, cols):
    window = near[0].shape[-1]
    vmem = pl.BlockSpec(memory_space=pltpu.VMEM)
    tall = window + (stripe + 7) // 8 * 8 + window + 8
    canvas = (2, tall, cols + 128)
    limit = pltpu.CompilerParams(vmem_limit_bytes=24 * 1024 * 1024)
    start = pl.pallas_call(
        functools.partial(first_kernel, stripe),
        out_shape=jax.ShapeDtypeStruct(canvas, f32),
        in_specs=[vmem] * len(near),
        out_specs=vmem,
        compiler_params=limit,
        name="place_near",
    )(*near)
    return pl.pallas_call(
        second_kernel,
        out_shape=jax.ShapeDtypeStruct((2, stripe, cols), f32),
        in_specs=[vmem] * (1 + len(far)),
        out_specs=vmem,
        scratch_shapes=[pltpu.VMEM(canvas, f32)],
        compiler_params=limit,
        name="place_far",
    )(start, *far)


def swap(block, depth_distance, dp_distance):
    depth, dp = lax.axis_size("depth"), lax.axis_size("dp")
    route = [
        (d * dp + j, (d ^ depth_distance) * dp + (j ^ dp_distance))
        for d in range(depth)
        for j in range(dp)
    ]
    return lax.ppermute(block, ("depth", "dp"), route)


def on_device(object_slices, positions, probe_field, propagator_phase, measured):
    depth, dp = lax.axis_size("depth"), lax.axis_size("dp")
    clusters = depth // 2
    members = dp // clusters
    rows, cols = object_slices.shape[-2:]
    window = probe_field.shape[-1]

    homes = [m * members for m in range(1, clusters)]
    all_positions = [positions] + [swap(positions, 0, home) for home in homes]
    windows, code = take_windows(fetch(object_slices[0]), all_positions, window, members)
    phase, code = lax.optimization_barrier((propagator_phase, code))
    windows = [windows[0]] + [swap(windows[m // 2], m, 0) for m in range(1, depth)]
    targets = [measured] + [swap(measured, 0, home) for home in homes]
    kern = jnp.stack([jnp.cos(phase), jnp.sin(phase)])
    terms = run_waves(probe_field, kern, code, targets, windows, members)

    blocks = [
        swap(terms[m // 2], m, plane) if m or plane else terms[0]
        for plane in range(0, members, 2)
        for m in range(0, depth, 2)
    ]
    return place_windows(blocks, [swap(block, 0, 1) for block in blocks], rows // dp, cols)[None]


def solution(mesh):
    placed = (P("depth", None, None, None), P("dp", None), P(), P(), P("dp", None, None))
    return jax.shard_map(
        on_device,
        mesh=mesh,
        in_specs=placed,
        out_specs=P("depth", None, "dp", None),
        check_vma=False,
    )
```

```python
import functools
import math

import jax
import jax.numpy as jnp
import numpy as np
from jax import lax
from jax.experimental import pallas as pl
from jax.experimental.pallas import tpu as pltpu
from jax.sharding import PartitionSpec as P

grad_scale = 0.03125
f32 = jnp.float32
bf16 = jnp.bfloat16


def dft_matrices(size):
    k = np.arange(size)
    angles = 2.0 * np.pi * ((k[:, None] * k[None, :]) % size) / size
    c = np.cos(angles) / math.sqrt(size)
    s = np.sin(angles) / math.sqrt(size)
    plus = np.block([[c, s], [-s, c]]).astype(np.float32)
    minus = np.block([[c, -s], [s, c]]).astype(np.float32)
    parts = []
    for full in (plus, minus):
        high = full.astype(bf16)
        low = (full - high.astype(np.float32)).astype(bf16)
        parts.append((high, low))
    (ph, plo), (mh, mlo) = parts
    right = np.stack([np.concatenate([ph, ph, plo], 0), np.concatenate([mh, mh, mlo], 0)])
    left = np.stack([np.concatenate([mh, mh, mlo], 1), np.concatenate([ph, ph, plo], 1)])
    return left, right


code_rows = 16


def touch_kernel(obj_ref, out_ref):
    out_ref[...] = obj_ref[0, :8, :128]


def touch(obj):
    vmem = pl.BlockSpec(memory_space=pltpu.VMEM)
    return pl.pallas_call(
        touch_kernel,
        out_shape=jax.ShapeDtypeStruct((8, 128), obj.dtype),
        in_specs=[vmem],
        out_specs=vmem,
        compiler_params=pltpu.CompilerParams(vmem_limit_bytes=16 * 1024 * 1024),
        cost_estimate=pl.CostEstimate(
            flops=0, bytes_accessed=4 * math.prod(obj.shape), transcendentals=0
        ),
        name="touch_slice",
    )(obj)


def window_kernel(members, obj_ref, touched_ref, *rest):
    del touched_ref
    table, table_sems = rest[-2:]
    clusters, count = table.shape[:2]
    pos_refs, out_refs, code_ref = rest[:clusters], rest[clusters:-3], rest[-3]
    window = out_refs[0].shape[-1]
    rows, cols = obj_ref.shape[-2:]
    tall, wide = window + 8, window + 128
    cluster = lax.div(lax.axis_index("dp"), members)
    home = lax.div(lax.axis_index("depth"), 2)

    fetches = [
        pltpu.make_async_copy(pos_refs[m], table.at[m], table_sems.at[m])
        for m in range(1, clusters)
    ]
    for fetch in fetches:
        fetch.start()
    for p in range(count):
        for axis in range(2):
            table[0, p, axis] = pos_refs[0][p, axis]
    for fetch in fetches:
        fetch.wait()

    def corner(m, p):
        at = home ^ cluster ^ m
        row, col = table[at, p, 0], table[at, p, 1]
        row_base = pl.multiple_of(jnp.minimum(row >> 3, (rows - tall) // 8) * 8, 8)
        col_base = pl.multiple_of(jnp.minimum(col >> 7, (cols - wide) // 128) * 128, 128)
        return row_base, col_base, row - row_base, col - col_base

    line = lax.broadcasted_iota(jnp.int32, (code_rows, window), 0)
    code = jnp.zeros((code_rows, window), jnp.int32)
    for p in range(count):
        row, col = table[home ^ cluster, p, 0], table[home ^ cluster, p, 1]
        for n, value in enumerate((row >> 3, row & 7, col >> 3, col & 7)):
            code = jnp.where(line == 4 * p + n, value, code)
    code_ref[...] = code.astype(f32).astype(bf16)
    for m in reversed(range(clusters)):
        for p in range(count):
            row_base, col_base, row_off, col_off = corner(m, p)
            lift = jnp.where(row_off == 0, 0, tall - row_off)
            shift = jnp.where(col_off == 0, 0, wide - col_off)
            for part in range(2):
                block = obj_ref[part, pl.ds(row_base, tall), pl.ds(col_base, wide)]
                block = pltpu.roll(block, shift, 1)[:, :window]
                block = pltpu.roll(block, lift, 0)[:window]
                out_refs[m][p, part] = block.astype(bf16)


def take_windows(obj, touched, positions, window, members):
    clusters, count = len(positions), positions[0].shape[0]
    any_space = pl.BlockSpec(memory_space=pl.ANY)
    smem = pl.BlockSpec(memory_space=pltpu.SMEM)
    vmem = pl.BlockSpec(memory_space=pltpu.VMEM)
    out = pl.pallas_call(
        functools.partial(window_kernel, members),
        out_shape=[jax.ShapeDtypeStruct((count, 2, window, window), bf16)] * clusters
        + [jax.ShapeDtypeStruct((code_rows, window), bf16)],
        in_specs=[vmem, vmem, smem] + [any_space] * (clusters - 1),
        out_specs=[vmem] * (clusters + 1),
        scratch_shapes=[
            pltpu.SMEM((clusters, count, 2), jnp.int32),
            pltpu.SemaphoreType.DMA((clusters,)),
        ],
        compiler_params=pltpu.CompilerParams(vmem_limit_bytes=16 * 1024 * 1024),
        name="take_windows",
    )(obj, touched, *positions)
    return out[:clusters], out[clusters]


def split(x):
    high = x.astype(bf16)
    return high, (x - high.astype(f32)).astype(bf16)


def cmul(a, b):
    return a[0] * b[0] - a[1] * b[1], a[0] * b[1] + a[1] * b[0]


def cmul_conj(a, b):
    return a[0] * b[0] + a[1] * b[1], a[0] * b[1] - a[1] * b[0]


def wave_kernel(members, clusters, probe_ref, kern_ref, left_ref, right_ref, code_ref, *rest):
    trans, terms, meas = rest[-3:]
    slices, count, _, _, window = trans.shape
    meas_refs, t_refs, out_refs = rest[:clusters], rest[clusters : clusters + slices], rest[clusters + slices : -3]
    own, cluster = lax.axis_index("depth"), lax.div(lax.axis_index("dp"), members)
    everyone = range(count)

    for m in range(slices):
        trans[own ^ m] = t_refs[m][...]
    for m, meas_ref in enumerate(meas_refs):

        @pl.when(lax.div(own, 2) ^ cluster == m)
        def _():
            meas[...] = meas_ref[...]

    def t_of(k, p):
        return trans[k, p, 0].astype(f32), trans[k, p, 1].astype(f32)

    def passes(x, axis, exact):
        if not exact:
            return x.astype(bf16)
        high, low = split(x)
        return jnp.concatenate([high, low, high], axis=axis)

    def rows(fields, sign, exact):
        x = jnp.concatenate([jnp.concatenate(f, axis=0) for f in fields], axis=1)
        x = passes(x, 0, exact)
        y = jnp.dot(left_ref[sign, :, : x.shape[0]], x, preferred_element_type=f32)
        cut = [y[:, p * window : (p + 1) * window] for p in everyone]
        return [(c[:window], c[window:]) for c in cut]

    def cols(fields, sign, exact):
        x = jnp.concatenate([jnp.concatenate(f, axis=1) for f in fields], axis=0)
        x = passes(x, 1, exact)
        y = jnp.dot(x, right_ref[sign, : x.shape[1]], preferred_element_type=f32)
        cut = [y[p * window : (p + 1) * window] for p in everyone]
        return [(c[:, :window], c[:, window:]) for c in cut]

    plus, minus = 0, 1

    def transform(fields, sign, exact):
        return cols(rows(fields, sign, exact), sign, exact)

    kern = (kern_ref[0], kern_ref[1])
    psi = [(probe_ref[0], probe_ref[1])] * count
    kept = []
    for k in range(slices):
        kept.append(psi)
        spectrum = transform([cmul(t_of(k, p), psi[p]) for p in everyone], minus, True)
        if k < slices - 1:
            psi = transform([cmul(kern, s) for s in spectrum], plus, True)

    def source(p):
        re, im = spectrum[p]
        scale = 2.0 * (re * re + im * im - meas[p])
        return scale * re, scale * im

    returned = transform([source(p) for p in everyone], plus, False)
    for k in reversed(range(slices)):
        for p in everyone:
            re, im = cmul_conj(kept[k][p], returned[p])
            terms[own ^ k, p, :window] = (re * grad_scale).astype(bf16)
            terms[own ^ k, p, window:] = (im * grad_scale).astype(bf16)
        if k > 0:
            chi = [cmul_conj(t_of(k, p), returned[p]) for p in everyone]
            spectrum = transform(chi, minus, False)
            returned = transform([cmul_conj(kern, s) for s in spectrum], plus, False)
    for n, out_ref in enumerate(out_refs):
        for p in everyone:
            out_ref[2 * p * window : 2 * (p + 1) * window] = terms[2 * n, p]
        out_ref[2 * count * window :] = code_ref[...]


def run_waves(probe, kern, code, measured, windows, members):
    slices, (count, _, _, window) = len(windows), windows[0].shape
    left, right = dft_matrices(window)
    vmem = pl.BlockSpec(memory_space=pltpu.VMEM)
    block = jax.ShapeDtypeStruct((2 * count * window + code_rows, window), bf16)
    return pl.pallas_call(
        functools.partial(wave_kernel, members, len(measured)),
        out_shape=[block] * (slices // 2),
        in_specs=[vmem] * (5 + len(measured) + slices),
        out_specs=[vmem] * (slices // 2),
        scratch_shapes=[
            pltpu.VMEM((slices, count, 2, window, window), bf16),
            pltpu.VMEM((slices, count, 2 * window, window), bf16),
            pltpu.VMEM((count, window, window), f32),
        ],
        compiler_params=pltpu.CompilerParams(vmem_limit_bytes=40 * 1024 * 1024),
        name="run_waves",
    )(probe, kern, jnp.asarray(left), jnp.asarray(right), code, *measured, *windows)


def add_blocks(block_refs, canvas, stripe):
    height, window = block_refs[0].shape
    count = (height - code_rows) // (2 * window)
    cols = canvas.shape[-1] - 128
    wide = window + 128
    first_row = lax.axis_index("dp") * stripe
    corners = []
    for block_ref in block_refs:
        code = block_ref[2 * count * window :].astype(f32)
        for p in range(count):
            row = (8.0 * code[4 * p : 4 * p + 1] + code[4 * p + 1 : 4 * p + 2]).astype(jnp.int32)
            col = (8.0 * code[4 * p + 2 : 4 * p + 3] + code[4 * p + 3 : 4 * p + 4]).astype(jnp.int32)
            corners.append((row[0, 0], col[0, 0]))
    for n, (row, col) in enumerate(corners):
        block_ref, p = block_refs[n // count], n % count
        row = row - first_row + window
        row_base = pl.multiple_of((row >> 3) << 3, 8)
        col_base = pl.multiple_of((col >> 7) << 7, 128)

        @pl.when((row > 0) & (row < window + stripe))
        def _():
            for part in range(2):
                block = block_ref[(2 * p + part) * window : (2 * p + part + 1) * window].astype(f32)
                block = jnp.concatenate([block, jnp.zeros((8, window), f32)], axis=0)
                block = pltpu.roll(block, row - row_base, 0)
                block = jnp.concatenate([block, jnp.zeros((window + 8, 128), f32)], axis=1)
                block = pltpu.roll(block, col - col_base, 1)
                put = (part, pl.ds(row_base, window + 8), pl.ds(col_base, wide))
                canvas[put] = canvas[put] + block


def first_kernel(stripe, *refs):
    block_refs, canvas = refs[:-1], refs[-1]
    window = block_refs[0].shape[-1]
    canvas[:, window : window + stripe, :] = jnp.zeros((2, stripe, canvas.shape[2]), f32)
    add_blocks(block_refs, canvas, stripe)


def second_kernel(start_ref, *refs):
    block_refs, (out_ref, canvas) = refs[:-2], refs[-2:]
    _, stripe, cols = out_ref.shape
    window = block_refs[0].shape[-1]
    canvas[:, window : window + stripe, :] = start_ref[:, window : window + stripe, :]
    add_blocks(block_refs, canvas, stripe)
    out_ref[...] = canvas[:, window : window + stripe, :cols]


def place_windows(near, far, stripe, cols):
    window = near[0].shape[-1]
    vmem = pl.BlockSpec(memory_space=pltpu.VMEM)
    tall = window + (stripe + 7) // 8 * 8 + window + 8
    canvas = (2, tall, cols + 128)
    limit = pltpu.CompilerParams(vmem_limit_bytes=24 * 1024 * 1024)
    start = pl.pallas_call(
        functools.partial(first_kernel, stripe),
        out_shape=jax.ShapeDtypeStruct(canvas, f32),
        in_specs=[vmem] * len(near),
        out_specs=vmem,
        compiler_params=limit,
        name="place_near",
    )(*near)
    return pl.pallas_call(
        second_kernel,
        out_shape=jax.ShapeDtypeStruct((2, stripe, cols), f32),
        in_specs=[vmem] * (1 + len(far)),
        out_specs=vmem,
        scratch_shapes=[pltpu.VMEM(canvas, f32)],
        compiler_params=limit,
        name="place_far",
    )(start, *far)


def swap(block, depth_distance, dp_distance):
    depth, dp = lax.axis_size("depth"), lax.axis_size("dp")
    route = [
        (d * dp + j, (d ^ depth_distance) * dp + (j ^ dp_distance))
        for d in range(depth)
        for j in range(dp)
    ]
    return lax.ppermute(block, ("depth", "dp"), route)


def on_device(object_slices, positions, probe_field, propagator_phase, measured):
    depth, dp = lax.axis_size("depth"), lax.axis_size("dp")
    clusters = depth // 2
    members = dp // clusters
    rows, cols = object_slices.shape[-2:]
    window = probe_field.shape[-1]

    homes = [m * members for m in range(1, clusters)]
    all_positions = [positions] + [swap(positions, 0, home) for home in homes]
    obj = object_slices[0]
    windows, code = take_windows(obj, touch(obj), all_positions, window, members)
    phase, code = lax.optimization_barrier((propagator_phase, code))
    windows = [windows[0]] + [swap(windows[m // 2], m, 0) for m in range(1, depth)]
    targets = [measured] + [swap(measured, 0, home) for home in homes]
    kern = jnp.stack([jnp.cos(phase), jnp.sin(phase)])
    terms = run_waves(probe_field, kern, code, targets, windows, members)

    blocks = [
        swap(terms[m // 2], m, plane) if m or plane else terms[0]
        for plane in range(0, members, 2)
        for m in range(0, depth, 2)
    ]
    return place_windows(blocks, [swap(block, 0, 1) for block in blocks], rows // dp, cols)[None]


def solution(mesh):
    placed = (P("depth", None, None, None), P("dp", None), P(), P(), P("dp", None, None))
    return jax.shard_map(
        on_device,
        mesh=mesh,
        in_specs=placed,
        out_specs=P("depth", None, "dp", None),
        check_vma=False,
    )
```

```python
import functools
import math

import jax
import jax.numpy as jnp
import numpy as np
from jax import lax
from jax.experimental import pallas as pl
from jax.experimental.pallas import tpu as pltpu
from jax.sharding import PartitionSpec as P

grad_scale = 0.03125
f32 = jnp.float32
bf16 = jnp.bfloat16


def dft_matrices(size):
    k = np.arange(size)
    angles = 2.0 * np.pi * ((k[:, None] * k[None, :]) % size) / size
    c = np.cos(angles) / math.sqrt(size)
    s = np.sin(angles) / math.sqrt(size)
    plus = np.block([[c, s], [-s, c]]).astype(np.float32)
    minus = np.block([[c, -s], [s, c]]).astype(np.float32)
    parts = []
    for full in (plus, minus):
        high = full.astype(bf16)
        low = (full - high.astype(np.float32)).astype(bf16)
        parts.append((high, low))
    (ph, plo), (mh, mlo) = parts
    right = np.stack([np.concatenate([ph, ph, plo], 0), np.concatenate([mh, mh, mlo], 0)])
    left = np.stack([np.concatenate([mh, mh, mlo], 1), np.concatenate([ph, ph, plo], 1)])
    return left, right


code_rows = 16


def touch_kernel(obj_ref, out_ref):
    out_ref[...] = obj_ref[0, :8, :128]


def touch(obj):
    vmem = pl.BlockSpec(memory_space=pltpu.VMEM)
    return pl.pallas_call(
        touch_kernel,
        out_shape=jax.ShapeDtypeStruct((8, 128), obj.dtype),
        in_specs=[vmem],
        out_specs=vmem,
        compiler_params=pltpu.CompilerParams(vmem_limit_bytes=16 * 1024 * 1024),
        cost_estimate=pl.CostEstimate(
            flops=0, bytes_accessed=4 * math.prod(obj.shape), transcendentals=0
        ),
        name="touch_slice",
    )(obj)


def window_kernel(members, obj_ref, touched_ref, *rest):
    del touched_ref
    table, cut, table_sems = rest[-3:]
    clusters, count = table.shape[:2]
    pos_refs, out_refs, code_ref = rest[:clusters], rest[clusters:-4], rest[-4]
    window = out_refs[0].shape[-1]
    rows, cols = obj_ref.shape[-2:]
    tall, wide = window + 8, window + 128
    cluster = lax.div(lax.axis_index("dp"), members)
    home = lax.div(lax.axis_index("depth"), 2)

    fetches = [
        pltpu.make_async_copy(pos_refs[m], table.at[m], table_sems.at[m])
        for m in range(1, clusters)
    ]
    for fetch in fetches:
        fetch.start()
    for p in range(count):
        for axis in range(2):
            table[0, p, axis] = pos_refs[0][p, axis]

    def take(a):
        for p in range(count):
            row, col = table[a, p, 0], table[a, p, 1]
            row_base = pl.multiple_of(jnp.minimum(row >> 3, (rows - tall) // 8) * 8, 8)
            col_base = pl.multiple_of(jnp.minimum(col >> 7, (cols - wide) // 128) * 128, 128)
            lift = jnp.where(row == row_base, 0, tall - (row - row_base))
            shift = jnp.where(col == col_base, 0, wide - (col - col_base))
            for part in range(2):
                block = obj_ref[part, pl.ds(row_base, tall), pl.ds(col_base, wide)]
                block = pltpu.roll(block, shift, 1)[:, :window]
                block = pltpu.roll(block, lift, 0)[:window]
                cut[home ^ cluster ^ a, p, part] = block.astype(bf16)

    take(0)
    for a in range(1, clusters):
        fetches[a - 1].wait()
        take(a)
    line = lax.broadcasted_iota(jnp.int32, (code_rows, window), 0)
    code = jnp.zeros((code_rows, window), jnp.int32)
    for p in range(count):
        row, col = table[home ^ cluster, p, 0], table[home ^ cluster, p, 1]
        for n, value in enumerate((row >> 3, row & 7, col >> 3, col & 7)):
            code = jnp.where(line == 4 * p + n, value, code)
    code_ref[...] = code.astype(f32).astype(bf16)
    for m, out_ref in enumerate(out_refs):
        out_ref[...] = cut[m]


def take_windows(obj, touched, positions, window, members):
    clusters, count = len(positions), positions[0].shape[0]
    any_space = pl.BlockSpec(memory_space=pl.ANY)
    smem = pl.BlockSpec(memory_space=pltpu.SMEM)
    vmem = pl.BlockSpec(memory_space=pltpu.VMEM)
    out = pl.pallas_call(
        functools.partial(window_kernel, members),
        out_shape=[jax.ShapeDtypeStruct((count, 2, window, window), bf16)] * clusters
        + [jax.ShapeDtypeStruct((code_rows, window), bf16)],
        in_specs=[vmem, vmem, smem] + [any_space] * (clusters - 1),
        out_specs=[vmem] * (clusters + 1),
        scratch_shapes=[
            pltpu.SMEM((clusters, count, 2), jnp.int32),
            pltpu.VMEM((clusters, count, 2, window, window), bf16),
            pltpu.SemaphoreType.DMA((clusters,)),
        ],
        compiler_params=pltpu.CompilerParams(vmem_limit_bytes=16 * 1024 * 1024),
        name="take_windows",
    )(obj, touched, *positions)
    return out[:clusters], out[clusters]


def split(x):
    high = x.astype(bf16)
    return high, (x - high.astype(f32)).astype(bf16)


def cmul(a, b):
    return a[0] * b[0] - a[1] * b[1], a[0] * b[1] + a[1] * b[0]


def cmul_conj(a, b):
    return a[0] * b[0] + a[1] * b[1], a[0] * b[1] - a[1] * b[0]


def wave_kernel(members, clusters, probe_ref, kern_ref, left_ref, right_ref, code_ref, *rest):
    trans, terms, meas = rest[-3:]
    slices, count, _, _, window = trans.shape
    meas_refs, t_refs, out_refs = rest[:clusters], rest[clusters : clusters + slices], rest[clusters + slices : -3]
    own, cluster = lax.axis_index("depth"), lax.div(lax.axis_index("dp"), members)
    everyone = range(count)

    for m in range(slices):
        trans[own ^ m] = t_refs[m][...]
    for m, meas_ref in enumerate(meas_refs):

        @pl.when(lax.div(own, 2) ^ cluster == m)
        def _():
            meas[...] = meas_ref[...]

    def t_of(k, p):
        return trans[k, p, 0].astype(f32), trans[k, p, 1].astype(f32)

    def passes(x, axis, exact):
        if not exact:
            return x.astype(bf16)
        high, low = split(x)
        return jnp.concatenate([high, low, high], axis=axis)

    def rows(fields, sign, exact):
        x = jnp.concatenate([jnp.concatenate(f, axis=0) for f in fields], axis=1)
        x = passes(x, 0, exact)
        y = jnp.dot(left_ref[sign, :, : x.shape[0]], x, preferred_element_type=f32)
        cut = [y[:, p * window : (p + 1) * window] for p in everyone]
        return [(c[:window], c[window:]) for c in cut]

    def cols(fields, sign, exact):
        x = jnp.concatenate([jnp.concatenate(f, axis=1) for f in fields], axis=0)
        x = passes(x, 1, exact)
        y = jnp.dot(x, right_ref[sign, : x.shape[1]], preferred_element_type=f32)
        cut = [y[p * window : (p + 1) * window] for p in everyone]
        return [(c[:, :window], c[:, window:]) for c in cut]

    plus, minus = 0, 1

    def transform(fields, sign, exact):
        return cols(rows(fields, sign, exact), sign, exact)

    kern = (kern_ref[0], kern_ref[1])
    psi = [(probe_ref[0], probe_ref[1])] * count
    kept = []
    for k in range(slices):
        kept.append(psi)
        spectrum = transform([cmul(t_of(k, p), psi[p]) for p in everyone], minus, True)
        if k < slices - 1:
            psi = transform([cmul(kern, s) for s in spectrum], plus, True)

    def source(p):
        re, im = spectrum[p]
        scale = 2.0 * (re * re + im * im - meas[p])
        return scale * re, scale * im

    returned = transform([source(p) for p in everyone], plus, False)
    for k in reversed(range(slices)):
        for p in everyone:
            re, im = cmul_conj(kept[k][p], returned[p])
            terms[own ^ k, p, :window] = (re * grad_scale).astype(bf16)
            terms[own ^ k, p, window:] = (im * grad_scale).astype(bf16)
        if k > 0:
            chi = [cmul_conj(t_of(k, p), returned[p]) for p in everyone]
            spectrum = transform(chi, minus, False)
            returned = transform([cmul_conj(kern, s) for s in spectrum], plus, False)
    for n, out_ref in enumerate(out_refs):
        for p in everyone:
            out_ref[2 * p * window : 2 * (p + 1) * window] = terms[2 * n, p]
        out_ref[2 * count * window :] = code_ref[...]


def run_waves(probe, kern, code, measured, windows, members):
    slices, (count, _, _, window) = len(windows), windows[0].shape
    left, right = dft_matrices(window)
    vmem = pl.BlockSpec(memory_space=pltpu.VMEM)
    block = jax.ShapeDtypeStruct((2 * count * window + code_rows, window), bf16)
    return pl.pallas_call(
        functools.partial(wave_kernel, members, len(measured)),
        out_shape=[block] * (slices // 2),
        in_specs=[vmem] * (5 + len(measured) + slices),
        out_specs=[vmem] * (slices // 2),
        scratch_shapes=[
            pltpu.VMEM((slices, count, 2, window, window), bf16),
            pltpu.VMEM((slices, count, 2 * window, window), bf16),
            pltpu.VMEM((count, window, window), f32),
        ],
        compiler_params=pltpu.CompilerParams(vmem_limit_bytes=40 * 1024 * 1024),
        name="run_waves",
    )(probe, kern, jnp.asarray(left), jnp.asarray(right), code, *measured, *windows)


def add_blocks(block_refs, canvas, stripe):
    height, window = block_refs[0].shape
    count = (height - code_rows) // (2 * window)
    cols = canvas.shape[-1] - 128
    wide = window + 128
    first_row = lax.axis_index("dp") * stripe
    corners = []
    for block_ref in block_refs:
        code = block_ref[2 * count * window :].astype(f32)
        for p in range(count):
            row = (8.0 * code[4 * p : 4 * p + 1] + code[4 * p + 1 : 4 * p + 2]).astype(jnp.int32)
            col = (8.0 * code[4 * p + 2 : 4 * p + 3] + code[4 * p + 3 : 4 * p + 4]).astype(jnp.int32)
            corners.append((row[0, 0], col[0, 0]))
    for n, (row, col) in enumerate(corners):
        block_ref, p = block_refs[n // count], n % count
        row = row - first_row + window
        row_base = pl.multiple_of((row >> 3) << 3, 8)
        col_base = pl.multiple_of((col >> 7) << 7, 128)

        @pl.when((row > 0) & (row < window + stripe))
        def _():
            for part in range(2):
                block = block_ref[(2 * p + part) * window : (2 * p + part + 1) * window].astype(f32)
                block = jnp.concatenate([block, jnp.zeros((8, window), f32)], axis=0)
                block = pltpu.roll(block, row - row_base, 0)
                block = jnp.concatenate([block, jnp.zeros((window + 8, 128), f32)], axis=1)
                block = pltpu.roll(block, col - col_base, 1)
                put = (part, pl.ds(row_base, window + 8), pl.ds(col_base, wide))
                canvas[put] = canvas[put] + block


def first_kernel(stripe, *refs):
    block_refs, canvas = refs[:-1], refs[-1]
    window = block_refs[0].shape[-1]
    canvas[:, window : window + stripe, :] = jnp.zeros((2, stripe, canvas.shape[2]), f32)
    add_blocks(block_refs, canvas, stripe)


def second_kernel(start_ref, *refs):
    block_refs, (out_ref, canvas) = refs[:-2], refs[-2:]
    _, stripe, cols = out_ref.shape
    window = block_refs[0].shape[-1]
    canvas[:, window : window + stripe, :] = start_ref[:, window : window + stripe, :]
    add_blocks(block_refs, canvas, stripe)
    out_ref[...] = canvas[:, window : window + stripe, :cols]


def place_windows(near, far, stripe, cols):
    window = near[0].shape[-1]
    vmem = pl.BlockSpec(memory_space=pltpu.VMEM)
    tall = window + (stripe + 7) // 8 * 8 + window + 8
    canvas = (2, tall, cols + 128)
    limit = pltpu.CompilerParams(vmem_limit_bytes=24 * 1024 * 1024)
    start = pl.pallas_call(
        functools.partial(first_kernel, stripe),
        out_shape=jax.ShapeDtypeStruct(canvas, f32),
        in_specs=[vmem] * len(near),
        out_specs=vmem,
        compiler_params=limit,
        name="place_near",
    )(*near)
    return pl.pallas_call(
        second_kernel,
        out_shape=jax.ShapeDtypeStruct((2, stripe, cols), f32),
        in_specs=[vmem] * (1 + len(far)),
        out_specs=vmem,
        scratch_shapes=[pltpu.VMEM(canvas, f32)],
        compiler_params=limit,
        name="place_far",
    )(start, *far)


def swap(block, depth_distance, dp_distance):
    depth, dp = lax.axis_size("depth"), lax.axis_size("dp")
    route = [
        (d * dp + j, (d ^ depth_distance) * dp + (j ^ dp_distance))
        for d in range(depth)
        for j in range(dp)
    ]
    return lax.ppermute(block, ("depth", "dp"), route)


def on_device(object_slices, positions, probe_field, propagator_phase, measured):
    depth, dp = lax.axis_size("depth"), lax.axis_size("dp")
    clusters = depth // 2
    members = dp // clusters
    rows, cols = object_slices.shape[-2:]
    window = probe_field.shape[-1]

    homes = [m * members for m in range(1, clusters)]
    all_positions = [positions] + [swap(positions, 0, home) for home in homes]
    obj = object_slices[0]
    windows, code = take_windows(obj, touch(obj), all_positions, window, members)
    phase, code = lax.optimization_barrier((propagator_phase, code))
    windows = [windows[0]] + [swap(windows[m // 2], m, 0) for m in range(1, depth)]
    targets = [measured] + [swap(measured, 0, home) for home in homes]
    kern = jnp.stack([jnp.cos(phase), jnp.sin(phase)])
    terms = run_waves(probe_field, kern, code, targets, windows, members)

    blocks = [
        swap(terms[m // 2], m, plane) if m or plane else terms[0]
        for plane in range(0, members, 2)
        for m in range(0, depth, 2)
    ]
    return place_windows(blocks, [swap(block, 0, 1) for block in blocks], rows // dp, cols)[None]


def solution(mesh):
    placed = (P("depth", None, None, None), P("dp", None), P(), P(), P("dp", None, None))
    return jax.shard_map(
        on_device,
        mesh=mesh,
        in_specs=placed,
        out_specs=P("depth", None, "dp", None),
        check_vma=False,
    )
```

```python
import functools
import math

import jax
import jax.numpy as jnp
import numpy as np
from jax import lax
from jax.experimental import pallas as pl
from jax.experimental.pallas import tpu as pltpu
from jax.sharding import PartitionSpec as P

grad_scale = 0.03125
f32 = jnp.float32
bf16 = jnp.bfloat16


def dft_matrices(size):
    k = np.arange(size)
    angles = 2.0 * np.pi * ((k[:, None] * k[None, :]) % size) / size
    c = np.cos(angles) / math.sqrt(size)
    s = np.sin(angles) / math.sqrt(size)
    plus = np.block([[c, s], [-s, c]]).astype(np.float32)
    minus = np.block([[c, -s], [s, c]]).astype(np.float32)
    parts = []
    for full in (plus, minus):
        high = full.astype(bf16)
        low = (full - high.astype(np.float32)).astype(bf16)
        parts.append((high, low))
    (ph, plo), (mh, mlo) = parts
    right = np.stack([np.concatenate([ph, ph, plo], 0), np.concatenate([mh, mh, mlo], 0)])
    left = np.stack([np.concatenate([mh, mh, mlo], 1), np.concatenate([ph, ph, plo], 1)])
    return left, right


code_rows = 16


def touch_kernel(obj_ref, out_ref):
    out_ref[...] = obj_ref[0, :8, :128]


def touch(obj):
    vmem = pl.BlockSpec(memory_space=pltpu.VMEM)
    return pl.pallas_call(
        touch_kernel,
        out_shape=jax.ShapeDtypeStruct((8, 128), obj.dtype),
        in_specs=[vmem],
        out_specs=vmem,
        compiler_params=pltpu.CompilerParams(vmem_limit_bytes=16 * 1024 * 1024),
        cost_estimate=pl.CostEstimate(
            flops=0, bytes_accessed=4 * math.prod(obj.shape), transcendentals=0
        ),
        name="touch_slice",
    )(obj)


def window_kernel(members, obj_ref, touched_ref, *rest):
    del touched_ref
    table, cut, table_sems = rest[-3:]
    clusters, count = table.shape[:2]
    pos_refs, out_refs, code_ref = rest[:clusters], rest[clusters:-4], rest[-4]
    window = out_refs[0].shape[-1]
    rows, cols = obj_ref.shape[-2:]
    tall, wide = window + 8, window + 128
    cluster = lax.div(lax.axis_index("dp"), members)
    home = lax.div(lax.axis_index("depth"), 2)

    fetches = [
        pltpu.make_async_copy(pos_refs[m], table.at[m], table_sems.at[m])
        for m in range(1, clusters)
    ]
    for fetch in fetches:
        fetch.start()
    for p in range(count):
        for axis in range(2):
            table[0, p, axis] = pos_refs[0][p, axis]

    def take(a):
        for p in range(count):
            row, col = table[a, p, 0], table[a, p, 1]
            row_base = pl.multiple_of(jnp.minimum(row >> 3, (rows - tall) // 8) * 8, 8)
            col_base = pl.multiple_of(jnp.minimum(col >> 7, (cols - wide) // 128) * 128, 128)
            lift = jnp.where(row == row_base, 0, tall - (row - row_base))
            shift = jnp.where(col == col_base, 0, wide - (col - col_base))
            for part in range(2):
                block = obj_ref[part, pl.ds(row_base, tall), pl.ds(col_base, wide)]
                block = pltpu.roll(block, shift, 1)[:, :window]
                block = pltpu.roll(block, lift, 0)[:window]
                cut[home ^ cluster ^ a, p, part] = block.astype(bf16)

    take(0)
    for a in range(1, clusters):
        fetches[a - 1].wait()
        take(a)
    line = lax.broadcasted_iota(jnp.int32, (code_rows, window), 0)
    code = jnp.zeros((code_rows, window), jnp.int32)
    for p in range(count):
        row, col = table[home ^ cluster, p, 0], table[home ^ cluster, p, 1]
        for n, value in enumerate((row >> 3, row & 7, col >> 3, col & 7)):
            code = jnp.where(line == 4 * p + n, value, code)
    code_ref[...] = code.astype(f32).astype(bf16)
    for m, out_ref in enumerate(out_refs):
        out_ref[...] = cut[m]


def take_windows(obj, touched, positions, window, members):
    clusters, count = len(positions), positions[0].shape[0]
    any_space = pl.BlockSpec(memory_space=pl.ANY)
    smem = pl.BlockSpec(memory_space=pltpu.SMEM)
    vmem = pl.BlockSpec(memory_space=pltpu.VMEM)
    out = pl.pallas_call(
        functools.partial(window_kernel, members),
        out_shape=[jax.ShapeDtypeStruct((count, 2, window, window), bf16)] * clusters
        + [jax.ShapeDtypeStruct((code_rows, window), bf16)],
        in_specs=[vmem, vmem, smem] + [any_space] * (clusters - 1),
        out_specs=[vmem] * (clusters + 1),
        scratch_shapes=[
            pltpu.SMEM((clusters, count, 2), jnp.int32),
            pltpu.VMEM((clusters, count, 2, window, window), bf16),
            pltpu.SemaphoreType.DMA((clusters,)),
        ],
        compiler_params=pltpu.CompilerParams(vmem_limit_bytes=16 * 1024 * 1024),
        name="take_windows",
    )(obj, touched, *positions)
    return out[:clusters], out[clusters]


def split(x):
    high = x.astype(bf16)
    return high, (x - high.astype(f32)).astype(bf16)


def cmul(a, b):
    return a[0] * b[0] - a[1] * b[1], a[0] * b[1] + a[1] * b[0]


def cmul_conj(a, b):
    return a[0] * b[0] + a[1] * b[1], a[0] * b[1] - a[1] * b[0]


def wave_kernel(members, clusters, probe_ref, kern_ref, left_ref, right_ref, code_ref, *rest):
    trans, terms, meas = rest[-3:]
    slices, count, _, _, window = trans.shape
    meas_refs, t_refs, out_refs = rest[:clusters], rest[clusters : clusters + slices], rest[clusters + slices : -3]
    own, cluster = lax.axis_index("depth"), lax.div(lax.axis_index("dp"), members)
    everyone = range(count)

    for m in range(slices):
        trans[own ^ m] = t_refs[m][...]
    for m, meas_ref in enumerate(meas_refs):

        @pl.when(lax.div(own, 2) ^ cluster == m)
        def _():
            meas[...] = meas_ref[...]

    def t_of(k, p):
        return trans[k, p, 0].astype(f32), trans[k, p, 1].astype(f32)

    def passes(x, axis, exact):
        if not exact:
            return x.astype(bf16)
        high, low = split(x)
        return jnp.concatenate([high, low, high], axis=axis)

    def rows(fields, sign, exact):
        x = jnp.concatenate([jnp.concatenate(f, axis=0) for f in fields], axis=1)
        x = passes(x, 0, exact)
        y = jnp.dot(left_ref[sign, :, : x.shape[0]], x, preferred_element_type=f32)
        cut = [y[:, p * window : (p + 1) * window] for p in everyone]
        return [(c[:window], c[window:]) for c in cut]

    def cols(fields, sign, exact):
        x = jnp.concatenate([jnp.concatenate(f, axis=1) for f in fields], axis=0)
        x = passes(x, 1, exact)
        y = jnp.dot(x, right_ref[sign, : x.shape[1]], preferred_element_type=f32)
        cut = [y[p * window : (p + 1) * window] for p in everyone]
        return [(c[:, :window], c[:, window:]) for c in cut]

    plus, minus = 0, 1

    def transform(fields, sign, exact):
        return cols(rows(fields, sign, exact), sign, exact)

    kern = (kern_ref[0], kern_ref[1])
    psi = [(probe_ref[0], probe_ref[1])] * count
    kept = []
    for k in range(slices):
        kept.append(psi)
        spectrum = transform([cmul(t_of(k, p), psi[p]) for p in everyone], minus, True)
        if k < slices - 1:
            psi = transform([cmul(kern, s) for s in spectrum], plus, True)

    def source(p):
        re, im = spectrum[p]
        scale = 2.0 * (re * re + im * im - meas[p])
        return scale * re, scale * im

    returned = transform([source(p) for p in everyone], plus, False)
    for k in reversed(range(slices)):
        for p in everyone:
            re, im = cmul_conj(kept[k][p], returned[p])
            terms[own ^ k, p, :window] = (re * grad_scale).astype(bf16)
            terms[own ^ k, p, window:] = (im * grad_scale).astype(bf16)
        if k > 0:
            chi = [cmul_conj(t_of(k, p), returned[p]) for p in everyone]
            spectrum = transform(chi, minus, False)
            returned = transform([cmul_conj(kern, s) for s in spectrum], plus, False)
    for n, out_ref in enumerate(out_refs):
        for p in everyone:
            out_ref[2 * p * window : 2 * (p + 1) * window] = terms[2 * n, p]
        out_ref[2 * count * window :] = code_ref[...]


def run_waves(probe, kern, code, measured, windows, members):
    slices, (count, _, _, window) = len(windows), windows[0].shape
    left, right = dft_matrices(window)
    vmem = pl.BlockSpec(memory_space=pltpu.VMEM)
    block = jax.ShapeDtypeStruct((2 * count * window + code_rows, window), bf16)
    return pl.pallas_call(
        functools.partial(wave_kernel, members, len(measured)),
        out_shape=[block] * (slices // 2),
        in_specs=[vmem] * (5 + len(measured) + slices),
        out_specs=[vmem] * (slices // 2),
        scratch_shapes=[
            pltpu.VMEM((slices, count, 2, window, window), bf16),
            pltpu.VMEM((slices, count, 2 * window, window), bf16),
            pltpu.VMEM((count, window, window), f32),
        ],
        compiler_params=pltpu.CompilerParams(vmem_limit_bytes=40 * 1024 * 1024),
        name="run_waves",
    )(probe, kern, jnp.asarray(left), jnp.asarray(right), code, *measured, *windows)


def add_blocks(block_refs, canvas, stripe):
    height, window = block_refs[0].shape
    count = (height - code_rows) // (2 * window)
    cols = canvas.shape[-1] - 128
    wide = window + 128
    first_row = lax.axis_index("dp") * stripe
    corners = []
    for block_ref in block_refs:
        code = block_ref[2 * count * window :].astype(f32)
        for p in range(count):
            row = (8.0 * code[4 * p : 4 * p + 1] + code[4 * p + 1 : 4 * p + 2]).astype(jnp.int32)
            col = (8.0 * code[4 * p + 2 : 4 * p + 3] + code[4 * p + 3 : 4 * p + 4]).astype(jnp.int32)
            corners.append((row[0, 0], col[0, 0]))
    for n, (row, col) in enumerate(corners):
        block_ref, p = block_refs[n // count], n % count
        row = row - first_row + window
        row_base = pl.multiple_of((row >> 3) << 3, 8)
        col_base = pl.multiple_of((col >> 7) << 7, 128)

        @pl.when((row > 0) & (row < window + stripe))
        def _():
            for part in range(2):
                block = block_ref[(2 * p + part) * window : (2 * p + part + 1) * window].astype(f32)
                block = jnp.concatenate([block, jnp.zeros((8, window), f32)], axis=0)
                block = pltpu.roll(block, row - row_base, 0)
                block = jnp.concatenate([block, jnp.zeros((window + 8, 128), f32)], axis=1)
                block = pltpu.roll(block, col - col_base, 1)
                put = (part, pl.ds(row_base, window + 8), pl.ds(col_base, wide))
                canvas[put] = canvas[put] + block


def first_kernel(stripe, *refs):
    block_refs, canvas = refs[:-1], refs[-1]
    window = block_refs[0].shape[-1]
    canvas[:, window : window + stripe, :] = jnp.zeros((2, stripe, canvas.shape[2]), f32)
    add_blocks(block_refs, canvas, stripe)


def second_kernel(start_ref, *refs):
    block_refs, (out_ref, canvas) = refs[:-2], refs[-2:]
    _, stripe, cols = out_ref.shape
    window = block_refs[0].shape[-1]
    canvas[:, window : window + stripe, :] = start_ref[:, window : window + stripe, :]
    add_blocks(block_refs, canvas, stripe)
    out_ref[...] = canvas[:, window : window + stripe, :cols]


def place_windows(near, far, stripe, cols):
    window = near[0].shape[-1]
    vmem = pl.BlockSpec(memory_space=pltpu.VMEM)
    tall = window + (stripe + 7) // 8 * 8 + window + 8
    canvas = (2, tall, cols + 128)
    limit = pltpu.CompilerParams(vmem_limit_bytes=24 * 1024 * 1024)
    start = pl.pallas_call(
        functools.partial(first_kernel, stripe),
        out_shape=jax.ShapeDtypeStruct(canvas, f32),
        in_specs=[vmem] * len(near),
        out_specs=vmem,
        compiler_params=limit,
        name="place_near",
    )(*near)
    return pl.pallas_call(
        second_kernel,
        out_shape=jax.ShapeDtypeStruct((2, stripe, cols), f32),
        in_specs=[vmem] * (1 + len(far)),
        out_specs=vmem,
        scratch_shapes=[pltpu.VMEM(canvas, f32)],
        compiler_params=limit,
        name="place_far",
    )(start, *far)


def swap(block, depth_distance, dp_distance):
    depth, dp = lax.axis_size("depth"), lax.axis_size("dp")
    route = [
        (d * dp + j, (d ^ depth_distance) * dp + (j ^ dp_distance))
        for d in range(depth)
        for j in range(dp)
    ]
    return lax.ppermute(block, ("depth", "dp"), route)


def on_device(object_slices, positions, probe_field, propagator_phase, measured):
    depth, dp = lax.axis_size("depth"), lax.axis_size("dp")
    clusters = depth // 2
    members = dp // clusters
    rows, cols = object_slices.shape[-2:]
    window = probe_field.shape[-1]

    homes = [m * members for m in range(1, clusters)]
    all_positions = [positions] + [swap(positions, 0, home) for home in homes]
    obj = object_slices[0]
    windows, code = take_windows(obj, touch(obj), all_positions, window, members)
    phase, code = lax.optimization_barrier((propagator_phase, code))
    windows = [windows[0]] + [swap(windows[m // 2], m, 0) for m in range(1, depth)]
    targets = [measured] + [swap(measured, 0, home) for home in homes]
    kern = jnp.stack([jnp.cos(phase), jnp.sin(phase)])
    terms = run_waves(probe_field, kern, code, targets, windows, members)

    blocks = [
        swap(terms[m // 2], m, plane) if m or plane else terms[0]
        for plane in range(0, members, 2)
        for m in range(0, depth, 2)
    ]
    passed = [swap(block, 0, 1) for block in blocks]
    early, late = blocks + [passed[0], passed[-1]], passed[1:-1]
    return place_windows(early, late, rows // dp, cols)[None]


def solution(mesh):
    placed = (P("depth", None, None, None), P("dp", None), P(), P(), P("dp", None, None))
    return jax.shard_map(
        on_device,
        mesh=mesh,
        in_specs=placed,
        out_specs=P("depth", None, "dp", None),
        check_vma=False,
    )
```

```python
import functools
import math

import jax
import jax.numpy as jnp
import numpy as np
from jax import lax
from jax.experimental import pallas as pl
from jax.experimental.pallas import tpu as pltpu
from jax.sharding import PartitionSpec as P

grad_scale = 0.03125
f32 = jnp.float32
bf16 = jnp.bfloat16


def dft_matrices(size):
    k = np.arange(size)
    angles = 2.0 * np.pi * ((k[:, None] * k[None, :]) % size) / size
    c = np.cos(angles) / math.sqrt(size)
    s = np.sin(angles) / math.sqrt(size)
    plus = np.block([[c, s], [-s, c]]).astype(np.float32)
    minus = np.block([[c, -s], [s, c]]).astype(np.float32)
    parts = []
    for full in (plus, minus):
        high = full.astype(bf16)
        low = (full - high.astype(np.float32)).astype(bf16)
        parts.append((high, low))
    (ph, plo), (mh, mlo) = parts
    right = np.stack([np.concatenate([ph, ph, plo], 0), np.concatenate([mh, mh, mlo], 0)])
    left = np.stack([np.concatenate([mh, mh, mlo], 1), np.concatenate([ph, ph, plo], 1)])
    return left, right


code_rows = 16


def touch_kernel(obj_ref, out_ref):
    out_ref[...] = obj_ref[0, :8, :128]


def touch(obj):
    vmem = pl.BlockSpec(memory_space=pltpu.VMEM)
    return pl.pallas_call(
        touch_kernel,
        out_shape=jax.ShapeDtypeStruct((8, 128), obj.dtype),
        in_specs=[vmem],
        out_specs=vmem,
        compiler_params=pltpu.CompilerParams(vmem_limit_bytes=16 * 1024 * 1024),
        cost_estimate=pl.CostEstimate(
            flops=0, bytes_accessed=4 * math.prod(obj.shape), transcendentals=0
        ),
        name="touch_slice",
    )(obj)


def window_kernel(members, obj_ref, touched_ref, *rest):
    del touched_ref
    table, cut, table_sems = rest[-3:]
    clusters, count = table.shape[:2]
    pos_refs, out_refs, code_ref = rest[:clusters], rest[clusters:-4], rest[-4]
    window = out_refs[0].shape[-1]
    rows, cols = obj_ref.shape[-2:]
    tall, wide = window + 8, window + 128
    cluster = lax.div(lax.axis_index("dp"), members)
    home = lax.div(lax.axis_index("depth"), 2)

    fetches = [
        pltpu.make_async_copy(pos_refs[m], table.at[m], table_sems.at[m])
        for m in range(1, clusters)
    ]
    for fetch in fetches:
        fetch.start()
    for p in range(count):
        for axis in range(2):
            table[0, p, axis] = pos_refs[0][p, axis]

    def take(a):
        for p in range(count):
            row, col = table[a, p, 0], table[a, p, 1]
            row_base = pl.multiple_of(jnp.minimum(row >> 3, (rows - tall) // 8) * 8, 8)
            col_base = pl.multiple_of(jnp.minimum(col >> 7, (cols - wide) // 128) * 128, 128)
            lift = jnp.where(row == row_base, 0, tall - (row - row_base))
            shift = jnp.where(col == col_base, 0, wide - (col - col_base))
            for part in range(2):
                block = obj_ref[part, pl.ds(row_base, tall), pl.ds(col_base, wide)]
                block = pltpu.roll(block, shift, 1)[:, :window]
                block = pltpu.roll(block, lift, 0)[:window]
                cut[home ^ cluster ^ a, p, part] = block.astype(bf16)

    take(0)
    for a in range(1, clusters):
        fetches[a - 1].wait()
        take(a)
    line = lax.broadcasted_iota(jnp.int32, (code_rows, window), 0)
    code = jnp.zeros((code_rows, window), jnp.int32)
    for p in range(count):
        row, col = table[home ^ cluster, p, 0], table[home ^ cluster, p, 1]
        for n, value in enumerate((row >> 3, row & 7, col >> 3, col & 7)):
            code = jnp.where(line == 4 * p + n, value, code)
    code_ref[...] = code.astype(f32).astype(bf16)
    for m, out_ref in enumerate(out_refs):
        out_ref[...] = cut[m]


def take_windows(obj, touched, positions, window, members):
    clusters, count = len(positions), positions[0].shape[0]
    any_space = pl.BlockSpec(memory_space=pl.ANY)
    smem = pl.BlockSpec(memory_space=pltpu.SMEM)
    vmem = pl.BlockSpec(memory_space=pltpu.VMEM)
    out = pl.pallas_call(
        functools.partial(window_kernel, members),
        out_shape=[jax.ShapeDtypeStruct((count, 2, window, window), bf16)] * clusters
        + [jax.ShapeDtypeStruct((code_rows, window), bf16)],
        in_specs=[vmem, vmem, smem] + [any_space] * (clusters - 1),
        out_specs=[vmem] * (clusters + 1),
        scratch_shapes=[
            pltpu.SMEM((clusters, count, 2), jnp.int32),
            pltpu.VMEM((clusters, count, 2, window, window), bf16),
            pltpu.SemaphoreType.DMA((clusters,)),
        ],
        compiler_params=pltpu.CompilerParams(vmem_limit_bytes=16 * 1024 * 1024),
        name="take_windows",
    )(obj, touched, *positions)
    return out[:clusters], out[clusters]


def split(x):
    high = x.astype(bf16)
    return high, (x - high.astype(f32)).astype(bf16)


def cmul(a, b):
    return a[0] * b[0] - a[1] * b[1], a[0] * b[1] + a[1] * b[0]


def cmul_conj(a, b):
    return a[0] * b[0] + a[1] * b[1], a[0] * b[1] - a[1] * b[0]


def wave_kernel(members, clusters, probe_ref, kern_ref, left_ref, right_ref, code_ref, *rest):
    trans, terms, meas = rest[-3:]
    slices, count, _, _, window = trans.shape
    meas_refs, t_refs, out_refs = rest[:clusters], rest[clusters : clusters + slices], rest[clusters + slices : -3]
    own, cluster = lax.axis_index("depth"), lax.div(lax.axis_index("dp"), members)
    everyone = range(count)

    for m in range(slices):
        trans[own ^ m] = t_refs[m][...]
    for m, meas_ref in enumerate(meas_refs):

        @pl.when(lax.div(own, 2) ^ cluster == m)
        def _():
            meas[...] = meas_ref[...]

    def t_of(k, p):
        return trans[k, p, 0].astype(f32), trans[k, p, 1].astype(f32)

    def passes(x, axis, exact):
        if not exact:
            return x.astype(bf16)
        high, low = split(x)
        return jnp.concatenate([high, low, high], axis=axis)

    def rows(fields, sign, exact):
        x = jnp.concatenate([jnp.concatenate(f, axis=0) for f in fields], axis=1)
        x = passes(x, 0, exact)
        y = jnp.dot(left_ref[sign, :, : x.shape[0]], x, preferred_element_type=f32)
        cut = [y[:, p * window : (p + 1) * window] for p in everyone]
        return [(c[:window], c[window:]) for c in cut]

    def cols(fields, sign, exact):
        x = jnp.concatenate([jnp.concatenate(f, axis=1) for f in fields], axis=0)
        x = passes(x, 1, exact)
        y = jnp.dot(x, right_ref[sign, : x.shape[1]], preferred_element_type=f32)
        cut = [y[p * window : (p + 1) * window] for p in everyone]
        return [(c[:, :window], c[:, window:]) for c in cut]

    plus, minus = 0, 1

    def transform(fields, sign, exact):
        return cols(rows(fields, sign, exact), sign, exact)

    kern = (kern_ref[0], kern_ref[1])
    psi = [(probe_ref[0], probe_ref[1])] * count
    kept = []
    for k in range(slices):
        kept.append(psi)
        spectrum = transform([cmul(t_of(k, p), psi[p]) for p in everyone], minus, True)
        if k < slices - 1:
            psi = transform([cmul(kern, s) for s in spectrum], plus, True)

    def source(p):
        re, im = spectrum[p]
        scale = 2.0 * (re * re + im * im - meas[p])
        return scale * re, scale * im

    returned = transform([source(p) for p in everyone], plus, False)
    for k in reversed(range(slices)):
        for p in everyone:
            re, im = cmul_conj(kept[k][p], returned[p])
            terms[own ^ k, p, :window] = (re * grad_scale).astype(bf16)
            terms[own ^ k, p, window:] = (im * grad_scale).astype(bf16)
        if k > 0:
            chi = [cmul_conj(t_of(k, p), returned[p]) for p in everyone]
            spectrum = transform(chi, minus, False)
            returned = transform([cmul_conj(kern, s) for s in spectrum], plus, False)
    for n, out_ref in enumerate(out_refs):
        for p in everyone:
            out_ref[2 * p * window : 2 * (p + 1) * window] = terms[2 * n, p]
        out_ref[2 * count * window :] = code_ref[...]


def run_waves(probe, kern, code, measured, windows, members):
    slices, (count, _, _, window) = len(windows), windows[0].shape
    left, right = dft_matrices(window)
    vmem = pl.BlockSpec(memory_space=pltpu.VMEM)
    block = jax.ShapeDtypeStruct((2 * count * window + code_rows, window), bf16)
    return pl.pallas_call(
        functools.partial(wave_kernel, members, len(measured)),
        out_shape=[block] * (slices // 2),
        in_specs=[vmem] * (5 + len(measured) + slices),
        out_specs=[vmem] * (slices // 2),
        scratch_shapes=[
            pltpu.VMEM((slices, count, 2, window, window), bf16),
            pltpu.VMEM((slices, count, 2 * window, window), bf16),
            pltpu.VMEM((count, window, window), f32),
        ],
        compiler_params=pltpu.CompilerParams(vmem_limit_bytes=40 * 1024 * 1024),
        name="run_waves",
    )(probe, kern, jnp.asarray(left), jnp.asarray(right), code, *measured, *windows)


def add_blocks(block_refs, canvas, stripe):
    height, window = block_refs[0].shape
    count = (height - code_rows) // (2 * window)
    cols = canvas.shape[-1] - 128
    wide = window + 128
    first_row = lax.axis_index("dp") * stripe
    corners = []
    for block_ref in block_refs:
        code = block_ref[2 * count * window :].astype(f32)
        for p in range(count):
            row = (8.0 * code[4 * p : 4 * p + 1] + code[4 * p + 1 : 4 * p + 2]).astype(jnp.int32)
            col = (8.0 * code[4 * p + 2 : 4 * p + 3] + code[4 * p + 3 : 4 * p + 4]).astype(jnp.int32)
            corners.append((row[0, 0], col[0, 0]))
    for n, (row, col) in enumerate(corners):
        block_ref, p = block_refs[n // count], n % count
        row = row - first_row + window
        row_base = pl.multiple_of((row >> 3) << 3, 8)
        col_base = pl.multiple_of((col >> 7) << 7, 128)

        @pl.when((row > 0) & (row < window + stripe))
        def _():
            for part in range(2):
                block = block_ref[(2 * p + part) * window : (2 * p + part + 1) * window].astype(f32)
                block = jnp.concatenate([block, jnp.zeros((8, window), f32)], axis=0)
                block = pltpu.roll(block, row - row_base, 0)
                block = jnp.concatenate([block, jnp.zeros((window + 8, 128), f32)], axis=1)
                block = pltpu.roll(block, col - col_base, 1)
                put = (part, pl.ds(row_base, window + 8), pl.ds(col_base, wide))
                canvas[put] = canvas[put] + block


def first_kernel(stripe, *refs):
    block_refs, canvas = refs[:-1], refs[-1]
    window = block_refs[0].shape[-1]
    canvas[:, window : window + stripe, :] = jnp.zeros((2, stripe, canvas.shape[2]), f32)
    add_blocks(block_refs, canvas, stripe)


def second_kernel(start_ref, *refs):
    block_refs, (out_ref, canvas) = refs[:-2], refs[-2:]
    _, stripe, cols = out_ref.shape
    window = block_refs[0].shape[-1]
    canvas[:, window : window + stripe, :] = start_ref[:, window : window + stripe, :]
    add_blocks(block_refs, canvas, stripe)
    out_ref[...] = canvas[:, window : window + stripe, :cols]


def place_windows(near, far, stripe, cols):
    window = near[0].shape[-1]
    vmem = pl.BlockSpec(memory_space=pltpu.VMEM)
    tall = window + (stripe + 7) // 8 * 8 + window + 8
    canvas = (2, tall, cols + 128)
    limit = pltpu.CompilerParams(vmem_limit_bytes=24 * 1024 * 1024)
    start = pl.pallas_call(
        functools.partial(first_kernel, stripe),
        out_shape=jax.ShapeDtypeStruct(canvas, f32),
        in_specs=[vmem] * len(near),
        out_specs=vmem,
        compiler_params=limit,
        name="place_near",
    )(*near)
    return pl.pallas_call(
        second_kernel,
        out_shape=jax.ShapeDtypeStruct((2, stripe, cols), f32),
        in_specs=[vmem] * (1 + len(far)),
        out_specs=vmem,
        scratch_shapes=[pltpu.VMEM(canvas, f32)],
        compiler_params=limit,
        name="place_far",
    )(start, *far)


def swap(block, depth_distance, dp_distance):
    depth, dp = lax.axis_size("depth"), lax.axis_size("dp")
    route = [
        (d * dp + j, (d ^ depth_distance) * dp + (j ^ dp_distance))
        for d in range(depth)
        for j in range(dp)
    ]
    return lax.ppermute(block, ("depth", "dp"), route)


def on_device(object_slices, positions, probe_field, propagator_phase, measured):
    depth, dp = lax.axis_size("depth"), lax.axis_size("dp")
    clusters = depth // 2
    members = dp // clusters
    rows, cols = object_slices.shape[-2:]
    window = probe_field.shape[-1]

    homes = [m * members for m in range(1, clusters)]
    all_positions = [positions] + [swap(positions, 0, home) for home in homes]
    obj = object_slices[0]
    windows, code = take_windows(obj, touch(obj), all_positions, window, members)
    phase, code = lax.optimization_barrier((propagator_phase, code))
    arrivals = [swap(windows[m // 2], m, 0) for m in reversed(range(1, depth))]
    windows = [windows[0]] + arrivals[::-1]
    targets = [measured] + [swap(measured, 0, home) for home in homes]
    kern = jnp.stack([jnp.cos(phase), jnp.sin(phase)])
    terms = run_waves(probe_field, kern, code, targets, windows, members)

    blocks = [
        swap(terms[m // 2], m, plane) if m or plane else terms[0]
        for plane in range(0, members, 2)
        for m in range(0, depth, 2)
    ]
    passed = [swap(block, 0, 1) for block in blocks]
    early, late = blocks + [passed[0], passed[-1]], passed[1:-1]
    return place_windows(early, late, rows // dp, cols)[None]


def solution(mesh):
    placed = (P("depth", None, None, None), P("dp", None), P(), P(), P("dp", None, None))
    return jax.shard_map(
        on_device,
        mesh=mesh,
        in_specs=placed,
        out_specs=P("depth", None, "dp", None),
        check_vma=False,
    )
```
